32 devices in a mesh: ta: 4 (over y, x), ha: 2 (over core), wa: 4 (over z).
Axes of the slice: x: 2, y: 2, z: 4, core: 2. Of those that a mesh axis runs over, the one named last changes fastest.
Arguments:
- queries: bfloat16 [12, 8, 32, 1536], P('ta', 'ha', 'wa'), may hold values from -6 to 6
- keys: bfloat16 [12, 8, 32, 1536], P('ta', 'ha', 'wa'), may hold values from -6 to 6
- values: bfloat16 [12, 8, 32, 1536], P('ta', 'ha', 'wa'), may hold values from -6 to 6
- radius: int32 [12, 3], replicated, may hold values from 0 to 1
- out_weight: bfloat16 [1536, 3072], P(('ha', 'wa')), may hold values from -0.15625 to 0.15625
Outputs:
- mixed_out: bfloat16 [12, 8, 32, 3072], P('ta', 'ha', 'wa')
The draws below stay inside these ranges and needn't reach their ends.
All inputs are finite; a program needn't handle non-finite values.
Results may differ from the reference program's by a relative error of at most 0.0057.
Values may be sent and summed in bfloat16 or wider, within the bound.
No kernel may reach another device: no remote copies, remote signals or barrier semaphores. Data moves between devices by JAX's collectives and lax.ppermute only.
A program may use at most 128 MiB of HBM per device.

```python
import math
import jax
import jax.numpy as jnp
from jax import lax

D = 3072
HEADS = 12
HEAD_DIM = 128
TILE = 4
R = 1536
FRAMES = 12
HEIGHT = 8
WIDTH = 32


def draw_queries(key, part):
    shape = (FRAMES, HEIGHT, WIDTH, HEADS * HEAD_DIM)
    base = jnp.clip(jax.random.normal(jax.random.fold_in(key, 711), shape, jnp.float32), -6.0, 6.0)
    return base.astype(jnp.bfloat16)


def draw_keys(key, part):
    shape = (FRAMES, HEIGHT, WIDTH, HEADS * HEAD_DIM)
    base = jnp.clip(jax.random.normal(jax.random.fold_in(key, 721), shape, jnp.float32), -6.0, 6.0)
    return base.astype(jnp.bfloat16)


def set_ends(result, stream_key, least, top_value):
    longest = result.shape.index(max(result.shape))
    spots = []
    for shift in (0, 1):
        where = [jax.random.randint(jax.random.fold_in(stream_key, axis), (), 0, length) for axis, length in enumerate(result.shape)]
        where[longest] = (where[longest] + shift) % result.shape[longest]
        spots.append(tuple(where))
    return result.at[spots[0]].set(least).at[spots[1]].set(top_value)


def levels(own_key, shape, cuts, least, largest):
    def one(dim, parts):
        draws = jax.random.uniform(jax.random.fold_in(jax.random.fold_in(own_key, 6), dim), (parts,), jnp.float32, least / len(cuts), largest / len(cuts))
        return jnp.repeat(jnp.exp(draws), shape[dim] // parts).reshape((-1,) + (1,) * (len(shape) - dim - 1))

    loudness = one(*cuts[0])
    for cut in cuts[1:]:
        loudness = loudness * one(*cut)
    return loudness


def centred(rng, dims, scale, limit, shards=(), held_as=jnp.bfloat16):
    values = scale * jax.random.normal(rng, dims, jnp.float32)
    if shards:
        values = values * levels(rng, dims, shards, -0.22, 0.18)
    return jnp.clip(values, -limit, limit).astype(held_as)


def setup_inputs(seed: int = 0) -> dict:
    streams_of = jax.random.split(jax.random.key(seed), 6)
    queries = draw_queries(jax.random.fold_in(streams_of[5], 71), 0)
    keys = draw_keys(jax.random.fold_in(streams_of[5], 71), 0)
    values = centred(streams_of[2], (FRAMES, HEIGHT, WIDTH, R), 1.0, 6.0, ((0, 4), (1, 2), (2, 4)))
    radius = set_ends(jax.random.randint(streams_of[3], (HEADS, 3), 0, 2), jax.random.fold_in(streams_of[3], 1), 0, 1).astype(jnp.int32)
    out_weight = centred(streams_of[4], (R, D), R ** -0.5, 0.15625, ((0, 8),))
    return {"queries": queries, "keys": keys, "values": values, "radius": radius, "out_weight": out_weight}


def reference(queries, keys, values, radius, out_weight):
    frames, height, width_all, features = queries.shape
    head_count = radius.shape[0]
    head_dim = features // head_count
    tiles_h = height // TILE
    tiles_w = width_all // TILE
    pad_spec = ((1, 1), (TILE, TILE), (TILE, TILE), (0, 0))
    key_pad = jnp.pad(keys, pad_spec)
    value_pad = jnp.pad(values, pad_spec)
    inside = jnp.pad(jnp.ones((frames, height, width_all), jnp.float32), pad_spec[:3])
    shape_four = (3, 3 * TILE, 3, TILE)
    off_t = lax.broadcasted_iota(jnp.int32, shape_four, 0).reshape(-1) - 1
    off_h = lax.broadcasted_iota(jnp.int32, shape_four, 1).reshape(-1) // TILE - 1
    off_w = lax.broadcasted_iota(jnp.int32, shape_four, 2).reshape(-1) - 1
    allowed_head = (jnp.abs(off_t)[None, :] <= radius[:, 0:1]) & (jnp.abs(off_h)[None, :] <= radius[:, 1:2]) & (jnp.abs(off_w)[None, :] <= radius[:, 2:3])
    score_scale = 1.0 / math.sqrt(head_dim)

    def arrange(block):
        others = block.shape[3:]
        split = block.reshape((3, 3 * TILE, tiles_w + 2, TILE) + others)
        stacked = jnp.stack([split[:, :, offset:offset + tiles_w] for offset in range(3)], axis=2)
        moved = jnp.moveaxis(stacked, 3, 0)
        return moved.reshape((tiles_w, 27 * TILE * TILE) + others)

    def one_row(position):
        frame = position // tiles_h
        band = position % tiles_h
        anchor = jnp.int32(0)
        query_block = lax.dynamic_slice(queries, (frame, band * TILE, anchor, anchor), (1, TILE, width_all, features))
        query_tiles = query_block.reshape(TILE, tiles_w, TILE, head_count, head_dim).transpose(1, 0, 2, 3, 4).reshape(tiles_w, TILE * TILE, head_count, head_dim)
        corner = (frame, band * TILE, anchor, anchor)
        extent = (3, 3 * TILE, width_all + 2 * TILE, features)
        key_tiles = arrange(lax.dynamic_slice(key_pad, corner, extent)).reshape(tiles_w, -1, head_count, head_dim)
        value_tiles = arrange(lax.dynamic_slice(value_pad, corner, extent)).reshape(tiles_w, -1, head_count, head_dim)
        inside_tiles = arrange(lax.dynamic_slice(inside, (frame, band * TILE, anchor), (3, 3 * TILE, width_all + 2 * TILE)))
        allowed = allowed_head[None, :, None, :] & (inside_tiles[:, None, None, :] > 0.5)
        scores = jnp.einsum('jqhd,jkhd->jhqk', query_tiles.astype(jnp.float32), key_tiles.astype(jnp.float32), precision=lax.Precision.HIGHEST) * score_scale
        scores = jnp.where(allowed, scores, -jnp.inf)
        biggest = lax.optimization_barrier(jnp.max(scores, axis=-1, keepdims=True))
        expo = jnp.exp(scores - biggest)
        probs = (expo / lax.optimization_barrier(jnp.sum(expo, axis=-1, keepdims=True))).astype(jnp.bfloat16)
        attended = jnp.einsum('jhqk,jkhd->jqhd', probs.astype(jnp.float32), value_tiles.astype(jnp.float32), precision=lax.Precision.HIGHEST).astype(jnp.bfloat16)
        return attended.reshape(tiles_w, TILE, TILE, features).transpose(1, 0, 2, 3).reshape(TILE, width_all, features)
    bands = lax.map(one_row, jnp.arange(frames * tiles_h, dtype=jnp.int32))
    attended = bands.reshape(frames * height * width_all, features)
    mixed_out = jnp.dot(attended, out_weight, preferred_element_type=jnp.float32).astype(jnp.bfloat16)
    return mixed_out.reshape(frames, height, width_all, out_weight.shape[1])
```

```python
import functools
import math

import jax
import jax.numpy as jnp
import numpy as np
from jax import lax
from jax.experimental import pallas as pl
from jax.experimental.pallas import tpu as pltpu
from jax.sharding import PartitionSpec as P

TILE = 4
PAIR = 2
FAR = -1e30
LANES = 128
VMEM = pl.BlockSpec(memory_space=pltpu.VMEM)
SMEM = pl.BlockSpec(memory_space=pltpu.SMEM)
HBM = pl.BlockSpec(memory_space=pl.ANY)
PARAMS = pltpu.CompilerParams(vmem_limit_bytes=40 * 1024 * 1024)


def line(count, step):
    return [(i, i + step) for i in range(count) if 0 <= i + step < count]


def cycle(count, step):
    return [(i, (i + step) % count) for i in range(count)]


def code_table(rows, cols, rims):
    tile_cols = cols // TILE
    span = rows // TILE
    tables = []
    for core in range(PAIR):
        own = core * span
        other = (1 - core) * span
        query_row, query_col, key_row, key_col = [], [], [], []
        for base in (own, other):
            for row in range(rows):
                for col in range(cols):
                    query_row.append(base + row // TILE)
                    query_col.append(col // TILE)
        blocks = [(own, rows), (other, rows)] + ([(-1, TILE), (2 * span, TILE)] if rims else [])
        for tile_col in [None, -1, tile_cols]:
            for base, length in blocks:
                for c in range(tile_cols) if tile_col is None else [tile_col]:
                    for row in range(length):
                        for _ in range(TILE):
                            key_row.append(base + row // TILE)
                            key_col.append(c)
        key_row, key_col = np.array(key_row)[None], np.array(key_col)[None]
        apart_row = np.abs(np.array(query_row)[:, None] - key_row)
        apart_col = np.abs(np.array(query_col)[:, None] - key_col)
        base_code = (
            2 * (apart_row == 1)
            + 4 * (apart_col == 1)
            + 8 * ((apart_row > 1) | (apart_col > 1))
        )
        outside = [key_col < 0, key_col >= tile_cols, key_row < 0, key_row >= 2 * span]
        for bits in range(16):
            code = base_code
            for which, mask in enumerate(outside):
                if bits >> which & 1:
                    code = np.where(mask, 8, code)
            tables.append(code)
            if not rims and bits == 3:
                break
    return np.stack(tables).astype(np.int32)


def split3(x):
    high = x.astype(jnp.bfloat16)
    rest = x - high.astype(jnp.float32)
    mid = rest.astype(jnp.bfloat16)
    return high, mid, (rest - mid.astype(jnp.float32)).astype(jnp.bfloat16)


def head_bias(code, radius_ref, head):
    barred = (
        8
        + jnp.where(radius_ref[head, 1] == 0, 2, 0)
        + jnp.where(radius_ref[head, 2] == 0, 4, 0)
    )
    return jnp.where((code & barred) == 0, 0.0, FAR)


def window(parts, kind, frame, lanes):
    own, other, rims, low, high = parts
    pieces = [own[1 + kind, frame, :, lanes], other[1 + kind, frame, :, lanes]]
    if rims is not None:
        pieces.append(rims[kind, frame, :, lanes])
    pieces += [low[kind, frame, :, lanes], high[kind, frame, :, lanes]]
    return jnp.concatenate(pieces, axis=0)


def scores_of(query, key, scale):
    return (
        lax.dot_general(
            query, key, (((1,), (1,)), ((), ())), preferred_element_type=jnp.float32
        )
        * scale
    )


def unpack(refs, rims):
    refs = list(refs)
    own, other = refs[:2]
    rim = refs[2] if rims else None
    rest = refs[3 if rims else 2 :]
    return (own, other, rim, rest[0], rest[1]), rest[2:]


def guest_kernel(rims, heads, width, meta_ref, radius_ref, code_ref, *refs):
    parts, rest = unpack(refs, rims)
    before_ref, after_ref, to_before, to_after = rest
    frames = parts[0].shape[1]
    code = code_ref[...]
    scale = 1.0 / math.sqrt(width)
    first = meta_ref[0] * heads
    lane = lax.broadcasted_iota(jnp.int32, (code.shape[0], LANES), 1)
    for query_ref, out_ref, frame in ((before_ref, to_before, 0), (after_ref, to_after, frames - 1)):
        stats = jnp.zeros((code.shape[0], LANES), jnp.float32)
        for head in range(heads):
            lanes = pl.ds(head * width, width)
            bias = head_bias(code, radius_ref, first + head)
            key = window(parts, 0, frame, lanes)
            value = window(parts, 1, frame, lanes)
            score = scores_of(query_ref[:, lanes], key, scale) + bias
            top = jnp.max(score, axis=1, keepdims=True)
            expo = jnp.exp(score - top)
            total = jnp.sum(expo, axis=1, keepdims=True)
            mixed = jnp.dot(
                expo.astype(jnp.bfloat16), value, preferred_element_type=jnp.float32
            )
            out_ref[:, lanes] = (mixed / total).astype(jnp.bfloat16)
            for spot, piece in enumerate(split3(top + jnp.log(total))):
                stats = jnp.where(
                    lane == 3 * head + spot, piece.astype(jnp.float32), stats
                )
        out_ref[:, pl.ds(heads * width, LANES)] = stats.astype(jnp.bfloat16)


def host_kernel(rims, heads, width, meta_ref, radius_ref, code_ref, *refs):
    parts, rest = unpack(refs, rims)
    mixed_ref, stats_ref = rest
    own, other = parts[:2]
    frames = own.shape[1]
    code = code_ref[...]
    count = code.shape[0]
    scale = 1.0 / math.sqrt(width)
    first = meta_ref[0] * heads
    lane = lax.broadcasted_iota(jnp.int32, (count, LANES), 1)
    stats = [jnp.zeros((count, LANES), jnp.float32) for _ in range(frames)]
    for head in range(heads):
        lanes = pl.ds(head * width, width)
        bias = head_bias(code, radius_ref, first + head)
        bias_apart = jnp.where(radius_ref[first + head, 0] == 0, FAR, bias)
        query = [
            jnp.concatenate([own[0, f, :, lanes], other[0, f, :, lanes]], axis=0)
            for f in range(frames)
        ]
        score = {}
        for frame in range(frames):
            near = range(max(0, frame - 1), min(frames, frame + 2))
            block = scores_of(
                jnp.concatenate([query[f] for f in near], axis=0),
                window(parts, 0, frame, lanes),
                scale,
            )
            for spot, f in enumerate(near):
                score[f, frame] = block[spot * count : (spot + 1) * count] + (
                    bias if f == frame else bias_apart
                )
        value = [window(parts, 1, f, lanes) for f in range(frames)]
        for f in range(frames):
            near = range(max(0, f - 1), min(frames, f + 2))
            row = jnp.concatenate([score[f, g] for g in near], axis=1)
            top = jnp.max(row, axis=1, keepdims=True)
            expo = jnp.exp(row - top)
            total = jnp.sum(expo, axis=1, keepdims=True)
            mixed = jnp.dot(
                expo.astype(jnp.bfloat16),
                jnp.concatenate([value[g] for g in near], axis=0),
                preferred_element_type=jnp.float32,
            )
            mixed_ref[f, :, lanes] = mixed / total
            stats[f] = jnp.where(lane == head, top + jnp.log(total), stats[f])
    for f in range(frames):
        stats_ref[f] = stats[f]


def merge_kernel(heads, width, meta_ref, radius_ref, mixed_ref, stats_ref, before_ref, after_ref, own_out, other_out):
    frames, count, _ = mixed_ref.shape
    half = count // PAIR
    first = meta_ref[0] * heads
    tail = pl.ds(heads * width, LANES)
    for f in range(frames):
        guests = []
        if f == 0:
            guests.append((before_ref, meta_ref[1]))
        if f == frames - 1:
            guests.append((after_ref, meta_ref[2]))
        guests = [(ref, ref[:, tail].astype(jnp.float32), there) for ref, there in guests]
        for head in range(heads):
            lanes = pl.ds(head * width, width)
            mixed = mixed_ref[f, :, lanes]
            if guests:
                logs = [stats_ref[f, :, head : head + 1]]
                values = [mixed]
                for ref, stats, there in guests:
                    use = (there != 0) & (radius_ref[first + head, 0] != 0)
                    log = (
                        stats[:, 3 * head : 3 * head + 1]
                        + stats[:, 3 * head + 1 : 3 * head + 2]
                        + stats[:, 3 * head + 2 : 3 * head + 3]
                    )
                    logs.append(jnp.where(use, log, FAR))
                    values.append(ref[:, lanes].astype(jnp.float32))
                top = functools.reduce(jnp.maximum, logs)
                weights = [jnp.exp(log - top) for log in logs]
                total = functools.reduce(jnp.add, weights)
                mixed = functools.reduce(
                    jnp.add, [v * (w / total) for v, w in zip(values, weights)]
                )
            mixed = mixed.astype(jnp.bfloat16)
            own_out[f, :, lanes] = mixed[:half]
            other_out[f, :, lanes] = mixed[half:]


def project_kernel(senders, pieces, shards, meta_ref, *refs):
    own, other = refs[:2]
    received = refs[2 : 2 + senders]
    weights = refs[2 + senders : 2 + senders + pieces]
    outs = refs[2 + senders + pieces : 3 + 2 * senders + pieces]
    held, weight, sems = refs[3 + 2 * senders + pieces :]
    half = own.shape[1]
    here = pl.ds(pl.multiple_of(meta_ref[0] * half, LANES), half)
    there = pl.ds(pl.multiple_of((1 - meta_ref[0]) * half, LANES), half)
    copies = [
        (own, held.at[0, :, here]),
        (other, held.at[0, :, there]),
    ]
    for spot, ref in enumerate(received):
        copies.append((ref.at[:, pl.ds(0, half)], held.at[1 + spot, :, here]))
        copies.append((ref.at[:, pl.ds(half, half)], held.at[1 + spot, :, there]))
    n_rows, n_cols = shards
    depth = weights[0].shape[0]
    for spot, ref in enumerate(weights):
        row = lax.rem(meta_ref[1] + n_rows - spot // n_cols, n_rows)
        col = lax.rem(meta_ref[2] + n_cols - spot % n_cols, n_cols)
        begin = pl.multiple_of((row * n_cols + col) * depth, depth)
        copies.append((ref, weight.at[pl.ds(begin, depth)]))
    copies = [pltpu.make_async_copy(a, b, sems.at[i]) for i, (a, b) in enumerate(copies)]
    for copy in copies:
        copy.start()
    for copy in copies:
        copy.wait()
    for spot, out in enumerate(outs):
        out[...] = jnp.dot(
            held[spot], weight[...], preferred_element_type=jnp.float32
        ).astype(jnp.bfloat16)


def place_kernel(count, meta_ref, *refs):
    pieces, out, sems = refs[:count], refs[count], refs[count + 1]
    wide = pieces[0].shape[-1]
    copies = []
    for spot, ref in enumerate(pieces):
        origin = lax.rem(meta_ref[3] + count - spot, count)
        where = pl.ds(pl.multiple_of(origin * wide, LANES), wide)
        copies.append(pltpu.make_async_copy(ref, out.at[:, where], sems.at[spot]))
    for copy in copies:
        copy.start()
    for copy in copies:
        copy.wait()


def cost(flops, size):
    return pl.CostEstimate(flops=flops, bytes_accessed=size, transcendentals=0)


def shards(queries, keys, values, radius, out_weight):
    n_time, n_rows, n_cols = (lax.axis_size(a) for a in ("ta", "ha", "wa"))
    at_time, at_row, at_col = (lax.axis_index(a) for a in ("ta", "ha", "wa"))
    core = at_row % PAIR
    frames, rows, cols, features = queries.shape
    heads = radius.shape[0] // PAIR
    width = features // radius.shape[0]
    half = features // PAIR
    tile_cols = cols // TILE
    area = rows * cols
    rims = n_rows > PAIR

    def tiled(block):
        block = block.reshape(frames, rows, tile_cols, TILE, block.shape[-1])
        return block.transpose(0, 2, 1, 3, 4).reshape(frames, area, block.shape[-1])

    def heads_of(which):
        def cut(x):
            return lax.dynamic_slice_in_dim(x, which * half, half, axis=-1)

        return jnp.stack(
            [cut(queries).reshape(frames, area, half), tiled(cut(keys)), tiled(cut(values))]
        )

    pairs = [(i, i ^ 1) for i in range(n_rows)]
    other = lax.ppermute(heads_of(1 - core), "ha", pairs)
    own = heads_of(core)

    def frame_queries(f):
        return jnp.concatenate([own[0, f], other[0, f]], axis=0)

    guest_after = lax.ppermute(frame_queries(0), "ta", line(n_time, -1))
    guest_before = lax.ppermute(frame_queries(frames - 1), "ta", line(n_time, 1))

    blocks = [x[1:].reshape(2, frames, tile_cols, rows * TILE, half) for x in (own, other)]
    rim = None
    if rims:
        even, odd = (jnp.where(core == i, blocks[0], blocks[1]) for i in range(PAIR))
        up = lax.ppermute(odd[:, :, :, -TILE * TILE :], "ha", line(n_rows, PAIR))
        down = lax.ppermute(even[:, :, :, : TILE * TILE], "ha", line(n_rows, -PAIR))
        blocks += [up, down]
        rim = jnp.concatenate(
            [x.reshape(2, frames, -1, half) for x in (up, down)], axis=2
        )
    low = lax.ppermute(
        jnp.concatenate([x[:, :, -1] for x in blocks], axis=2), "wa", line(n_cols, 1)
    )
    high = lax.ppermute(
        jnp.concatenate([x[:, :, 0] for x in blocks], axis=2), "wa", line(n_cols, -1)
    )

    slab = features // (n_rows * n_cols)
    wide = out_weight.shape[1] // n_time
    mine = lax.dynamic_slice_in_dim(out_weight, at_time * wide, wide, axis=1)
    mine, _ = lax.optimization_barrier((mine, other))
    weights = [mine] + [lax.ppermute(mine, "wa", cycle(n_cols, s)) for s in range(1, n_cols)]
    shard_cols = n_cols
    if slab % 16:
        weights = [jnp.roll(jnp.stack(weights[::-1]), at_col + 1, axis=0).reshape(-1, wide)]
        shard_cols = 1
    for step in range(1, n_rows):
        weights += [lax.ppermute(w, "ha", cycle(n_rows, step)) for w in weights[:shard_cols]]

    table = jnp.asarray(code_table(rows, cols, rims))
    spot = jnp.where(at_col == 0, 1, 0) + jnp.where(at_col == n_cols - 1, 2, 0)
    if rims:
        spot += jnp.where(at_row < PAIR, 4, 0) + jnp.where(at_row >= n_rows - PAIR, 8, 0)
    spot += core * (table.shape[0] // PAIR)
    code = lax.dynamic_index_in_dim(table, spot, 0, keepdims=False)
    meta = jnp.stack(
        [core, jnp.where(at_time > 0, 1, 0), jnp.where(at_time < n_time - 1, 1, 0)]
    ).astype(jnp.int32)
    place = jnp.stack([core, at_row, at_col, at_time]).astype(jnp.int32)

    parts = [own, other] + ([rim] if rims else []) + [low, high]
    count = PAIR * area
    unit = 4 * heads * width * count * code.shape[1]
    payload = jax.ShapeDtypeStruct((count, half + LANES), jnp.bfloat16)
    to_before, to_after = pl.pallas_call(
        functools.partial(guest_kernel, rims, heads, width),
        out_shape=(payload, payload),
        in_specs=[SMEM, SMEM] + [VMEM] * (1 + len(parts) + 2),
        out_specs=(VMEM, VMEM),
        compiler_params=PARAMS,
        cost_estimate=cost(2 * unit, 4_000_000),
        name="guest",
    )(meta, radius, code, *parts, guest_before, guest_after)
    from_after = lax.ppermute(to_before, "ta", line(n_time, -1))
    from_before = lax.ppermute(to_after, "ta", line(n_time, 1))
    mixed, stats = pl.pallas_call(
        functools.partial(host_kernel, rims, heads, width),
        out_shape=(
            jax.ShapeDtypeStruct((frames, count, half), jnp.float32),
            jax.ShapeDtypeStruct((frames, count, LANES), jnp.float32),
        ),
        in_specs=[SMEM, SMEM] + [VMEM] * (1 + len(parts)),
        out_specs=(VMEM, VMEM),
        compiler_params=PARAMS,
        cost_estimate=cost(7 * unit, 6_000_000),
        name="host",
    )(meta, radius, code, *parts)
    att = jax.ShapeDtypeStruct((frames, area, half), jnp.bfloat16)
    kept, given = pl.pallas_call(
        functools.partial(merge_kernel, heads, width),
        out_shape=(att, att),
        in_specs=[SMEM, SMEM] + [VMEM] * 4,
        out_specs=(VMEM, VMEM),
        compiler_params=PARAMS,
        cost_estimate=cost(1000, 3_000_000),
        name="merge",
    )(meta, radius, mixed, stats, from_before, from_after)
    tokens = frames * area
    kept = kept.reshape(tokens, half)
    taken = lax.ppermute(given, "ha", pairs).reshape(tokens, half)
    whole = jnp.concatenate([kept, taken], axis=1)
    received = [lax.ppermute(whole, "ta", cycle(n_time, s)) for s in range(1, n_time)]

    copies = 2 * n_time + len(weights)
    piece = jax.ShapeDtypeStruct((tokens, wide), jnp.bfloat16)
    products = pl.pallas_call(
        functools.partial(project_kernel, n_time - 1, len(weights), (n_rows, shard_cols)),
        out_shape=(piece,) * n_time,
        in_specs=[SMEM] + [HBM] * (1 + n_time + len(weights)),
        out_specs=(VMEM,) * n_time,
        scratch_shapes=[
            pltpu.VMEM((n_time, tokens, features), jnp.bfloat16),
            pltpu.VMEM((features, wide), jnp.bfloat16),
            pltpu.SemaphoreType.DMA((copies,)),
        ],
        compiler_params=PARAMS,
        cost_estimate=cost(2 * n_time * tokens * features * wide, 6_000_000),
        name="project",
    )(place, kept, taken, *received, *weights)
    back = [products[0]] + [
        lax.ppermute(products[n_time - s], "ta", cycle(n_time, s)) for s in range(1, n_time)
    ]
    out = pl.pallas_call(
        functools.partial(place_kernel, n_time),
        out_shape=jax.ShapeDtypeStruct((tokens, wide * n_time), jnp.bfloat16),
        in_specs=[SMEM] + [HBM] * n_time,
        out_specs=HBM,
        scratch_shapes=[pltpu.SemaphoreType.DMA((n_time,))],
        compiler_params=PARAMS,
        cost_estimate=cost(1000, 1_200_000),
        name="place",
    )(place, *back)
    return out.reshape(frames, rows, cols, wide * n_time)


def solution(mesh):
    return jax.shard_map(
        shards,
        mesh=mesh,
        in_specs=(
            P("ta", "ha", "wa", None),
            P("ta", "ha", "wa", None),
            P("ta", "ha", "wa", None),
            P(),
            P(("ha", "wa"), None),
        ),
        out_specs=P("ta", "ha", "wa", None),
        check_vma=False,
    )
```

```python
import functools
import math

import jax
import jax.numpy as jnp
import numpy as np
from jax import lax
from jax.experimental import pallas as pl
from jax.experimental.pallas import tpu as pltpu
from jax.sharding import PartitionSpec as P

TILE = 4
PAIR = 2
FAR = -1e30
LANES = 128
STRIDE = 32
VMEM = pl.BlockSpec(memory_space=pltpu.VMEM)
SMEM = pl.BlockSpec(memory_space=pltpu.SMEM)
HBM = pl.BlockSpec(memory_space=pl.ANY)
PARAMS = pltpu.CompilerParams(vmem_limit_bytes=16 * 1024 * 1024)


def cycle(count, step):
    return [(i, (i + step) % count) for i in range(count)]


def swaps(count, phase):
    partners = [(i ^ 1) if phase == 0 else ((i + 1) ^ 1) - 1 for i in range(count)]
    return [(i, p if 0 <= p < count else i) for i, p in enumerate(partners)]


def line(count, step):
    return [(i, i + step) for i in range(count) if 0 <= i + step < count]


def sides(index, count):
    even = index % 2 == 0
    inside_after, inside_before = index < count - 1, index > 0
    return (even, ~even), (
        jnp.where(even, inside_after, inside_before),
        jnp.where(even, inside_before, inside_after),
    )


def code_table(rows, cols, rims):
    tile_cols = cols // TILE
    span = rows // TILE
    tables = []
    for core in range(PAIR):
        own = core * span
        other = (1 - core) * span
        blocks = [(own, rows), (other, rows)] + ([(-1, TILE), (2 * span, TILE)] if rims else [])
        for odd in range(2):
            query_row, query_col, key_row, key_col, key_side = [], [], [], [], []
            for base in (own, other):
                for row in range(rows):
                    for col in range(cols):
                        query_row.append(base + row // TILE)
                        query_col.append(col // TILE)
            for base, length in blocks:
                for row in range(length):
                    for col in range(cols):
                        key_row.append(base + row // TILE)
                        key_col.append(col // TILE)
                        key_side.append(-1)
            for phase in range(2):
                for base, length in blocks:
                    for row in range(length):
                        for _ in range(TILE):
                            key_row.append(base + row // TILE)
                            key_col.append(tile_cols if phase == odd else -1)
                            key_side.append(phase)
            key_row, key_col, key_side = (np.array(x)[None] for x in (key_row, key_col, key_side))
            apart_row = np.abs(np.array(query_row)[:, None] - key_row)
            apart_col = np.abs(np.array(query_col)[:, None] - key_col)
            base_code = (
                2 * (apart_row == 1)
                + 4 * (apart_col == 1)
                + 8 * ((apart_row > 1) | (apart_col > 1))
            )
            outside = [key_side == 0, key_side == 1]
            outside += [key_row < 0, key_row >= 2 * span] if rims else []
            for bits in range(2 ** len(outside)):
                code = base_code
                for which, mask in enumerate(outside):
                    if bits >> which & 1:
                        code = np.where(mask, 8, code)
                tables.append(code)
    return np.stack(tables).astype(np.int32)


def head_bias(code, radius_ref, head):
    barred = (
        8
        + jnp.where(radius_ref[head, 1] == 0, 2, 0)
        + jnp.where(radius_ref[head, 2] == 0, 4, 0)
    )
    return jnp.where((code & barred) == 0, 0.0, FAR)


class Window:
    def __init__(self, refs, rims, heads, width):
        refs = list(refs)
        self.blocks = refs[:2]
        self.extra = refs[2 : 5 if rims else 4]
        self.rest = refs[5 if rims else 4 :]
        self.frames = self.blocks[0].shape[1]
        self.width = width

    def near(self, kind, frame, head):
        lanes = pl.ds(head * self.width, self.width)
        return [ref[kind, frame, :, lanes] for ref in self.blocks]

    def query(self, frame, head):
        return jnp.concatenate(self.near(0, frame, head), axis=0)

    def pair(self, frame, head):
        lanes = pl.ds(head * self.width, self.width)
        return [
            jnp.concatenate(
                self.near(1 + kind, frame, head)
                + [ref[kind, frame, :, lanes] for ref in self.extra],
                axis=0,
            )
            for kind in range(2)
        ]


def scores_of(query, key, scale):
    return (
        lax.dot_general(
            query, key, (((1,), (1,)), ((), ())), preferred_element_type=jnp.float32
        )
        * scale
    )


def edge_kernel(rims, cols, meta_ref, *refs):
    own, other = refs[:2]
    rim = refs[2] if rims else None
    sides_out, query_out = refs[-4:-2], refs[-2:]
    frames, area, half = other.shape[1:]

    def pick(rows):
        deep = rows * TILE
        shape = (2 * deep, rows * cols)
        to, of = (lax.broadcasted_iota(jnp.int32, shape, d) for d in range(2))
        spot = jnp.where(to < deep, meta_ref[5], meta_ref[6])
        to = lax.rem(to, deep)
        wanted = (to // TILE) * cols + spot * TILE + lax.rem(to, TILE)
        return deep, (of == wanted).astype(jnp.bfloat16)

    block = pick(area // cols)
    strip = pick(TILE)
    for kind in range(2):
        for frame in range(frames):
            work = [
                (own[1 + kind, frame], block),
                (other[1 + kind, frame], block),
            ]
            if rims:
                band = TILE * cols
                work += [(rim[kind, frame, i * band : (i + 1) * band], strip) for i in range(2)]
            begin = 0
            for rows, (deep, chosen) in work:
                found = jnp.dot(chosen, rows, preferred_element_type=jnp.float32)
                found = found.astype(jnp.bfloat16)
                for phase in range(2):
                    sides_out[phase][kind, frame, begin : begin + deep] = found[
                        phase * deep : (phase + 1) * deep
                    ]
                begin += deep
    for phase in range(2):
        frame = meta_ref[1 + phase]
        query_out[phase][:area] = own[0, frame]
        query_out[phase][area:] = other[0, frame]


def guest_kernel(rims, heads, width, meta_ref, radius_ref, code_ref, *refs):
    window = Window(refs, rims, heads, width)
    guests, (shard, _, *outs, sent, sem) = window.rest[:2], window.rest[2:]
    passing = pltpu.make_async_copy(shard, sent, sem)
    passing.start()
    code = code_ref[...]
    count = code.shape[0]
    scale = 1.0 / math.sqrt(width)
    first = meta_ref[0] * heads
    lane = lax.broadcasted_iota(jnp.int32, (count, LANES), 1)
    tops = [jnp.zeros((count, LANES), jnp.float32) for _ in guests]
    totals = [jnp.ones((count, LANES), jnp.float32) for _ in guests]
    work = [(head, phase) for head in range(heads) for phase in range(2)]
    score, value = {}, {}
    for head in range(heads):
        bias = head_bias(code, radius_ref, first + head)
        for phase in range(2):
            key, value[head, phase] = window.pair(meta_ref[1 + phase], head)
            query = guests[phase][:, pl.ds(head * width, width)]
            score[head, phase] = scores_of(query, key, scale) + bias
    top = {at: jnp.max(score[at], axis=1, keepdims=True) for at in work}
    expo = {at: jnp.exp(score[at] - top[at]) for at in work}
    total = {at: jnp.sum(expo[at], axis=1, keepdims=True) for at in work}
    for at in work:
        head, phase = at
        probs = (expo[at] * (1.0 / total[at])).astype(jnp.bfloat16)
        mixed = jnp.dot(probs, value[at], preferred_element_type=jnp.float32)
        outs[phase][:, pl.ds(head * width, width)] = mixed.astype(jnp.bfloat16)
        tops[phase] = jnp.where(lane == head, top[at], tops[phase])
        totals[phase] = jnp.where(lane == head, total[at], totals[phase])
    for out_ref, top, total in zip(outs, tops, totals):
        rest = top + jnp.log(total)
        stats = jnp.zeros((count, LANES), jnp.float32)
        for part in range(3):
            piece = rest.astype(jnp.bfloat16).astype(jnp.float32)
            rest = rest - piece
            stats = stats + (pltpu.roll(piece, part * STRIDE, 1) if part else piece)
        out_ref[:, pl.ds(heads * width, LANES)] = stats.astype(jnp.bfloat16)
    passing.wait()


def host_kernel(rims, heads, width, meta_ref, radius_ref, code_ref, *refs):
    window = Window(refs, rims, heads, width)
    mixed_ref, stats_ref = window.rest
    frames = window.frames
    code = code_ref[...]
    count = code.shape[0]
    scale = 1.0 / math.sqrt(width)
    first = meta_ref[0] * heads
    lane = lax.broadcasted_iota(jnp.int32, (count, LANES), 1)
    tops = [jnp.zeros((count, LANES), jnp.float32) for _ in range(frames)]
    totals = [jnp.ones((count, LANES), jnp.float32) for _ in range(frames)]
    work = [(head, f) for head in range(heads) for f in range(frames)]
    score, value = {}, {}
    for head in range(heads):
        bias = head_bias(code, radius_ref, first + head)
        bias_apart = jnp.where(radius_ref[first + head, 0] == 0, FAR, bias)
        query = [window.query(f, head) for f in range(frames)]
        pairs = [window.pair(f, head) for f in range(frames)]
        blocks = {}
        for frame in range(frames):
            near = range(max(0, frame - 1), min(frames, frame + 2))
            block = scores_of(
                jnp.concatenate([query[f] for f in near], axis=0), pairs[frame][0], scale
            )
            for spot, f in enumerate(near):
                blocks[f, frame] = block[spot * count : (spot + 1) * count] + (
                    bias if f == frame else bias_apart
                )
        for f in range(frames):
            near = range(max(0, f - 1), min(frames, f + 2))
            score[head, f] = jnp.concatenate([blocks[f, g] for g in near], axis=1)
            value[head, f] = jnp.concatenate([pairs[g][1] for g in near], axis=0)
    top = {at: jnp.max(score[at], axis=1, keepdims=True) for at in work}
    expo = {at: jnp.exp(score[at] - top[at]) for at in work}
    total = {at: jnp.sum(expo[at], axis=1, keepdims=True) for at in work}
    for at in work:
        head, f = at
        probs = (expo[at] * (1.0 / total[at])).astype(jnp.bfloat16)
        mixed_ref[f, :, pl.ds(head * width, width)] = jnp.dot(
            probs, value[at], preferred_element_type=jnp.float32
        )
        tops[f] = jnp.where(lane == head, top[at], tops[f])
        totals[f] = jnp.where(lane == head, total[at], totals[f])
    for f in range(frames):
        stats_ref[f] = tops[f] + jnp.log(totals[f])


def merge_kernel(
    heads, width, meta_ref, radius_ref, mixed_ref, stats_ref, ref_0, ref_1, _, own_out, other_out, held, logs
):
    frames, count, _ = mixed_ref.shape
    half = count // PAIR
    first = meta_ref[0] * heads
    lane = lax.broadcasted_iota(jnp.int32, (count, LANES), 1)
    use = jnp.zeros((count, LANES), jnp.int32)
    for head in range(heads):
        use = jnp.where(lane == head, radius_ref[first + head, 0], use)
    held[...] = mixed_ref[...]
    logs[...] = stats_ref[...]
    for phase, ref in enumerate((ref_0, ref_1)):
        f = meta_ref[1 + phase]
        there = jnp.where(meta_ref[3 + phase] == 0, 0, use)
        stats = ref[:, pl.ds(heads * width, LANES)].astype(jnp.float32)
        guest = (
            stats
            + pltpu.roll(stats, LANES - STRIDE, 1)
            + pltpu.roll(stats, LANES - 2 * STRIDE, 1)
        )
        guest = jnp.where(there == 0, FAR, guest)
        own = logs[f]
        top = jnp.maximum(own, guest)
        own_weight, guest_weight = jnp.exp(own - top), jnp.exp(guest - top)
        total = own_weight + guest_weight
        if frames == 1:
            logs[f] = top + jnp.log(total)
        own_weight, guest_weight = own_weight / total, guest_weight / total
        for head in range(heads):
            lanes = pl.ds(head * width, width)
            held[f, :, lanes] = (
                held[f, :, lanes] * own_weight[:, head : head + 1]
                + ref[:, lanes].astype(jnp.float32) * guest_weight[:, head : head + 1]
            )
    mixed = held[...].astype(jnp.bfloat16)
    own_out[...] = mixed[:, :half]
    other_out[...] = mixed[:, half:]


def join_kernel(count, meta_ref, *refs):
    pieces, out = refs[:count], refs[-1]
    depth = pieces[0].shape[0]
    for spot, ref in enumerate(pieces):
        begin = pl.multiple_of(meta_ref[spot] * depth, depth)
        out[pl.ds(begin, depth)] = ref[...]


def project_kernel(*refs):
    rows, (near, far), out = refs[:-3], refs[-3:-1], refs[-1]
    half = near.shape[0]
    if len(rows) == 1:
        first, second = rows[0][:, :half], rows[0][:, half:]
    else:
        first, second = rows[0][...], rows[1][...]
    out[...] = (
        jnp.dot(first, near[...], preferred_element_type=jnp.float32)
        + jnp.dot(second, far[...], preferred_element_type=jnp.float32)
    ).astype(out.dtype)


def place_kernel(count, meta_ref, *refs):
    pieces, out, sems = refs[:count], refs[count], refs[count + 1]
    wide = pieces[0].shape[-1]
    copies = []
    for spot, ref in enumerate(pieces):
        origin = lax.rem(meta_ref[0] + count - spot, count)
        where = pl.ds(pl.multiple_of(origin * wide, LANES), wide)
        copies.append(pltpu.make_async_copy(ref, out.at[:, where], sems.at[spot]))
    for copy in copies:
        copy.start()
    for copy in copies:
        copy.wait()


def cost(flops, size):
    return pl.CostEstimate(flops=flops, bytes_accessed=size, transcendentals=0)


def shards(queries, keys, values, radius, out_weight):
    n_time, n_rows, n_cols = (lax.axis_size(a) for a in ("ta", "ha", "wa"))
    at_time, at_row, at_col = (lax.axis_index(a) for a in ("ta", "ha", "wa"))
    core = at_row % PAIR
    frames, rows, cols, features = queries.shape
    heads = radius.shape[0] // PAIR
    width = features // radius.shape[0]
    half = features // PAIR
    tile_cols = cols // TILE
    area = rows * cols
    rims = n_rows > PAIR

    after, there = sides(at_col, n_cols)
    later, present = sides(at_time, n_time)
    ends = [jnp.where(x, frames - 1, 0) for x in later]
    borders = [jnp.where(x, tile_cols - 1, 0) for x in after]
    meta = jnp.stack([core, *ends, *present, *borders]).astype(jnp.int32)

    raw = [x.reshape(frames, area, features) for x in (queries, keys, values)]
    pairs = [(i, i ^ 1) for i in range(n_rows)]
    own, other = (
        jnp.stack([lax.dynamic_slice_in_dim(x, which * half, half, axis=2) for x in raw])
        for which in (core, 1 - core)
    )
    other = lax.ppermute(other, "ha", pairs)
    rim = None
    if rims:
        even, odd = (jnp.where(core == i, own[1:], other[1:]) for i in range(PAIR))
        band = TILE * cols
        up = lax.ppermute(odd[:, :, -band:], "ha", line(n_rows, PAIR))
        down = lax.ppermute(even[:, :, :band], "ha", line(n_rows, -PAIR))
        rim = jnp.concatenate([up, down], axis=2)
    deep = PAIR * rows * TILE + (PAIR * TILE * TILE if rims else 0)
    side = jax.ShapeDtypeStruct((2, frames, deep, half), queries.dtype)
    end = jax.ShapeDtypeStruct((PAIR * area, half), queries.dtype)
    *edges, first_end, second_end = pl.pallas_call(
        functools.partial(edge_kernel, rims, cols),
        out_shape=(side, side, end, end),
        in_specs=[SMEM] + [VMEM] * (3 if rims else 2),
        out_specs=(VMEM,) * 4,
        compiler_params=PARAMS,
        cost_estimate=cost(1000, 2_000_000),
        name="edge",
    )(meta, own, other, *([rim] if rims else []))
    beside = [lax.ppermute(x, "wa", swaps(n_cols, phase)) for phase, x in enumerate(edges)]
    guests = [
        lax.ppermute(x, "ta", swaps(n_time, phase))
        for phase, x in enumerate((first_end, second_end))
    ]

    slab = features // (n_rows * n_cols)
    wide = out_weight.shape[1] // n_time
    mine = lax.dynamic_slice_in_dim(out_weight, at_time * wide, wide, axis=1)
    held = {0: mine}
    if n_cols > 1:
        held[n_cols - 1] = lax.ppermute(mine, "wa", cycle(n_cols, n_cols - 1))

    table = jnp.asarray(code_table(rows, cols, rims))
    absent = [~x for x in there]
    if rims:
        absent += [at_row < PAIR, at_row >= n_rows - PAIR]
    spot = core * 2 + at_col % 2
    spot = spot * 2 ** len(absent) + sum(jnp.where(x, 2**i, 0) for i, x in enumerate(absent))
    code = lax.dynamic_index_in_dim(table, spot, 0, keepdims=False)
    place = jnp.stack([at_time]).astype(jnp.int32)

    parts = [own, other] + ([rim] if rims else []) + beside
    count = PAIR * area
    unit = 4 * heads * width * count * code.shape[1]
    payload = jax.ShapeDtypeStruct((count, half + LANES), jnp.bfloat16)
    *answers, sent = pl.pallas_call(
        functools.partial(guest_kernel, rims, heads, width),
        out_shape=(payload, payload, jax.ShapeDtypeStruct(mine.shape, mine.dtype)),
        in_specs=[SMEM, SMEM] + [VMEM] * (1 + len(parts) + 2) + [VMEM, HBM],
        out_specs=(VMEM, VMEM, VMEM),
        scratch_shapes=[pltpu.SemaphoreType.DMA],
        compiler_params=PARAMS,
        cost_estimate=cost(2 * unit, 4_000_000),
        name="guest",
    )(meta, radius, code, *parts, *guests, mine, held[max(held)])
    if n_cols > 2:
        held[1] = lax.ppermute(sent, "wa", cycle(n_cols, 1))
    answers = [
        lax.ppermute(x, "ta", swaps(n_time, phase)) for phase, x in enumerate(answers)
    ]
    mixed_shape, stats_shape = (frames, count, half), (frames, count, LANES)
    mixed, stats = pl.pallas_call(
        functools.partial(host_kernel, rims, heads, width),
        out_shape=(
            jax.ShapeDtypeStruct(mixed_shape, jnp.float32),
            jax.ShapeDtypeStruct(stats_shape, jnp.float32),
        ),
        in_specs=[SMEM, SMEM] + [VMEM] * (1 + len(parts)),
        out_specs=(VMEM, VMEM),
        compiler_params=PARAMS,
        cost_estimate=cost(7 * unit, 6_000_000),
        name="host",
    )(meta, radius, code, *parts)
    att = jax.ShapeDtypeStruct((frames, area, half), jnp.bfloat16)
    kept, given = pl.pallas_call(
        functools.partial(merge_kernel, heads, width),
        out_shape=(att, att),
        in_specs=[SMEM, SMEM] + [VMEM] * 4 + [HBM],
        out_specs=(VMEM, VMEM),
        scratch_shapes=[
            pltpu.VMEM(mixed_shape, jnp.float32),
            pltpu.VMEM(stats_shape, jnp.float32),
        ],
        compiler_params=PARAMS,
        cost_estimate=cost(1000, 3_000_000),
        name="merge",
    )(meta, radius, mixed, stats, *answers, held[min(1, n_cols - 1)])
    tokens = frames * area
    kept = kept.reshape(tokens, half)
    taken = lax.ppermute(given, "ha", pairs).reshape(tokens, half)
    whole = jnp.concatenate([kept, taken], axis=1)
    for s in range(1, n_cols):
        if s not in held:
            held[s] = lax.ppermute(sent, "wa", cycle(n_cols, s))
    received = [lax.ppermute(whole, "ta", cycle(n_time, s)) for s in range(1, n_time)]

    def joined(shards, at):
        count = len(shards)
        spots = jnp.stack([(at - s) % count for s in range(count)]).astype(jnp.int32)
        if shards[0].shape[0] % 16:
            return jnp.roll(jnp.stack(shards[::-1]), at + 1, axis=0).reshape(-1, wide)
        return pl.pallas_call(
            functools.partial(join_kernel, count),
            out_shape=jax.ShapeDtypeStruct((count * shards[0].shape[0], wide), mine.dtype),
            in_specs=[SMEM] + [VMEM] * count + [HBM] * len(received),
            out_specs=VMEM,
            compiler_params=PARAMS,
            cost_estimate=cost(1000, 2_400_000),
            name="join",
        )(spots, *shards, *received)

    near = joined([held[s] for s in range(n_cols)], at_col)
    across = [lax.ppermute(near, "ha", cycle(n_rows, r)) for r in range(1, n_rows)]
    if n_rows == PAIR:
        far = across[0]
    else:
        full = joined([near, *across], at_row)
        near, far = (
            lax.dynamic_slice_in_dim(full, which * half, half, axis=0)
            for which in (core, 1 - core)
        )

    def project(*rows):
        return pl.pallas_call(
            project_kernel,
            out_shape=jax.ShapeDtypeStruct((tokens, wide), queries.dtype),
            in_specs=[VMEM] * (len(rows) + 2),
            out_specs=VMEM,
            compiler_params=PARAMS,
            cost_estimate=cost(2 * tokens * features * wide, 3_000_000),
            name="project",
        )(*rows, near, far)

    products = [project(kept, taken)] + [project(x) for x in received]
    back = [products[0]] + [
        lax.ppermute(products[n_time - s], "ta", cycle(n_time, s)) for s in range(1, n_time)
    ]
    out = pl.pallas_call(
        functools.partial(place_kernel, n_time),
        out_shape=jax.ShapeDtypeStruct((tokens, wide * n_time), jnp.bfloat16),
        in_specs=[SMEM] + [HBM] * n_time,
        out_specs=HBM,
        scratch_shapes=[pltpu.SemaphoreType.DMA((n_time,))],
        compiler_params=PARAMS,
        cost_estimate=cost(1000, 1_200_000),
        name="place",
    )(place, *back)
    return out.reshape(frames, rows, cols, wide * n_time)


def solution(mesh):
    return jax.shard_map(
        shards,
        mesh=mesh,
        in_specs=(
            P("ta", "ha", "wa", None),
            P("ta", "ha", "wa", None),
            P("ta", "ha", "wa", None),
            P(),
            P(("ha", "wa"), None),
        ),
        out_specs=P("ta", "ha", "wa", None),
        check_vma=False,
    )
```

```python
import functools
import math

import jax
import jax.numpy as jnp
import numpy as np
from jax import lax
from jax.experimental import pallas as pl
from jax.experimental.pallas import tpu as pltpu
from jax.sharding import PartitionSpec as P

TILE = 4
PAIR = 2
FAR = -1e30
LANES = 128
STRIDE = 32
VMEM = pl.BlockSpec(memory_space=pltpu.VMEM)
SMEM = pl.BlockSpec(memory_space=pltpu.SMEM)
HBM = pl.BlockSpec(memory_space=pl.ANY)
PARAMS = pltpu.CompilerParams(vmem_limit_bytes=16 * 1024 * 1024)


def cycle(count, step):
    return [(i, (i + step) % count) for i in range(count)]


def swaps(count, phase):
    partners = [(i ^ 1) if phase == 0 else ((i + 1) ^ 1) - 1 for i in range(count)]
    return [(i, p if 0 <= p < count else i) for i, p in enumerate(partners)]


def line(count, step):
    return [(i, i + step) for i in range(count) if 0 <= i + step < count]


def sides(index, count):
    even = index % 2 == 0
    inside_after, inside_before = index < count - 1, index > 0
    return (even, ~even), (
        jnp.where(even, inside_after, inside_before),
        jnp.where(even, inside_before, inside_after),
    )


def code_table(rows, cols, rims):
    tile_cols = cols // TILE
    span = rows // TILE
    tables = []
    for core in range(PAIR):
        own = core * span
        other = (1 - core) * span
        blocks = [(own, rows), (other, rows)] + ([(-1, TILE), (2 * span, TILE)] if rims else [])
        for odd in range(2):
            query_row, query_col, key_row, key_col, key_side = [], [], [], [], []
            for base in (own, other):
                for row in range(rows):
                    for col in range(cols):
                        query_row.append(base + row // TILE)
                        query_col.append(col // TILE)
            for base, length in blocks:
                for row in range(length):
                    for col in range(cols):
                        key_row.append(base + row // TILE)
                        key_col.append(col // TILE)
                        key_side.append(-1)
            for phase in range(2):
                for base, length in blocks:
                    for row in range(length):
                        for _ in range(TILE):
                            key_row.append(base + row // TILE)
                            key_col.append(tile_cols if phase == odd else -1)
                            key_side.append(phase)
            key_row, key_col, key_side = (np.array(x)[None] for x in (key_row, key_col, key_side))
            apart_row = np.abs(np.array(query_row)[:, None] - key_row)
            apart_col = np.abs(np.array(query_col)[:, None] - key_col)
            base_code = (
                2 * (apart_row == 1)
                + 4 * (apart_col == 1)
                + 8 * ((apart_row > 1) | (apart_col > 1))
            )
            outside = [key_side == 0, key_side == 1]
            outside += [key_row < 0, key_row >= 2 * span] if rims else []
            for bits in range(2 ** len(outside)):
                code = base_code
                for which, mask in enumerate(outside):
                    if bits >> which & 1:
                        code = np.where(mask, 8, code)
                tables.append(code)
    return np.stack(tables).astype(np.int32)


def head_bias(code, radius_ref, head):
    barred = (
        8
        + jnp.where(radius_ref[head, 1] == 0, 2, 0)
        + jnp.where(radius_ref[head, 2] == 0, 4, 0)
    )
    return jnp.where((code & barred) == 0, 0.0, FAR)


class Window:
    def __init__(self, refs, rims, heads, width):
        refs = list(refs)
        self.blocks = refs[:2]
        self.extra = refs[2 : 5 if rims else 4]
        self.rest = refs[5 if rims else 4 :]
        self.frames = self.blocks[0].shape[1]
        self.width = width

    def near(self, kind, frame, head):
        lanes = pl.ds(head * self.width, self.width)
        return [ref[kind, frame, :, lanes] for ref in self.blocks]

    def query(self, frame, head):
        return jnp.concatenate(self.near(0, frame, head), axis=0)

    def pair(self, frame, head):
        lanes = pl.ds(head * self.width, self.width)
        return [
            jnp.concatenate(
                self.near(1 + kind, frame, head)
                + [ref[kind, frame, :, lanes] for ref in self.extra],
                axis=0,
            )
            for kind in range(2)
        ]


def scores_of(query, key, scale):
    return (
        lax.dot_general(
            query, key, (((1,), (1,)), ((), ())), preferred_element_type=jnp.float32
        )
        * scale
    )


def edge_kernel(rims, cols, meta_ref, *refs):
    own, other = refs[:2]
    rim = refs[2] if rims else None
    sides_out, query_out = refs[-4:-2], refs[-2:]
    frames, area, half = other.shape[1:]

    def pick(rows):
        deep = rows * TILE
        shape = (2 * deep, rows * cols)
        to, of = (lax.broadcasted_iota(jnp.int32, shape, d) for d in range(2))
        spot = jnp.where(to < deep, meta_ref[5], meta_ref[6])
        to = lax.rem(to, deep)
        wanted = (to // TILE) * cols + spot * TILE + lax.rem(to, TILE)
        return deep, (of == wanted).astype(jnp.bfloat16)

    block = pick(area // cols)
    strip = pick(TILE)
    for kind in range(2):
        for frame in range(frames):
            work = [
                (own[1 + kind, frame], block),
                (other[1 + kind, frame], block),
            ]
            if rims:
                band = TILE * cols
                work += [(rim[kind, frame, i * band : (i + 1) * band], strip) for i in range(2)]
            begin = 0
            for rows, (deep, chosen) in work:
                found = jnp.dot(chosen, rows, preferred_element_type=jnp.float32)
                found = found.astype(jnp.bfloat16)
                for phase in range(2):
                    sides_out[phase][kind, frame, begin : begin + deep] = found[
                        phase * deep : (phase + 1) * deep
                    ]
                begin += deep
    for phase in range(2):
        frame = meta_ref[1 + phase]
        query_out[phase][:area] = own[0, frame]
        query_out[phase][area:] = other[0, frame]


def guest_kernel(rims, heads, width, meta_ref, radius_ref, code_ref, *refs):
    window = Window(refs, rims, heads, width)
    guests, (shard, *outs, sent, sem) = window.rest[:2], window.rest[2:]
    passing = pltpu.make_async_copy(shard, sent, sem)
    passing.start()
    code = code_ref[...]
    count = code.shape[0]
    scale = 1.0 / math.sqrt(width)
    first = meta_ref[0] * heads
    lane = lax.broadcasted_iota(jnp.int32, (count, LANES), 1)
    tops = [jnp.zeros((count, LANES), jnp.float32) for _ in guests]
    totals = [jnp.ones((count, LANES), jnp.float32) for _ in guests]
    work = [(head, phase) for head in range(heads) for phase in range(2)]
    score, value = {}, {}
    for head in range(heads):
        bias = head_bias(code, radius_ref, first + head)
        for phase in range(2):
            key, value[head, phase] = window.pair(meta_ref[1 + phase], head)
            query = guests[phase][:, pl.ds(head * width, width)]
            score[head, phase] = scores_of(query, key, scale) + bias
    top = {at: jnp.max(score[at], axis=1, keepdims=True) for at in work}
    expo = {at: jnp.exp(score[at] - top[at]) for at in work}
    total = {at: jnp.sum(expo[at], axis=1, keepdims=True) for at in work}
    for at in work:
        head, phase = at
        probs = (expo[at] * (1.0 / total[at])).astype(jnp.bfloat16)
        mixed = jnp.dot(probs, value[at], preferred_element_type=jnp.float32)
        outs[phase][:, pl.ds(head * width, width)] = mixed.astype(jnp.bfloat16)
        tops[phase] = jnp.where(lane == head, top[at], tops[phase])
        totals[phase] = jnp.where(lane == head, total[at], totals[phase])
    for out_ref, top, total in zip(outs, tops, totals):
        rest = top + jnp.log(total)
        stats = jnp.zeros((count, LANES), jnp.float32)
        for part in range(3):
            piece = rest.astype(jnp.bfloat16).astype(jnp.float32)
            rest = rest - piece
            stats = stats + (pltpu.roll(piece, part * STRIDE, 1) if part else piece)
        out_ref[:, pl.ds(heads * width, LANES)] = stats.astype(jnp.bfloat16)
    passing.wait()


def host_kernel(rims, heads, width, meta_ref, radius_ref, code_ref, *refs):
    window = Window(refs, rims, heads, width)
    mixed_ref, stats_ref = window.rest
    frames = window.frames
    code = code_ref[...]
    count = code.shape[0]
    scale = 1.0 / math.sqrt(width)
    first = meta_ref[0] * heads
    lane = lax.broadcasted_iota(jnp.int32, (count, LANES), 1)
    tops = [jnp.zeros((count, LANES), jnp.float32) for _ in range(frames)]
    totals = [jnp.ones((count, LANES), jnp.float32) for _ in range(frames)]
    work = [(head, f) for head in range(heads) for f in range(frames)]
    score, value = {}, {}
    for head in range(heads):
        bias = head_bias(code, radius_ref, first + head)
        bias_apart = jnp.where(radius_ref[first + head, 0] == 0, FAR, bias)
        query = [window.query(f, head) for f in range(frames)]
        pairs = [window.pair(f, head) for f in range(frames)]
        blocks = {}
        for frame in range(frames):
            near = range(max(0, frame - 1), min(frames, frame + 2))
            block = scores_of(
                jnp.concatenate([query[f] for f in near], axis=0), pairs[frame][0], scale
            )
            for spot, f in enumerate(near):
                blocks[f, frame] = block[spot * count : (spot + 1) * count] + (
                    bias if f == frame else bias_apart
                )
        for f in range(frames):
            near = range(max(0, f - 1), min(frames, f + 2))
            score[head, f] = jnp.concatenate([blocks[f, g] for g in near], axis=1)
            value[head, f] = jnp.concatenate([pairs[g][1] for g in near], axis=0)
    top = {at: jnp.max(score[at], axis=1, keepdims=True) for at in work}
    expo = {at: jnp.exp(score[at] - top[at]) for at in work}
    total = {at: jnp.sum(expo[at], axis=1, keepdims=True) for at in work}
    for at in work:
        head, f = at
        probs = (expo[at] * (1.0 / total[at])).astype(jnp.bfloat16)
        mixed_ref[f, :, pl.ds(head * width, width)] = jnp.dot(
            probs, value[at], preferred_element_type=jnp.float32
        )
        tops[f] = jnp.where(lane == head, top[at], tops[f])
        totals[f] = jnp.where(lane == head, total[at], totals[f])
    for f in range(frames):
        stats_ref[f] = tops[f] + jnp.log(totals[f])


def merge_kernel(
    heads, width, meta_ref, radius_ref, mixed_ref, stats_ref, ref_0, ref_1, out_ref, held, logs
):
    frames, count, _ = mixed_ref.shape
    half = count // PAIR
    first = meta_ref[0] * heads
    lane = lax.broadcasted_iota(jnp.int32, (count, LANES), 1)
    use = jnp.zeros((count, LANES), jnp.int32)
    for head in range(heads):
        use = jnp.where(lane == head, radius_ref[first + head, 0], use)
    held[...] = mixed_ref[...]
    logs[...] = stats_ref[...]
    for phase, ref in enumerate((ref_0, ref_1)):
        f = meta_ref[1 + phase]
        there = jnp.where(meta_ref[3 + phase] == 0, 0, use)
        stats = ref[:, pl.ds(heads * width, LANES)].astype(jnp.float32)
        guest = (
            stats
            + pltpu.roll(stats, LANES - STRIDE, 1)
            + pltpu.roll(stats, LANES - 2 * STRIDE, 1)
        )
        guest = jnp.where(there == 0, FAR, guest)
        own = logs[f]
        top = jnp.maximum(own, guest)
        own_weight, guest_weight = jnp.exp(own - top), jnp.exp(guest - top)
        total = own_weight + guest_weight
        if frames == 1:
            logs[f] = top + jnp.log(total)
        own_weight, guest_weight = own_weight / total, guest_weight / total
        for head in range(heads):
            lanes = pl.ds(head * width, width)
            held[f, :, lanes] = (
                held[f, :, lanes] * own_weight[:, head : head + 1]
                + ref[:, lanes].astype(jnp.float32) * guest_weight[:, head : head + 1]
            )
    mixed = held[...].astype(jnp.bfloat16)
    for part in range(PAIR):
        out_ref[part] = mixed[:, part * half : (part + 1) * half]


def join_kernel(count, meta_ref, *refs):
    pieces, out = refs[:count], refs[-1]
    depth = pieces[0].shape[0]
    for spot, ref in enumerate(pieces):
        begin = pl.multiple_of(meta_ref[spot] * depth, depth)
        out[pl.ds(begin, depth)] = ref[...]


def project_kernel(rows, near, own_out, other_out):
    both = jnp.dot(rows[...], near[...], preferred_element_type=jnp.float32)
    half = own_out.shape[0]
    own_out[...] = both[:half]
    other_out[...] = both[half:]


def total_kernel(part, partner, out):
    out[...] = (part[...] + partner[...]).astype(out.dtype)


def place_kernel(count, meta_ref, *refs):
    pieces, out, sems = refs[:count], refs[count], refs[count + 1]
    wide = pieces[0].shape[-1]
    copies = []
    for spot, ref in enumerate(pieces):
        origin = lax.rem(meta_ref[0] + count - spot, count)
        where = pl.ds(pl.multiple_of(origin * wide, LANES), wide)
        copies.append(pltpu.make_async_copy(ref, out.at[:, where], sems.at[spot]))
    for copy in copies:
        copy.start()
    for copy in copies:
        copy.wait()


def cost(flops, size):
    return pl.CostEstimate(flops=flops, bytes_accessed=size, transcendentals=0)


def shards(queries, keys, values, radius, out_weight):
    n_time, n_rows, n_cols = (lax.axis_size(a) for a in ("ta", "ha", "wa"))
    at_time, at_row, at_col = (lax.axis_index(a) for a in ("ta", "ha", "wa"))
    core = at_row % PAIR
    frames, rows, cols, features = queries.shape
    heads = radius.shape[0] // PAIR
    width = features // radius.shape[0]
    half = features // PAIR
    tile_cols = cols // TILE
    area = rows * cols
    rims = n_rows > PAIR

    after, there = sides(at_col, n_cols)
    later, present = sides(at_time, n_time)
    ends = [jnp.where(x, frames - 1, 0) for x in later]
    borders = [jnp.where(x, tile_cols - 1, 0) for x in after]
    meta = jnp.stack([core, *ends, *present, *borders]).astype(jnp.int32)

    raw = [x.reshape(frames, area, features) for x in (queries, keys, values)]
    pairs = [(i, i ^ 1) for i in range(n_rows)]
    own, other = (
        jnp.stack([lax.dynamic_slice_in_dim(x, which * half, half, axis=2) for x in raw])
        for which in (core, 1 - core)
    )
    other = lax.ppermute(other, "ha", pairs)
    rim = None
    if rims:
        even, odd = (jnp.where(core == i, own[1:], other[1:]) for i in range(PAIR))
        band = TILE * cols
        up = lax.ppermute(odd[:, :, -band:], "ha", line(n_rows, PAIR))
        down = lax.ppermute(even[:, :, :band], "ha", line(n_rows, -PAIR))
        rim = jnp.concatenate([up, down], axis=2)
    deep = PAIR * rows * TILE + (PAIR * TILE * TILE if rims else 0)
    side = jax.ShapeDtypeStruct((2, frames, deep, half), queries.dtype)
    end = jax.ShapeDtypeStruct((PAIR * area, half), queries.dtype)
    *edges, first_end, second_end = pl.pallas_call(
        functools.partial(edge_kernel, rims, cols),
        out_shape=(side, side, end, end),
        in_specs=[SMEM] + [VMEM] * (3 if rims else 2),
        out_specs=(VMEM,) * 4,
        compiler_params=PARAMS,
        cost_estimate=cost(1000, 2_000_000),
        name="edge",
    )(meta, own, other, *([rim] if rims else []))
    beside = [lax.ppermute(x, "wa", swaps(n_cols, phase)) for phase, x in enumerate(edges)]
    guests = [
        lax.ppermute(x, "ta", swaps(n_time, phase))
        for phase, x in enumerate((first_end, second_end))
    ]

    slab = features // (n_rows * n_cols)
    wide = out_weight.shape[1] // n_time
    mine = lax.dynamic_slice_in_dim(out_weight, at_time * wide, wide, axis=1)
    held = {0: mine}
    if n_cols > 1:
        held[1] = lax.ppermute(mine, "wa", cycle(n_cols, 1))

    table = jnp.asarray(code_table(rows, cols, rims))
    absent = [~x for x in there]
    if rims:
        absent += [at_row < PAIR, at_row >= n_rows - PAIR]
    spot = core * 2 + at_col % 2
    spot = spot * 2 ** len(absent) + sum(jnp.where(x, 2**i, 0) for i, x in enumerate(absent))
    code = lax.dynamic_index_in_dim(table, spot, 0, keepdims=False)
    place = jnp.stack([at_time]).astype(jnp.int32)

    parts = [own, other] + ([rim] if rims else []) + beside
    count = PAIR * area
    unit = 4 * heads * width * count * code.shape[1]
    payload = jax.ShapeDtypeStruct((count, half + LANES), jnp.bfloat16)
    *answers, sent = pl.pallas_call(
        functools.partial(guest_kernel, rims, heads, width),
        out_shape=(payload, payload, jax.ShapeDtypeStruct(mine.shape, mine.dtype)),
        in_specs=[SMEM, SMEM] + [VMEM] * (1 + len(parts) + 2) + [VMEM],
        out_specs=(VMEM, VMEM, VMEM),
        scratch_shapes=[pltpu.SemaphoreType.DMA],
        compiler_params=PARAMS,
        cost_estimate=cost(2 * unit, 4_000_000),
        name="guest",
    )(meta, radius, code, *parts, *guests, held[min(1, n_cols - 1)])
    if n_cols > 2:
        held[2] = lax.ppermute(sent, "wa", cycle(n_cols, 1))
    answers = [
        lax.ppermute(x, "ta", swaps(n_time, phase)) for phase, x in enumerate(answers)
    ]
    mixed_shape, stats_shape = (frames, count, half), (frames, count, LANES)
    mixed, stats = pl.pallas_call(
        functools.partial(host_kernel, rims, heads, width),
        out_shape=(
            jax.ShapeDtypeStruct(mixed_shape, jnp.float32),
            jax.ShapeDtypeStruct(stats_shape, jnp.float32),
        ),
        in_specs=[SMEM, SMEM] + [VMEM] * (1 + len(parts)),
        out_specs=(VMEM, VMEM),
        compiler_params=PARAMS,
        cost_estimate=cost(7 * unit, 6_000_000),
        name="host",
    )(meta, radius, code, *parts)
    attended = pl.pallas_call(
        functools.partial(merge_kernel, heads, width),
        out_shape=jax.ShapeDtypeStruct((PAIR, frames, area, half), jnp.bfloat16),
        in_specs=[SMEM, SMEM] + [VMEM] * 4,
        out_specs=VMEM,
        scratch_shapes=[
            pltpu.VMEM(mixed_shape, jnp.float32),
            pltpu.VMEM(stats_shape, jnp.float32),
        ],
        compiler_params=PARAMS,
        cost_estimate=cost(1000, 3_000_000),
        name="merge",
    )(meta, radius, mixed, stats, *answers)
    tokens = frames * area
    attended = attended.reshape(PAIR * tokens, half)
    for s in range(3, n_cols):
        held[s] = lax.ppermute(held[s - 1], "wa", cycle(n_cols, 1))
    received = [lax.ppermute(attended, "ta", cycle(n_time, s)) for s in range(1, n_time)]

    def joined(shards, at):
        count = len(shards)
        spots = jnp.stack([(at - s) % count for s in range(count)]).astype(jnp.int32)
        if shards[0].shape[0] % 16:
            return jnp.roll(jnp.stack(shards[::-1]), at + 1, axis=0).reshape(-1, wide)
        return pl.pallas_call(
            functools.partial(join_kernel, count),
            out_shape=jax.ShapeDtypeStruct((count * shards[0].shape[0], wide), mine.dtype),
            in_specs=[SMEM] + [VMEM] * count + [HBM],
            out_specs=VMEM,
            compiler_params=PARAMS,
            cost_estimate=cost(1000, 2_400_000),
            name="join",
        )(spots, *shards, received[0])

    near = joined([held[s] for s in range(n_cols)], at_col)
    if n_rows > PAIR:
        across = [lax.ppermute(near, "ha", cycle(n_rows, r)) for r in range(1, n_rows)]
        near = lax.dynamic_slice_in_dim(joined([near, *across], at_row), core * half, half, axis=0)

    def project(block):
        part = jax.ShapeDtypeStruct((tokens, wide), jnp.float32)
        return pl.pallas_call(
            project_kernel,
            out_shape=(part, part),
            in_specs=[VMEM, VMEM],
            out_specs=(VMEM, VMEM),
            compiler_params=PARAMS,
            cost_estimate=cost(2 * tokens * features * wide, 3_000_000),
            name="project",
        )(block, near)

    def total(part, partner):
        return pl.pallas_call(
            total_kernel,
            out_shape=jax.ShapeDtypeStruct((tokens, wide), queries.dtype),
            in_specs=[VMEM, VMEM],
            out_specs=VMEM,
            compiler_params=PARAMS,
            cost_estimate=cost(tokens * wide, 3_000_000),
            name="total",
        )(part, partner)

    products = []
    for block in [attended, *received]:
        part, given = project(block)
        products.append(total(part, lax.ppermute(given, "ha", pairs)))
    back = [products[0]] + [
        lax.ppermute(products[n_time - s], "ta", cycle(n_time, s)) for s in range(1, n_time)
    ]
    out = pl.pallas_call(
        functools.partial(place_kernel, n_time),
        out_shape=jax.ShapeDtypeStruct((tokens, wide * n_time), jnp.bfloat16),
        in_specs=[SMEM] + [HBM] * n_time,
        out_specs=HBM,
        scratch_shapes=[pltpu.SemaphoreType.DMA((n_time,))],
        compiler_params=PARAMS,
        cost_estimate=cost(1000, 1_200_000),
        name="place",
    )(place, *back)
    return out.reshape(frames, rows, cols, wide * n_time)


def solution(mesh):
    return jax.shard_map(
        shards,
        mesh=mesh,
        in_specs=(
            P("ta", "ha", "wa", None),
            P("ta", "ha", "wa", None),
            P("ta", "ha", "wa", None),
            P(),
            P(("ha", "wa"), None),
        ),
        out_specs=P("ta", "ha", "wa", None),
        check_vma=False,
    )
```

```python
import functools
import math

import jax
import jax.numpy as jnp
import numpy as np
from jax import lax
from jax.experimental import pallas as pl
from jax.experimental.pallas import tpu as pltpu
from jax.sharding import PartitionSpec as P

TILE = 4
PAIR = 2
FAR = -1e30
LANES = 128
STRIDE = 32
VMEM = pl.BlockSpec(memory_space=pltpu.VMEM)
SMEM = pl.BlockSpec(memory_space=pltpu.SMEM)
HBM = pl.BlockSpec(memory_space=pl.ANY)
PARAMS = pltpu.CompilerParams(vmem_limit_bytes=16 * 1024 * 1024)


def cycle(count, step):
    return [(i, (i + step) % count) for i in range(count)]


def swaps(count, phase, n_rows, rows_first):
    pairs = []
    for row in range(n_rows):
        for i in range(count):
            p = (i ^ 1) if phase == 0 else ((i + 1) ^ 1) - 1
            ends = ((row, i), (row, p) if 0 <= p < count else (row ^ 1, i))
            pairs.append(tuple(r * count + j if rows_first else j * n_rows + r for r, j in ends))
    return pairs


def line(count, step):
    return [(i, i + step) for i in range(count) if 0 <= i + step < count]


def sides(index, count):
    even = index % 2 == 0
    inside_after, inside_before = index < count - 1, index > 0
    return (even, ~even), (
        jnp.where(even, inside_after, inside_before),
        jnp.where(even, inside_before, inside_after),
    )


def code_table(rows, cols, rims):
    tile_cols = cols // TILE
    span = rows // TILE
    tables = []
    for core in range(PAIR):
        own = core * span
        other = (1 - core) * span
        blocks = [(own, rows), (other, rows)] + ([(-1, TILE), (2 * span, TILE)] if rims else [])
        for odd in range(2):
            query_row, query_col, key_row, key_col, key_side = [], [], [], [], []
            for base in (own, other):
                for row in range(rows):
                    for col in range(cols):
                        query_row.append(base + row // TILE)
                        query_col.append(col // TILE)
            for base, length in blocks:
                for row in range(length):
                    for col in range(cols):
                        key_row.append(base + row // TILE)
                        key_col.append(col // TILE)
                        key_side.append(-1)
            for phase in range(2):
                for base, length in blocks:
                    for row in range(length):
                        for _ in range(TILE):
                            key_row.append(base + row // TILE)
                            key_col.append(tile_cols if phase == odd else -1)
                            key_side.append(phase)
            key_row, key_col, key_side = (np.array(x)[None] for x in (key_row, key_col, key_side))
            apart_row = np.abs(np.array(query_row)[:, None] - key_row)
            apart_col = np.abs(np.array(query_col)[:, None] - key_col)
            base_code = (
                2 * (apart_row == 1)
                + 4 * (apart_col == 1)
                + 8 * ((apart_row > 1) | (apart_col > 1))
            )
            outside = [key_side == 0, key_side == 1]
            outside += [key_row < 0, key_row >= 2 * span] if rims else []
            for bits in range(2 ** len(outside)):
                code = base_code
                for which, mask in enumerate(outside):
                    if bits >> which & 1:
                        code = np.where(mask, 8, code)
                tables.append(code)
    return np.stack(tables).astype(np.int32)


def head_bias(code, radius_ref, head):
    barred = (
        8
        + jnp.where(radius_ref[head, 1] == 0, 2, 0)
        + jnp.where(radius_ref[head, 2] == 0, 4, 0)
    )
    return jnp.where((code & barred) == 0, 0.0, FAR)


class Window:
    def __init__(self, refs, rims, heads, width):
        refs = list(refs)
        self.blocks = refs[:2]
        self.extra = refs[2 : 5 if rims else 4]
        self.rest = refs[5 if rims else 4 :]
        self.frames = self.blocks[0].shape[1]
        self.width = width

    def near(self, kind, frame, head):
        lanes = pl.ds(head * self.width, self.width)
        return [ref[kind, frame, :, lanes] for ref in self.blocks]

    def query(self, frame, head):
        return jnp.concatenate(self.near(0, frame, head), axis=0)

    def pair(self, frame, head):
        lanes = pl.ds(head * self.width, self.width)
        return [
            jnp.concatenate(
                self.near(1 + kind, frame, head)
                + [ref[kind, frame, :, lanes] for ref in self.extra],
                axis=0,
            )
            for kind in range(2)
        ]


def scores_of(query, key, scale):
    return (
        lax.dot_general(
            query, key, (((1,), (1,)), ((), ())), preferred_element_type=jnp.float32
        )
        * scale
    )


def edge_kernel(rims, cols, meta_ref, *refs):
    own, other = refs[:2]
    rim = refs[2] if rims else None
    sides_out, query_out = refs[-4:-2], refs[-2:]
    frames, area, half = other.shape[1:]

    def pick(rows):
        deep = rows * TILE
        shape = (2 * deep, rows * cols)
        to, of = (lax.broadcasted_iota(jnp.int32, shape, d) for d in range(2))
        spot = jnp.where(to < deep, meta_ref[5], meta_ref[6])
        to = lax.rem(to, deep)
        wanted = (to // TILE) * cols + spot * TILE + lax.rem(to, TILE)
        return deep, (of == wanted).astype(jnp.bfloat16)

    block = pick(area // cols)
    strip = pick(TILE)
    for kind in range(2):
        for frame in range(frames):
            work = [
                (own[1 + kind, frame], block),
                (other[1 + kind, frame], block),
            ]
            if rims:
                band = TILE * cols
                work += [(rim[kind, frame, i * band : (i + 1) * band], strip) for i in range(2)]
            begin = 0
            for rows, (deep, chosen) in work:
                found = jnp.dot(chosen, rows, preferred_element_type=jnp.float32)
                found = found.astype(jnp.bfloat16)
                for phase in range(2):
                    sides_out[phase][kind, frame, begin : begin + deep] = found[
                        phase * deep : (phase + 1) * deep
                    ]
                begin += deep
    for phase in range(2):
        frame = meta_ref[1 + phase]
        query_out[phase][:area] = own[0, frame]
        query_out[phase][area:] = other[0, frame]


def guest_kernel(rims, heads, width, meta_ref, radius_ref, code_ref, *refs):
    window = Window(refs, rims, heads, width)
    guests, (shard, *outs, sent, sem) = window.rest[:2], window.rest[2:]
    passing = pltpu.make_async_copy(shard, sent, sem)
    passing.start()
    code = code_ref[...]
    count = code.shape[0]
    scale = 1.0 / math.sqrt(width)
    first = meta_ref[0] * heads
    lane = lax.broadcasted_iota(jnp.int32, (count, LANES), 1)
    tops = [jnp.zeros((count, LANES), jnp.float32) for _ in guests]
    totals = [jnp.ones((count, LANES), jnp.float32) for _ in guests]
    work = [(head, phase) for head in range(heads) for phase in range(2)]
    score, value = {}, {}
    for head in range(heads):
        bias = head_bias(code, radius_ref, first + head)
        for phase in range(2):
            key, value[head, phase] = window.pair(meta_ref[1 + phase], head)
            query = guests[phase][:, pl.ds(head * width, width)]
            score[head, phase] = scores_of(query, key, scale) + bias
    top = {at: jnp.max(score[at], axis=1, keepdims=True) for at in work}
    expo = {at: jnp.exp(score[at] - top[at]) for at in work}
    total = {at: jnp.sum(expo[at], axis=1, keepdims=True) for at in work}
    for at in work:
        head, phase = at
        probs = (expo[at] * (1.0 / total[at])).astype(jnp.bfloat16)
        mixed = jnp.dot(probs, value[at], preferred_element_type=jnp.float32)
        outs[phase][:, pl.ds(head * width, width)] = mixed.astype(jnp.bfloat16)
        tops[phase] = jnp.where(lane == head, top[at], tops[phase])
        totals[phase] = jnp.where(lane == head, total[at], totals[phase])
    for out_ref, top, total in zip(outs, tops, totals):
        rest = top + jnp.log(total)
        stats = jnp.zeros((count, LANES), jnp.float32)
        for part in range(3):
            piece = rest.astype(jnp.bfloat16).astype(jnp.float32)
            rest = rest - piece
            stats = stats + (pltpu.roll(piece, part * STRIDE, 1) if part else piece)
        out_ref[:, pl.ds(heads * width, LANES)] = stats.astype(jnp.bfloat16)
    passing.wait()


def host_kernel(rims, heads, width, meta_ref, radius_ref, code_ref, *refs):
    window = Window(refs, rims, heads, width)
    mixed_ref, stats_ref = window.rest
    frames = window.frames
    code = code_ref[...]
    count = code.shape[0]
    scale = 1.0 / math.sqrt(width)
    first = meta_ref[0] * heads
    lane = lax.broadcasted_iota(jnp.int32, (count, LANES), 1)
    tops = [jnp.zeros((count, LANES), jnp.float32) for _ in range(frames)]
    totals = [jnp.ones((count, LANES), jnp.float32) for _ in range(frames)]
    work = [(head, f) for head in range(heads) for f in range(frames)]
    score, value = {}, {}
    for head in range(heads):
        bias = head_bias(code, radius_ref, first + head)
        bias_apart = jnp.where(radius_ref[first + head, 0] == 0, FAR, bias)
        query = [window.query(f, head) for f in range(frames)]
        pairs = [window.pair(f, head) for f in range(frames)]
        blocks = {}
        for frame in range(frames):
            near = range(max(0, frame - 1), min(frames, frame + 2))
            block = scores_of(
                jnp.concatenate([query[f] for f in near], axis=0), pairs[frame][0], scale
            )
            for spot, f in enumerate(near):
                blocks[f, frame] = block[spot * count : (spot + 1) * count] + (
                    bias if f == frame else bias_apart
                )
        for f in range(frames):
            near = range(max(0, f - 1), min(frames, f + 2))
            score[head, f] = jnp.concatenate([blocks[f, g] for g in near], axis=1)
            value[head, f] = jnp.concatenate([pairs[g][1] for g in near], axis=0)
    top = {at: jnp.max(score[at], axis=1, keepdims=True) for at in work}
    expo = {at: jnp.exp(score[at] - top[at]) for at in work}
    total = {at: jnp.sum(expo[at], axis=1, keepdims=True) for at in work}
    for at in work:
        head, f = at
        probs = (expo[at] * (1.0 / total[at])).astype(jnp.bfloat16)
        mixed_ref[f, :, pl.ds(head * width, width)] = jnp.dot(
            probs, value[at], preferred_element_type=jnp.float32
        )
        tops[f] = jnp.where(lane == head, top[at], tops[f])
        totals[f] = jnp.where(lane == head, total[at], totals[f])
    for f in range(frames):
        stats_ref[f] = tops[f] + jnp.log(totals[f])


def merge_kernel(
    heads, width, meta_ref, radius_ref, mixed_ref, stats_ref, ref_0, ref_1, out_ref, held, logs
):
    frames, count, _ = mixed_ref.shape
    half = count // PAIR
    first = meta_ref[0] * heads
    lane = lax.broadcasted_iota(jnp.int32, (count, LANES), 1)
    use = jnp.zeros((count, LANES), jnp.int32)
    for head in range(heads):
        use = jnp.where(lane == head, radius_ref[first + head, 0], use)
    held[...] = mixed_ref[...]
    logs[...] = stats_ref[...]
    for phase, ref in enumerate((ref_0, ref_1)):
        f = meta_ref[1 + phase]
        there = jnp.where(meta_ref[3 + phase] == 0, 0, use)
        stats = ref[:, pl.ds(heads * width, LANES)].astype(jnp.float32)
        guest = (
            stats
            + pltpu.roll(stats, LANES - STRIDE, 1)
            + pltpu.roll(stats, LANES - 2 * STRIDE, 1)
        )
        guest = jnp.where(there == 0, FAR, guest)
        own = logs[f]
        top = jnp.maximum(own, guest)
        own_weight, guest_weight = jnp.exp(own - top), jnp.exp(guest - top)
        total = own_weight + guest_weight
        if frames == 1:
            logs[f] = top + jnp.log(total)
        own_weight, guest_weight = own_weight / total, guest_weight / total
        for head in range(heads):
            lanes = pl.ds(head * width, width)
            held[f, :, lanes] = (
                held[f, :, lanes] * own_weight[:, head : head + 1]
                + ref[:, lanes].astype(jnp.float32) * guest_weight[:, head : head + 1]
            )
    mixed = held[...].astype(jnp.bfloat16)
    for part in range(PAIR):
        out_ref[part] = mixed[:, part * half : (part + 1) * half]


def join_kernel(count, meta_ref, *refs):
    pieces, out = refs[:count], refs[-1]
    depth = pieces[0].shape[0]
    for spot, ref in enumerate(pieces):
        begin = pl.multiple_of(meta_ref[spot] * depth, depth)
        out[pl.ds(begin, depth)] = ref[...]


def project_kernel(rows, near, own_out, other_out):
    both = jnp.dot(rows[...], near[...], preferred_element_type=jnp.float32)
    half = own_out.shape[0]
    own_out[...] = both[:half]
    other_out[...] = both[half:]


def total_kernel(part, partner, out):
    out[...] = (part[...] + partner[...]).astype(out.dtype)


def place_kernel(count, meta_ref, *refs):
    pieces, out, sems = refs[:count], refs[count], refs[count + 1]
    wide = pieces[0].shape[-1]
    copies = []
    for spot, ref in enumerate(pieces):
        origin = lax.rem(meta_ref[0] + count - spot, count)
        where = pl.ds(pl.multiple_of(origin * wide, LANES), wide)
        copies.append(pltpu.make_async_copy(ref, out.at[:, where], sems.at[spot]))
    for copy in copies:
        copy.start()
    for copy in copies:
        copy.wait()


def cost(flops, size):
    return pl.CostEstimate(flops=flops, bytes_accessed=size, transcendentals=0)


def shards(queries, keys, values, radius, out_weight):
    n_time, n_rows, n_cols = (lax.axis_size(a) for a in ("ta", "ha", "wa"))
    at_time, at_row, at_col = (lax.axis_index(a) for a in ("ta", "ha", "wa"))
    core = at_row % PAIR
    frames, rows, cols, features = queries.shape
    heads = radius.shape[0] // PAIR
    width = features // radius.shape[0]
    half = features // PAIR
    tile_cols = cols // TILE
    area = rows * cols
    rims = n_rows > PAIR

    after, there = sides(at_col, n_cols)
    later, present = sides(at_time, n_time)
    ends = [jnp.where(x, frames - 1, 0) for x in later]
    borders = [jnp.where(x, tile_cols - 1, 0) for x in after]
    meta = jnp.stack([core, *ends, *present, *borders]).astype(jnp.int32)

    raw = [x.reshape(frames, area, features) for x in (queries, keys, values)]
    pairs = [(i, i ^ 1) for i in range(n_rows)]
    stacked = jnp.stack(raw)
    own, other = (
        lax.dynamic_slice_in_dim(stacked, which * half, half, axis=3) for which in (core, 1 - core)
    )
    other = lax.ppermute(other, "ha", pairs)
    rim = None
    if rims:
        even, odd = (jnp.where(core == i, own[1:], other[1:]) for i in range(PAIR))
        band = TILE * cols
        up = lax.ppermute(odd[:, :, -band:], "ha", line(n_rows, PAIR))
        down = lax.ppermute(even[:, :, :band], "ha", line(n_rows, -PAIR))
        rim = jnp.concatenate([up, down], axis=2)
    deep = PAIR * rows * TILE + (PAIR * TILE * TILE if rims else 0)
    side = jax.ShapeDtypeStruct((2, frames, deep, half), queries.dtype)
    end = jax.ShapeDtypeStruct((PAIR * area, half), queries.dtype)
    *edges, first_end, second_end = pl.pallas_call(
        functools.partial(edge_kernel, rims, cols),
        out_shape=(side, side, end, end),
        in_specs=[SMEM] + [VMEM] * (3 if rims else 2),
        out_specs=(VMEM,) * 4,
        compiler_params=PARAMS,
        cost_estimate=cost(1000, 2_000_000),
        name="edge",
    )(meta, own, other, *([rim] if rims else []))
    beside = [lax.ppermute(x, ("ha", "wa"), swaps(n_cols, phase, n_rows, True)) for phase, x in enumerate(edges)]
    guests = [
        lax.ppermute(x, ("ta", "ha"), swaps(n_time, phase, n_rows, False))
        for phase, x in enumerate((first_end, second_end))
    ]

    slab = features // (n_rows * n_cols)
    wide = out_weight.shape[1] // n_time
    mine = lax.dynamic_slice_in_dim(out_weight, at_time * wide, wide, axis=1)
    held = {0: mine}
    if n_cols > 1:
        held[1] = lax.ppermute(mine, "wa", cycle(n_cols, 1))

    table = jnp.asarray(code_table(rows, cols, rims))
    absent = [~x for x in there]
    if rims:
        absent += [at_row < PAIR, at_row >= n_rows - PAIR]
    spot = core * 2 + at_col % 2
    spot = spot * 2 ** len(absent) + sum(jnp.where(x, 2**i, 0) for i, x in enumerate(absent))
    code = lax.dynamic_index_in_dim(table, spot, 0, keepdims=False)
    place = jnp.stack([at_time]).astype(jnp.int32)

    parts = [own, other] + ([rim] if rims else []) + beside
    count = PAIR * area
    unit = 4 * heads * width * count * code.shape[1]
    payload = jax.ShapeDtypeStruct((count, half + LANES), jnp.bfloat16)
    *answers, sent = pl.pallas_call(
        functools.partial(guest_kernel, rims, heads, width),
        out_shape=(payload, payload, jax.ShapeDtypeStruct(mine.shape, mine.dtype)),
        in_specs=[SMEM, SMEM] + [VMEM] * (1 + len(parts) + 2) + [VMEM],
        out_specs=(VMEM, VMEM, VMEM),
        scratch_shapes=[pltpu.SemaphoreType.DMA],
        compiler_params=PARAMS,
        cost_estimate=cost(2 * unit, 4_000_000),
        name="guest",
    )(meta, radius, code, *parts, *guests, held[min(1, n_cols - 1)])
    if n_cols > 2:
        held[2] = lax.ppermute(sent, "wa", cycle(n_cols, 1))
    answers = [
        lax.ppermute(x, ("ta", "ha"), swaps(n_time, phase, n_rows, False)) for phase, x in enumerate(answers)
    ]
    mixed_shape, stats_shape = (frames, count, half), (frames, count, LANES)
    mixed, stats = pl.pallas_call(
        functools.partial(host_kernel, rims, heads, width),
        out_shape=(
            jax.ShapeDtypeStruct(mixed_shape, jnp.float32),
            jax.ShapeDtypeStruct(stats_shape, jnp.float32),
        ),
        in_specs=[SMEM, SMEM] + [VMEM] * (1 + len(parts)),
        out_specs=(VMEM, VMEM),
        compiler_params=PARAMS,
        cost_estimate=cost(7 * unit, 6_000_000),
        name="host",
    )(meta, radius, code, *parts)
    attended = pl.pallas_call(
        functools.partial(merge_kernel, heads, width),
        out_shape=jax.ShapeDtypeStruct((PAIR, frames, area, half), jnp.bfloat16),
        in_specs=[SMEM, SMEM] + [VMEM] * 4,
        out_specs=VMEM,
        scratch_shapes=[
            pltpu.VMEM(mixed_shape, jnp.float32),
            pltpu.VMEM(stats_shape, jnp.float32),
        ],
        compiler_params=PARAMS,
        cost_estimate=cost(1000, 3_000_000),
        name="merge",
    )(meta, radius, mixed, stats, *answers)
    tokens = frames * area
    attended = attended.reshape(PAIR * tokens, half)
    for s in range(3, n_cols):
        held[s] = lax.ppermute(held[s - 1], "wa", cycle(n_cols, 1))
    received = [lax.ppermute(attended, "ta", cycle(n_time, s)) for s in range(1, n_time)]

    def joined(shards, at):
        count = len(shards)
        spots = jnp.stack([(at - s) % count for s in range(count)]).astype(jnp.int32)
        if shards[0].shape[0] % 16:
            return jnp.roll(jnp.stack(shards[::-1]), at + 1, axis=0).reshape(-1, wide)
        return pl.pallas_call(
            functools.partial(join_kernel, count),
            out_shape=jax.ShapeDtypeStruct((count * shards[0].shape[0], wide), mine.dtype),
            in_specs=[SMEM] + [VMEM] * count + [HBM],
            out_specs=VMEM,
            compiler_params=PARAMS,
            cost_estimate=cost(1000, 2_400_000),
            name="join",
        )(spots, *shards, received[0])

    near = joined([held[s] for s in range(n_cols)], at_col)
    if n_rows > PAIR:
        across = [lax.ppermute(near, "ha", cycle(n_rows, r)) for r in range(1, n_rows)]
        near = lax.dynamic_slice_in_dim(joined([near, *across], at_row), core * half, half, axis=0)

    def project(block):
        part = jax.ShapeDtypeStruct((tokens, wide), jnp.float32)
        return pl.pallas_call(
            project_kernel,
            out_shape=(part, part),
            in_specs=[VMEM, VMEM],
            out_specs=(VMEM, VMEM),
            compiler_params=PARAMS,
            cost_estimate=cost(2 * tokens * features * wide, 3_000_000),
            name="project",
        )(block, near)

    def total(part, partner):
        return pl.pallas_call(
            total_kernel,
            out_shape=jax.ShapeDtypeStruct((tokens, wide), queries.dtype),
            in_specs=[VMEM, VMEM],
            out_specs=VMEM,
            compiler_params=PARAMS,
            cost_estimate=cost(tokens * wide, 3_000_000),
            name="total",
        )(part, partner)

    products = []
    for block in [attended, *received]:
        part, given = project(block)
        products.append(total(part, lax.ppermute(given, "ha", pairs)))
    back = [products[0]] + [
        lax.ppermute(products[n_time - s], "ta", cycle(n_time, s)) for s in range(1, n_time)
    ]
    out = pl.pallas_call(
        functools.partial(place_kernel, n_time),
        out_shape=jax.ShapeDtypeStruct((tokens, wide * n_time), jnp.bfloat16),
        in_specs=[SMEM] + [HBM] * n_time,
        out_specs=HBM,
        scratch_shapes=[pltpu.SemaphoreType.DMA((n_time,))],
        compiler_params=PARAMS,
        cost_estimate=cost(1000, 1_200_000),
        name="place",
    )(place, *back)
    return out.reshape(frames, rows, cols, wide * n_time)


def solution(mesh):
    return jax.shard_map(
        shards,
        mesh=mesh,
        in_specs=(
            P("ta", "ha", "wa", None),
            P("ta", "ha", "wa", None),
            P("ta", "ha", "wa", None),
            P(),
            P(("ha", "wa"), None),
        ),
        out_specs=P("ta", "ha", "wa", None),
        check_vma=False,
    )
```

```python
import functools
import math

import jax
import jax.numpy as jnp
import numpy as np
from jax import lax
from jax.experimental import pallas as pl
from jax.experimental.pallas import tpu as pltpu
from jax.sharding import PartitionSpec as P

TILE = 4
PAIR = 2
FAR = -1e30
LANES = 128
STRIDE = 32
VMEM = pl.BlockSpec(memory_space=pltpu.VMEM)
SMEM = pl.BlockSpec(memory_space=pltpu.SMEM)
HBM = pl.BlockSpec(memory_space=pl.ANY)
PARAMS = pltpu.CompilerParams(vmem_limit_bytes=6 * 1024 * 1024)


def cycle(count, step):
    return [(i, (i + step) % count) for i in range(count)]


def swaps(count, phase, n_rows, rows_first):
    pairs = []
    for row in range(n_rows):
        for i in range(count):
            p = (i ^ 1) if phase == 0 else ((i + 1) ^ 1) - 1
            ends = ((row, i), (row, p) if 0 <= p < count else (row ^ 1, i))
            pairs.append(tuple(r * count + j if rows_first else j * n_rows + r for r, j in ends))
    return pairs


def line(count, step):
    return [(i, i + step) for i in range(count) if 0 <= i + step < count]


def sides(index, count):
    even = index % 2 == 0
    inside_after, inside_before = index < count - 1, index > 0
    return (even, ~even), (
        jnp.where(even, inside_after, inside_before),
        jnp.where(even, inside_before, inside_after),
    )


def code_table(rows, cols, rims):
    tile_cols = cols // TILE
    span = rows // TILE
    tables = []
    for core in range(PAIR):
        own = core * span
        other = (1 - core) * span
        blocks = [(own, rows), (other, rows)] + ([(-1, TILE), (2 * span, TILE)] if rims else [])
        for odd in range(2):
            query_row, query_col, key_row, key_col, key_side = [], [], [], [], []
            for base in (own, other):
                for row in range(rows):
                    for col in range(cols):
                        query_row.append(base + row // TILE)
                        query_col.append(col // TILE)
            for base, length in blocks:
                for row in range(length):
                    for col in range(cols):
                        key_row.append(base + row // TILE)
                        key_col.append(col // TILE)
                        key_side.append(-1)
            for phase in range(2):
                for base, length in blocks:
                    for row in range(length):
                        for _ in range(TILE):
                            key_row.append(base + row // TILE)
                            key_col.append(tile_cols if phase == odd else -1)
                            key_side.append(phase)
            key_row, key_col, key_side = (np.array(x)[None] for x in (key_row, key_col, key_side))
            apart_row = np.abs(np.array(query_row)[:, None] - key_row)
            apart_col = np.abs(np.array(query_col)[:, None] - key_col)
            base_code = (
                2 * (apart_row == 1)
                + 4 * (apart_col == 1)
                + 8 * ((apart_row > 1) | (apart_col > 1))
            )
            outside = [key_side == 0, key_side == 1]
            outside += [key_row < 0, key_row >= 2 * span] if rims else []
            for bits in range(2 ** len(outside)):
                code = base_code
                for which, mask in enumerate(outside):
                    if bits >> which & 1:
                        code = np.where(mask, 8, code)
                tables.append(code)
    return np.stack(tables).astype(np.int32)


def head_bias(code, radius_ref, head):
    barred = (
        8
        + jnp.where(radius_ref[head, 1] == 0, 2, 0)
        + jnp.where(radius_ref[head, 2] == 0, 4, 0)
    )
    return jnp.where((code & barred) == 0, 0.0, FAR)


class Window:
    def __init__(self, refs, rims, heads, width):
        refs = list(refs)
        self.blocks = refs[:2]
        self.extra = refs[2 : 5 if rims else 4]
        self.rest = refs[5 if rims else 4 :]
        self.frames = self.blocks[0].shape[1]
        self.width = width

    def near(self, kind, frame, head):
        lanes = pl.ds(head * self.width, self.width)
        return [ref[kind, frame, :, lanes] for ref in self.blocks]

    def query(self, frame, head):
        return jnp.concatenate(self.near(0, frame, head), axis=0)

    def pair(self, frame, head):
        lanes = pl.ds(head * self.width, self.width)
        return [
            jnp.concatenate(
                self.near(1 + kind, frame, head)
                + [ref[kind, frame, :, lanes] for ref in self.extra],
                axis=0,
            )
            for kind in range(2)
        ]


def scores_of(query, key, scale):
    return (
        lax.dot_general(
            query, key, (((1,), (1,)), ((), ())), preferred_element_type=jnp.float32
        )
        * scale
    )


def edge_kernel(rims, cols, meta_ref, *refs):
    own, other = refs[:2]
    rim = refs[2] if rims else None
    sides_out, query_out = refs[-4:-2], refs[-2:]
    frames, area, half = other.shape[1:]

    def pick(rows):
        deep = rows * TILE
        shape = (2 * deep, rows * cols)
        to, of = (lax.broadcasted_iota(jnp.int32, shape, d) for d in range(2))
        spot = jnp.where(to < deep, meta_ref[5], meta_ref[6])
        to = lax.rem(to, deep)
        wanted = (to // TILE) * cols + spot * TILE + lax.rem(to, TILE)
        return deep, (of == wanted).astype(jnp.bfloat16)

    block = pick(area // cols)
    strip = pick(TILE)
    for kind in range(2):
        for frame in range(frames):
            work = [
                (own[1 + kind, frame], block),
                (other[1 + kind, frame], block),
            ]
            if rims:
                band = TILE * cols
                work += [(rim[kind, frame, i * band : (i + 1) * band], strip) for i in range(2)]
            begin = 0
            for rows, (deep, chosen) in work:
                found = jnp.dot(chosen, rows, preferred_element_type=jnp.float32)
                found = found.astype(jnp.bfloat16)
                for phase in range(2):
                    sides_out[phase][kind, frame, begin : begin + deep] = found[
                        phase * deep : (phase + 1) * deep
                    ]
                begin += deep
    for phase in range(2):
        frame = meta_ref[1 + phase]
        query_out[phase][:area] = own[0, frame]
        query_out[phase][area:] = other[0, frame]


def guest_kernel(rims, heads, width, meta_ref, radius_ref, code_ref, *refs):
    window = Window(refs, rims, heads, width)
    guests, (shard, *outs, sent, sem) = window.rest[:2], window.rest[2:]
    passing = pltpu.make_async_copy(shard, sent, sem)
    passing.start()
    code = code_ref[...]
    count = code.shape[0]
    scale = 1.0 / math.sqrt(width)
    first = meta_ref[0] * heads
    lane = lax.broadcasted_iota(jnp.int32, (count, LANES), 1)
    tops = [jnp.zeros((count, LANES), jnp.float32) for _ in guests]
    totals = [jnp.ones((count, LANES), jnp.float32) for _ in guests]
    work = [(head, phase) for head in range(heads) for phase in range(2)]
    score, value = {}, {}
    for head in range(heads):
        bias = head_bias(code, radius_ref, first + head)
        for phase in range(2):
            key, value[head, phase] = window.pair(meta_ref[1 + phase], head)
            query = guests[phase][:, pl.ds(head * width, width)]
            score[head, phase] = scores_of(query, key, scale) + bias
    top = {at: jnp.max(score[at], axis=1, keepdims=True) for at in work}
    expo = {at: jnp.exp(score[at] - top[at]) for at in work}
    total = {at: jnp.sum(expo[at], axis=1, keepdims=True) for at in work}
    for at in work:
        head, phase = at
        probs = (expo[at] * (1.0 / total[at])).astype(jnp.bfloat16)
        mixed = jnp.dot(probs, value[at], preferred_element_type=jnp.float32)
        outs[phase][:, pl.ds(head * width, width)] = mixed.astype(jnp.bfloat16)
        tops[phase] = jnp.where(lane == head, top[at], tops[phase])
        totals[phase] = jnp.where(lane == head, total[at], totals[phase])
    for out_ref, top, total in zip(outs, tops, totals):
        rest = top + jnp.log(total)
        stats = jnp.zeros((count, LANES), jnp.float32)
        for part in range(3):
            piece = rest.astype(jnp.bfloat16).astype(jnp.float32)
            rest = rest - piece
            stats = stats + (pltpu.roll(piece, part * STRIDE, 1) if part else piece)
        out_ref[:, pl.ds(heads * width, LANES)] = stats.astype(jnp.bfloat16)
    passing.wait()


def host_kernel(rims, heads, width, meta_ref, radius_ref, code_ref, *refs):
    window = Window(refs, rims, heads, width)
    mixed_ref, stats_ref = window.rest
    frames = window.frames
    code = code_ref[...]
    count = code.shape[0]
    scale = 1.0 / math.sqrt(width)
    first = meta_ref[0] * heads
    lane = lax.broadcasted_iota(jnp.int32, (count, LANES), 1)
    tops = [jnp.zeros((count, LANES), jnp.float32) for _ in range(frames)]
    totals = [jnp.ones((count, LANES), jnp.float32) for _ in range(frames)]
    work = [(head, f) for head in range(heads) for f in range(frames)]
    score, value = {}, {}
    for head in range(heads):
        bias = head_bias(code, radius_ref, first + head)
        bias_apart = jnp.where(radius_ref[first + head, 0] == 0, FAR, bias)
        query = [window.query(f, head) for f in range(frames)]
        pairs = [window.pair(f, head) for f in range(frames)]
        blocks = {}
        for frame in range(frames):
            near = range(max(0, frame - 1), min(frames, frame + 2))
            block = scores_of(
                jnp.concatenate([query[f] for f in near], axis=0), pairs[frame][0], scale
            )
            for spot, f in enumerate(near):
                blocks[f, frame] = block[spot * count : (spot + 1) * count] + (
                    bias if f == frame else bias_apart
                )
        for f in range(frames):
            near = range(max(0, f - 1), min(frames, f + 2))
            score[head, f] = jnp.concatenate([blocks[f, g] for g in near], axis=1)
            value[head, f] = jnp.concatenate([pairs[g][1] for g in near], axis=0)
    top = {at: jnp.max(score[at], axis=1, keepdims=True) for at in work}
    expo = {at: jnp.exp(score[at] - top[at]) for at in work}
    total = {at: jnp.sum(expo[at], axis=1, keepdims=True) for at in work}
    for at in work:
        head, f = at
        probs = (expo[at] * (1.0 / total[at])).astype(jnp.bfloat16)
        mixed_ref[f, :, pl.ds(head * width, width)] = jnp.dot(
            probs, value[at], preferred_element_type=jnp.float32
        )
        tops[f] = jnp.where(lane == head, top[at], tops[f])
        totals[f] = jnp.where(lane == head, total[at], totals[f])
    for f in range(frames):
        stats_ref[f] = tops[f] + jnp.log(totals[f])


def merge_kernel(
    heads, width, meta_ref, radius_ref, mixed_ref, stats_ref, ref_0, ref_1, out_ref, held, logs
):
    frames, count, _ = mixed_ref.shape
    half = count // PAIR
    first = meta_ref[0] * heads
    lane = lax.broadcasted_iota(jnp.int32, (count, LANES), 1)
    use = jnp.zeros((count, LANES), jnp.int32)
    for head in range(heads):
        use = jnp.where(lane == head, radius_ref[first + head, 0], use)
    held[...] = mixed_ref[...]
    logs[...] = stats_ref[...]
    for phase, ref in enumerate((ref_0, ref_1)):
        f = meta_ref[1 + phase]
        there = jnp.where(meta_ref[3 + phase] == 0, 0, use)
        stats = ref[:, pl.ds(heads * width, LANES)].astype(jnp.float32)
        guest = (
            stats
            + pltpu.roll(stats, LANES - STRIDE, 1)
            + pltpu.roll(stats, LANES - 2 * STRIDE, 1)
        )
        guest = jnp.where(there == 0, FAR, guest)
        own = logs[f]
        top = jnp.maximum(own, guest)
        own_weight, guest_weight = jnp.exp(own - top), jnp.exp(guest - top)
        total = own_weight + guest_weight
        if frames == 1:
            logs[f] = top + jnp.log(total)
        own_weight, guest_weight = own_weight / total, guest_weight / total
        for head in range(heads):
            lanes = pl.ds(head * width, width)
            held[f, :, lanes] = (
                held[f, :, lanes] * own_weight[:, head : head + 1]
                + ref[:, lanes].astype(jnp.float32) * guest_weight[:, head : head + 1]
            )
    mixed = held[...].astype(jnp.bfloat16)
    for part in range(PAIR):
        out_ref[part] = mixed[:, part * half : (part + 1) * half]


def join_kernel(count, meta_ref, *refs):
    pieces, out = refs[:count], refs[-1]
    depth = pieces[0].shape[0]
    for spot, ref in enumerate(pieces):
        begin = pl.multiple_of(meta_ref[spot] * depth, depth)
        out[pl.ds(begin, depth)] = ref[...]


def project_kernel(rows, near, own_out, other_out):
    both = jnp.dot(rows[...], near[...], preferred_element_type=jnp.float32)
    half = own_out.shape[0]
    own_out[...] = both[:half]
    other_out[...] = both[half:]


def total_kernel(part, partner, out):
    out[...] = (part[...] + partner[...]).astype(out.dtype)


def place_kernel(count, meta_ref, *refs):
    pieces, out, sems = refs[:count], refs[count], refs[count + 1]
    wide = pieces[0].shape[-1]
    copies = []
    for spot, ref in enumerate(pieces):
        origin = lax.rem(meta_ref[0] + count - spot, count)
        where = pl.ds(pl.multiple_of(origin * wide, LANES), wide)
        copies.append(pltpu.make_async_copy(ref, out.at[:, where], sems.at[spot]))
    for copy in copies:
        copy.start()
    for copy in copies:
        copy.wait()


def cost(flops, size):
    return pl.CostEstimate(flops=flops, bytes_accessed=size, transcendentals=0)


def shards(queries, keys, values, radius, out_weight):
    n_time, n_rows, n_cols = (lax.axis_size(a) for a in ("ta", "ha", "wa"))
    at_time, at_row, at_col = (lax.axis_index(a) for a in ("ta", "ha", "wa"))
    core = at_row % PAIR
    frames, rows, cols, features = queries.shape
    heads = radius.shape[0] // PAIR
    width = features // radius.shape[0]
    half = features // PAIR
    tile_cols = cols // TILE
    area = rows * cols
    rims = n_rows > PAIR

    after, there = sides(at_col, n_cols)
    later, present = sides(at_time, n_time)
    ends = [jnp.where(x, frames - 1, 0) for x in later]
    borders = [jnp.where(x, tile_cols - 1, 0) for x in after]
    meta = jnp.stack([core, *ends, *present, *borders]).astype(jnp.int32)

    raw = [x.reshape(frames, area, features) for x in (queries, keys, values)]
    pairs = [(i, i ^ 1) for i in range(n_rows)]
    stacked = jnp.stack(raw)
    own, other = (
        lax.dynamic_slice_in_dim(stacked, which * half, half, axis=3) for which in (core, 1 - core)
    )
    other = lax.ppermute(other, "ha", pairs)
    rim = None
    if rims:
        even, odd = (jnp.where(core == i, own[1:], other[1:]) for i in range(PAIR))
        band = TILE * cols
        up = lax.ppermute(odd[:, :, -band:], "ha", line(n_rows, PAIR))
        down = lax.ppermute(even[:, :, :band], "ha", line(n_rows, -PAIR))
        rim = jnp.concatenate([up, down], axis=2)
    deep = PAIR * rows * TILE + (PAIR * TILE * TILE if rims else 0)
    side = jax.ShapeDtypeStruct((2, frames, deep, half), queries.dtype)
    end = jax.ShapeDtypeStruct((PAIR * area, half), queries.dtype)
    *edges, first_end, second_end = pl.pallas_call(
        functools.partial(edge_kernel, rims, cols),
        out_shape=(side, side, end, end),
        in_specs=[SMEM] + [VMEM] * (3 if rims else 2),
        out_specs=(VMEM,) * 4,
        compiler_params=PARAMS,
        cost_estimate=cost(1000, 2_000_000),
        name="edge",
    )(meta, own, other, *([rim] if rims else []))
    beside = [lax.ppermute(x, ("ha", "wa"), swaps(n_cols, phase, n_rows, True)) for phase, x in enumerate(edges)]
    guests = [
        lax.ppermute(x, ("ta", "ha"), swaps(n_time, phase, n_rows, False))
        for phase, x in enumerate((first_end, second_end))
    ]

    slab = features // (n_rows * n_cols)
    wide = out_weight.shape[1] // n_time
    mine = lax.dynamic_slice_in_dim(out_weight, at_time * wide, wide, axis=1)
    held = {0: mine}

    table = jnp.asarray(code_table(rows, cols, rims))
    absent = [~x for x in there]
    if rims:
        absent += [at_row < PAIR, at_row >= n_rows - PAIR]
    spot = core * 2 + at_col % 2
    spot = spot * 2 ** len(absent) + sum(jnp.where(x, 2**i, 0) for i, x in enumerate(absent))
    code = lax.dynamic_index_in_dim(table, spot, 0, keepdims=False)
    place = jnp.stack([at_time]).astype(jnp.int32)

    parts = [own, other] + ([rim] if rims else []) + beside
    count = PAIR * area
    unit = 4 * heads * width * count * code.shape[1]
    payload = jax.ShapeDtypeStruct((count, half + LANES), jnp.bfloat16)
    *answers, sent = pl.pallas_call(
        functools.partial(guest_kernel, rims, heads, width),
        out_shape=(payload, payload, jax.ShapeDtypeStruct(mine.shape, mine.dtype)),
        in_specs=[SMEM, SMEM] + [VMEM] * (1 + len(parts) + 2) + [HBM],
        out_specs=(VMEM, VMEM, HBM),
        scratch_shapes=[pltpu.SemaphoreType.DMA],
        compiler_params=PARAMS,
        cost_estimate=cost(2 * unit, 4_000_000),
        name="guest",
    )(meta, radius, code, *parts, *guests, mine)
    if n_cols > 1:
        held[1] = lax.ppermute(sent, "wa", cycle(n_cols, 1))
    answers = [
        lax.ppermute(x, ("ta", "ha"), swaps(n_time, phase, n_rows, False)) for phase, x in enumerate(answers)
    ]
    mixed_shape, stats_shape = (frames, count, half), (frames, count, LANES)
    mixed, stats = pl.pallas_call(
        functools.partial(host_kernel, rims, heads, width),
        out_shape=(
            jax.ShapeDtypeStruct(mixed_shape, jnp.float32),
            jax.ShapeDtypeStruct(stats_shape, jnp.float32),
        ),
        in_specs=[SMEM, SMEM] + [VMEM] * (1 + len(parts)),
        out_specs=(VMEM, VMEM),
        compiler_params=PARAMS,
        cost_estimate=cost(7 * unit, 6_000_000),
        name="host",
    )(meta, radius, code, *parts)
    attended = pl.pallas_call(
        functools.partial(merge_kernel, heads, width),
        out_shape=jax.ShapeDtypeStruct((PAIR, frames, area, half), jnp.bfloat16),
        in_specs=[SMEM, SMEM] + [VMEM] * 4,
        out_specs=VMEM,
        scratch_shapes=[
            pltpu.VMEM(mixed_shape, jnp.float32),
            pltpu.VMEM(stats_shape, jnp.float32),
        ],
        compiler_params=PARAMS,
        cost_estimate=cost(1000, 3_000_000),
        name="merge",
    )(meta, radius, mixed, stats, *answers)
    tokens = frames * area
    attended = attended.reshape(PAIR * tokens, half)
    if n_cols > 2:
        held[n_cols - 1] = lax.ppermute(sent, "wa", cycle(n_cols, -1))
    for s in range(2, n_cols - 1):
        held[s] = lax.ppermute(held[s - 1], "wa", cycle(n_cols, 1))
    received = [lax.ppermute(attended, "ta", cycle(n_time, s)) for s in range(1, n_time)]

    def joined(shards, at):
        count = len(shards)
        spots = jnp.stack([(at - s) % count for s in range(count)]).astype(jnp.int32)
        if shards[0].shape[0] % 16:
            return jnp.roll(jnp.stack(shards[::-1]), at + 1, axis=0).reshape(-1, wide)
        return pl.pallas_call(
            functools.partial(join_kernel, count),
            out_shape=jax.ShapeDtypeStruct((count * shards[0].shape[0], wide), mine.dtype),
            in_specs=[SMEM] + [VMEM] * count + [HBM],
            out_specs=VMEM,
            compiler_params=PARAMS,
            cost_estimate=cost(1000, 2_400_000),
            name="join",
        )(spots, *shards, received[1])

    near = joined([held[s] for s in range(n_cols)], at_col)
    if n_rows > PAIR:
        across = [lax.ppermute(near, "ha", cycle(n_rows, r)) for r in range(1, n_rows)]
        near = lax.dynamic_slice_in_dim(joined([near, *across], at_row), core * half, half, axis=0)

    def project(block):
        part = jax.ShapeDtypeStruct((tokens, wide), jnp.float32)
        return pl.pallas_call(
            project_kernel,
            out_shape=(part, part),
            in_specs=[VMEM, VMEM],
            out_specs=(VMEM, VMEM),
            compiler_params=PARAMS,
            cost_estimate=cost(2 * tokens * features * wide, 3_000_000),
            name="project",
        )(block, near)

    def total(part, partner):
        return pl.pallas_call(
            total_kernel,
            out_shape=jax.ShapeDtypeStruct((tokens, wide), queries.dtype),
            in_specs=[VMEM, VMEM],
            out_specs=VMEM,
            compiler_params=PARAMS,
            cost_estimate=cost(tokens * wide, 3_000_000),
            name="total",
        )(part, partner)

    products = []
    for block in [attended, *received]:
        part, given = project(block)
        products.append(total(part, lax.ppermute(given, "ha", pairs)))
    back = [products[0]] + [
        lax.ppermute(products[n_time - s], "ta", cycle(n_time, s)) for s in range(1, n_time)
    ]
    out = pl.pallas_call(
        functools.partial(place_kernel, n_time),
        out_shape=jax.ShapeDtypeStruct((tokens, wide * n_time), jnp.bfloat16),
        in_specs=[SMEM] + [HBM] * n_time,
        out_specs=HBM,
        scratch_shapes=[pltpu.SemaphoreType.DMA((n_time,))],
        compiler_params=PARAMS,
        cost_estimate=cost(1000, 1_200_000),
        name="place",
    )(place, *back)
    return out.reshape(frames, rows, cols, wide * n_time)


def solution(mesh):
    return jax.shard_map(
        shards,
        mesh=mesh,
        in_specs=(
            P("ta", "ha", "wa", None),
            P("ta", "ha", "wa", None),
            P("ta", "ha", "wa", None),
            P(),
            P(("ha", "wa"), None),
        ),
        out_specs=P("ta", "ha", "wa", None),
        check_vma=False,
    )
```

```python
import functools
import math

import jax
import jax.numpy as jnp
import numpy as np
from jax import lax
from jax.experimental import pallas as pl
from jax.experimental.pallas import tpu as pltpu
from jax.sharding import PartitionSpec as P

TILE = 4
PAIR = 2
FAR = -1e30
LANES = 128
STRIDE = 32
VMEM = pl.BlockSpec(memory_space=pltpu.VMEM)
SMEM = pl.BlockSpec(memory_space=pltpu.SMEM)
HBM = pl.BlockSpec(memory_space=pl.ANY)
PARAMS = pltpu.CompilerParams(vmem_limit_bytes=6 * 1024 * 1024)


def cycle(count, step):
    return [(i, (i + step) % count) for i in range(count)]


def swaps(count, phase, n_rows, rows_first):
    pairs = []
    for row in range(n_rows):
        for i in range(count):
            p = (i ^ 1) if phase == 0 else ((i + 1) ^ 1) - 1
            ends = ((row, i), (row, p) if 0 <= p < count else (row ^ 1, i))
            pairs.append(tuple(r * count + j if rows_first else j * n_rows + r for r, j in ends))
    return pairs


def line(count, step):
    return [(i, i + step) for i in range(count) if 0 <= i + step < count]


def sides(index, count):
    even = index % 2 == 0
    inside_after, inside_before = index < count - 1, index > 0
    return (even, ~even), (
        jnp.where(even, inside_after, inside_before),
        jnp.where(even, inside_before, inside_after),
    )


def code_table(rows, cols, rims):
    tile_cols = cols // TILE
    span = rows // TILE
    tables = []
    for core in range(PAIR):
        own = core * span
        other = (1 - core) * span
        blocks = [(own, rows), (other, rows)] + ([(-1, TILE), (2 * span, TILE)] if rims else [])
        for odd in range(2):
            query_row, query_col, key_row, key_col, key_side = [], [], [], [], []
            for base in (own, other):
                for row in range(rows):
                    for col in range(cols):
                        query_row.append(base + row // TILE)
                        query_col.append(col // TILE)
            for base, length in blocks:
                for row in range(length):
                    for col in range(cols):
                        key_row.append(base + row // TILE)
                        key_col.append(col // TILE)
                        key_side.append(-1)
            for phase in range(2):
                for base, length in blocks:
                    for row in range(length):
                        for _ in range(TILE):
                            key_row.append(base + row // TILE)
                            key_col.append(tile_cols if phase == odd else -1)
                            key_side.append(phase)
            key_row, key_col, key_side = (np.array(x)[None] for x in (key_row, key_col, key_side))
            apart_row = np.abs(np.array(query_row)[:, None] - key_row)
            apart_col = np.abs(np.array(query_col)[:, None] - key_col)
            base_code = (
                2 * (apart_row == 1)
                + 4 * (apart_col == 1)
                + 8 * ((apart_row > 1) | (apart_col > 1))
            )
            outside = [key_side == 0, key_side == 1]
            outside += [key_row < 0, key_row >= 2 * span] if rims else []
            for bits in range(2 ** len(outside)):
                code = base_code
                for which, mask in enumerate(outside):
                    if bits >> which & 1:
                        code = np.where(mask, 8, code)
                tables.append(code)
    return np.stack(tables).astype(np.int32)


def head_bias(code, radius_ref, head):
    barred = (
        8
        + jnp.where(radius_ref[head, 1] == 0, 2, 0)
        + jnp.where(radius_ref[head, 2] == 0, 4, 0)
    )
    return jnp.where((code & barred) == 0, 0.0, FAR)


class Window:
    def __init__(self, refs, rims, heads, width):
        refs = list(refs)
        self.blocks = refs[:2]
        self.extra = refs[2 : 5 if rims else 4]
        self.rest = refs[5 if rims else 4 :]
        self.frames = self.blocks[0].shape[1]
        self.width = width

    def near(self, kind, frame, head):
        lanes = pl.ds(head * self.width, self.width)
        return [ref[kind, frame, :, lanes] for ref in self.blocks]

    def query(self, frame, head):
        return jnp.concatenate(self.near(0, frame, head), axis=0)

    def pair(self, frame, head):
        lanes = pl.ds(head * self.width, self.width)
        return [
            jnp.concatenate(
                self.near(1 + kind, frame, head)
                + [ref[kind, frame, :, lanes] for ref in self.extra],
                axis=0,
            )
            for kind in range(2)
        ]


def scores_of(query, key, scale):
    return (
        lax.dot_general(
            query, key, (((1,), (1,)), ((), ())), preferred_element_type=jnp.float32
        )
        * scale
    )


def edge_kernel(rims, cols, meta_ref, *refs):
    own, other = refs[:2]
    rim = refs[2] if rims else None
    sides_out = refs[-2:]
    frames, area, half = other.shape[1:]

    def pick(rows):
        deep = rows * TILE
        shape = (2 * deep, rows * cols)
        to, of = (lax.broadcasted_iota(jnp.int32, shape, d) for d in range(2))
        spot = jnp.where(to < deep, meta_ref[5], meta_ref[6])
        to = lax.rem(to, deep)
        wanted = (to // TILE) * cols + spot * TILE + lax.rem(to, TILE)
        return deep, (of == wanted).astype(jnp.bfloat16)

    block = pick(area // cols)
    strip = pick(TILE)
    for kind in range(2):
        for frame in range(frames):
            work = [
                (own[1 + kind, frame], block),
                (other[1 + kind, frame], block),
            ]
            if rims:
                band = TILE * cols
                work += [(rim[kind, frame, i * band : (i + 1) * band], strip) for i in range(2)]
            begin = 0
            for rows, (deep, chosen) in work:
                found = jnp.dot(chosen, rows, preferred_element_type=jnp.float32)
                found = found.astype(jnp.bfloat16)
                for phase in range(2):
                    sides_out[phase][kind, frame, begin : begin + deep] = found[
                        phase * deep : (phase + 1) * deep
                    ]
                begin += deep


def guest_kernel(rims, heads, width, meta_ref, radius_ref, code_ref, *refs):
    window = Window(refs, rims, heads, width)
    guests, (shard, *outs, sent, sem) = window.rest[:2], window.rest[2:]
    passing = pltpu.make_async_copy(shard, sent, sem)
    passing.start()
    code = code_ref[...]
    count = code.shape[0]
    scale = 1.0 / math.sqrt(width)
    first = meta_ref[0] * heads
    lane = lax.broadcasted_iota(jnp.int32, (count, LANES), 1)
    tops = [jnp.zeros((count, LANES), jnp.float32) for _ in guests]
    totals = [jnp.ones((count, LANES), jnp.float32) for _ in guests]
    work = [(head, phase) for head in range(heads) for phase in range(2)]
    score, value = {}, {}
    for head in range(heads):
        bias = head_bias(code, radius_ref, first + head)
        for phase in range(2):
            key, value[head, phase] = window.pair(meta_ref[1 + phase], head)
            query = guests[phase][:, pl.ds(head * width, width)]
            score[head, phase] = scores_of(query, key, scale) + bias
    top = {at: jnp.max(score[at], axis=1, keepdims=True) for at in work}
    expo = {at: jnp.exp(score[at] - top[at]) for at in work}
    total = {at: jnp.sum(expo[at], axis=1, keepdims=True) for at in work}
    for at in work:
        head, phase = at
        probs = (expo[at] * (1.0 / total[at])).astype(jnp.bfloat16)
        mixed = jnp.dot(probs, value[at], preferred_element_type=jnp.float32)
        outs[phase][:, pl.ds(head * width, width)] = mixed.astype(jnp.bfloat16)
        tops[phase] = jnp.where(lane == head, top[at], tops[phase])
        totals[phase] = jnp.where(lane == head, total[at], totals[phase])
    for out_ref, top, total in zip(outs, tops, totals):
        rest = top + jnp.log(total)
        stats = jnp.zeros((count, LANES), jnp.float32)
        for part in range(3):
            piece = rest.astype(jnp.bfloat16).astype(jnp.float32)
            rest = rest - piece
            stats = stats + (pltpu.roll(piece, part * STRIDE, 1) if part else piece)
        out_ref[:, pl.ds(heads * width, LANES)] = stats.astype(jnp.bfloat16)
    passing.wait()


def host_kernel(rims, heads, width, meta_ref, radius_ref, code_ref, *refs):
    window = Window(refs, rims, heads, width)
    mixed_ref, stats_ref = window.rest
    frames = window.frames
    code = code_ref[...]
    count = code.shape[0]
    scale = 1.0 / math.sqrt(width)
    first = meta_ref[0] * heads
    lane = lax.broadcasted_iota(jnp.int32, (count, LANES), 1)
    tops = [jnp.zeros((count, LANES), jnp.float32) for _ in range(frames)]
    totals = [jnp.ones((count, LANES), jnp.float32) for _ in range(frames)]
    work = [(head, f) for head in range(heads) for f in range(frames)]
    score, value = {}, {}
    for head in range(heads):
        bias = head_bias(code, radius_ref, first + head)
        bias_apart = jnp.where(radius_ref[first + head, 0] == 0, FAR, bias)
        query = [window.query(f, head) for f in range(frames)]
        pairs = [window.pair(f, head) for f in range(frames)]
        blocks = {}
        for frame in range(frames):
            near = range(max(0, frame - 1), min(frames, frame + 2))
            block = scores_of(
                jnp.concatenate([query[f] for f in near], axis=0), pairs[frame][0], scale
            )
            for spot, f in enumerate(near):
                blocks[f, frame] = block[spot * count : (spot + 1) * count] + (
                    bias if f == frame else bias_apart
                )
        for f in range(frames):
            near = range(max(0, f - 1), min(frames, f + 2))
            score[head, f] = jnp.concatenate([blocks[f, g] for g in near], axis=1)
            value[head, f] = jnp.concatenate([pairs[g][1] for g in near], axis=0)
    top = {at: jnp.max(score[at], axis=1, keepdims=True) for at in work}
    expo = {at: jnp.exp(score[at] - top[at]) for at in work}
    total = {at: jnp.sum(expo[at], axis=1, keepdims=True) for at in work}
    for at in work:
        head, f = at
        probs = (expo[at] * (1.0 / total[at])).astype(jnp.bfloat16)
        mixed_ref[f, :, pl.ds(head * width, width)] = jnp.dot(
            probs, value[at], preferred_element_type=jnp.float32
        )
        tops[f] = jnp.where(lane == head, top[at], tops[f])
        totals[f] = jnp.where(lane == head, total[at], totals[f])
    for f in range(frames):
        stats_ref[f] = tops[f] + jnp.log(totals[f])


def merge_kernel(
    heads, width, meta_ref, radius_ref, mixed_ref, stats_ref, ref_0, ref_1, out_ref
):
    frames, count, _ = mixed_ref.shape
    half = count // PAIR
    first = meta_ref[0] * heads
    lane = lax.broadcasted_iota(jnp.int32, (count, LANES), 1)
    use = jnp.zeros((count, LANES), jnp.int32)
    for head in range(heads):
        use = jnp.where(lane == head, radius_ref[first + head, 0], use)
    logs, shares = [], []
    for phase, ref in enumerate((ref_0, ref_1)):
        there = jnp.where(meta_ref[3 + phase] == 0, 0, use)
        stats = ref[:, pl.ds(heads * width, LANES)].astype(jnp.float32)
        guest = (
            stats
            + pltpu.roll(stats, LANES - STRIDE, 1)
            + pltpu.roll(stats, LANES - 2 * STRIDE, 1)
        )
        guest = jnp.where(there == 0, FAR, guest)
        own = stats_ref[meta_ref[1 + phase]]
        if frames == 1 and phase == 1:
            own = logs[0]
        top = jnp.maximum(own, guest)
        guest_weight = jnp.exp(guest - top)
        total = jnp.exp(own - top) + guest_weight
        logs.append(top + jnp.log(total) if frames == 1 else None)
        shares.append(guest_weight / total)

    def store(f, lanes, mixed):
        mixed = mixed.astype(out_ref.dtype)
        for part in range(PAIR):
            out_ref[part, f, :, lanes] = mixed[part * half : (part + 1) * half]

    def boundary(spots):
        for head in range(heads):
            lanes = pl.ds(head * width, width)
            for f in sorted(set(spots)):
                mixed = mixed_ref[f, :, lanes]
                for phase, ref in enumerate((ref_0, ref_1)):
                    if spots[phase] == f:
                        guest = ref[:, lanes].astype(jnp.float32)
                        mixed = mixed + (guest - mixed) * shares[phase][:, head : head + 1]
                store(f, lanes, mixed)

    pl.when(meta_ref[1] == 0)(lambda: boundary((0, frames - 1)))
    if frames > 1:
        pl.when(meta_ref[1] != 0)(lambda: boundary((frames - 1, 0)))
    for f in range(1, frames - 1):
        store(f, slice(None), mixed_ref[f])


def join_kernel(count, meta_ref, *refs):
    pieces, out = refs[:count], refs[-1]
    depth = pieces[0].shape[0]
    for spot, ref in enumerate(pieces):
        begin = pl.multiple_of(meta_ref[spot] * depth, depth)
        out[pl.ds(begin, depth)] = ref[...]


def project_kernel(rows, near, own_out, other_out):
    both = jnp.dot(rows[...], near[...], preferred_element_type=jnp.float32)
    half = own_out.shape[0]
    own_out[...] = both[:half]
    other_out[...] = both[half:]


def total_kernel(part, partner, out):
    out[...] = (part[...] + partner[...]).astype(out.dtype)


def place_kernel(count, meta_ref, *refs):
    pieces, out, sems = refs[:count], refs[-2], refs[-1]
    wide = pieces[0].shape[-1]
    copies = []
    for spot, ref in enumerate(pieces):
        where = pl.ds(pl.multiple_of(meta_ref[spot] * wide, LANES), wide)
        copies.append(pltpu.make_async_copy(ref, out.at[:, where], sems.at[spot]))
    for copy in copies:
        copy.start()
    for copy in copies:
        copy.wait()


def cost(flops, size):
    return pl.CostEstimate(flops=flops, bytes_accessed=size, transcendentals=0)


def shards(queries, keys, values, radius, out_weight):
    n_time, n_rows, n_cols = (lax.axis_size(a) for a in ("ta", "ha", "wa"))
    at_time, at_row, at_col = (lax.axis_index(a) for a in ("ta", "ha", "wa"))
    core = at_row % PAIR
    frames, rows, cols, features = queries.shape
    heads = radius.shape[0] // PAIR
    width = features // radius.shape[0]
    half = features // PAIR
    tile_cols = cols // TILE
    area = rows * cols
    rims = n_rows > PAIR

    after, there = sides(at_col, n_cols)
    later, present = sides(at_time, n_time)
    ends = [jnp.where(x, frames - 1, 0) for x in later]
    borders = [jnp.where(x, tile_cols - 1, 0) for x in after]
    meta = jnp.stack([core, *ends, *present, *borders]).astype(jnp.int32)

    raw = [x.reshape(frames, area, features) for x in (queries, keys, values)]
    pairs = [(i, i ^ 1) for i in range(n_rows)]
    stacked = jnp.stack(raw)
    own, other = (
        lax.dynamic_slice_in_dim(stacked, which * half, half, axis=3) for which in (core, 1 - core)
    )
    other = lax.ppermute(other, "ha", pairs)
    rim = None
    if rims:
        even, odd = (jnp.where(core == i, own[1:], other[1:]) for i in range(PAIR))
        band = TILE * cols
        up = lax.ppermute(odd[:, :, -band:], "ha", line(n_rows, PAIR))
        down = lax.ppermute(even[:, :, :band], "ha", line(n_rows, -PAIR))
        rim = jnp.concatenate([up, down], axis=2)
    deep = PAIR * rows * TILE + (PAIR * TILE * TILE if rims else 0)
    side = jax.ShapeDtypeStruct((2, frames, deep, half), queries.dtype)
    edges = pl.pallas_call(
        functools.partial(edge_kernel, rims, cols),
        out_shape=(side, side),
        in_specs=[SMEM] + [VMEM] * (3 if rims else 2),
        out_specs=(VMEM,) * 2,
        compiler_params=PARAMS,
        cost_estimate=cost(1000, 2_000_000),
        name="edge",
    )(meta, own, other, *([rim] if rims else []))
    beside = [lax.ppermute(x, ("ha", "wa"), swaps(n_cols, phase, n_rows, True)) for phase, x in enumerate(edges)]
    guests = []
    for phase, frame in enumerate(ends):
        end = [lax.dynamic_index_in_dim(x[0], frame, 0, keepdims=False) for x in (own, other)]
        end = jnp.concatenate(end, axis=0)
        guests.append(lax.ppermute(end, ("ta", "ha"), swaps(n_time, phase, n_rows, False)))

    slab = features // (n_rows * n_cols)
    wide = out_weight.shape[1] // n_time
    mine = lax.dynamic_slice_in_dim(out_weight, at_time * wide, wide, axis=1)
    held = {0: mine}

    table = jnp.asarray(code_table(rows, cols, rims))
    absent = [~x for x in there]
    if rims:
        absent += [at_row < PAIR, at_row >= n_rows - PAIR]
    spot = core * 2 + at_col % 2
    spot = spot * 2 ** len(absent) + sum(jnp.where(x, 2**i, 0) for i, x in enumerate(absent))
    code = lax.dynamic_index_in_dim(table, spot, 0, keepdims=False)

    parts = [own, other] + ([rim] if rims else []) + beside
    count = PAIR * area
    unit = 4 * heads * width * count * code.shape[1]
    payload = jax.ShapeDtypeStruct((count, half + LANES), jnp.bfloat16)
    *answers, sent = pl.pallas_call(
        functools.partial(guest_kernel, rims, heads, width),
        out_shape=(payload, payload, jax.ShapeDtypeStruct(mine.shape, mine.dtype)),
        in_specs=[SMEM, SMEM] + [VMEM] * (1 + len(parts) + 2) + [HBM],
        out_specs=(VMEM, VMEM, HBM),
        scratch_shapes=[pltpu.SemaphoreType.DMA],
        compiler_params=PARAMS,
        cost_estimate=cost(2 * unit, 4_000_000),
        name="guest",
    )(meta, radius, code, *parts, *guests, mine)
    if n_cols > 1:
        held[1] = lax.ppermute(sent, "wa", cycle(n_cols, 1))
    answers = [
        lax.ppermute(x, ("ta", "ha"), swaps(n_time, phase, n_rows, False)) for phase, x in enumerate(answers)
    ]
    mixed_shape, stats_shape = (frames, count, half), (frames, count, LANES)
    mixed, stats = pl.pallas_call(
        functools.partial(host_kernel, rims, heads, width),
        out_shape=(
            jax.ShapeDtypeStruct(mixed_shape, jnp.float32),
            jax.ShapeDtypeStruct(stats_shape, jnp.float32),
        ),
        in_specs=[SMEM, SMEM] + [VMEM] * (1 + len(parts)),
        out_specs=(VMEM, VMEM),
        compiler_params=PARAMS,
        cost_estimate=cost(7 * unit, 6_000_000),
        name="host",
    )(meta, radius, code, *parts)
    attended = pl.pallas_call(
        functools.partial(merge_kernel, heads, width),
        out_shape=jax.ShapeDtypeStruct((PAIR, frames, area, half), jnp.bfloat16),
        in_specs=[SMEM, SMEM] + [VMEM] * 4,
        out_specs=VMEM,
        compiler_params=PARAMS,
        cost_estimate=cost(1000, 3_000_000),
        name="merge",
    )(meta, radius, mixed, stats, *answers)
    tokens = frames * area
    attended = attended.reshape(PAIR * tokens, half)
    if n_cols > 2:
        held[n_cols - 1] = lax.ppermute(sent, "wa", cycle(n_cols, -1))
    for s in range(2, n_cols - 1):
        held[s] = lax.ppermute(held[s - 1], "wa", cycle(n_cols, 1))
    received = [lax.ppermute(attended, "ta", cycle(n_time, s)) for s in range(1, n_time)]

    def joined(shards, at):
        count = len(shards)
        spots = jnp.stack([(at - s) % count for s in range(count)]).astype(jnp.int32)
        if shards[0].shape[0] % 16:
            return jnp.roll(jnp.stack(shards[::-1]), at + 1, axis=0).reshape(-1, wide)
        return pl.pallas_call(
            functools.partial(join_kernel, count),
            out_shape=jax.ShapeDtypeStruct((count * shards[0].shape[0], wide), mine.dtype),
            in_specs=[SMEM] + [VMEM] * count + [HBM],
            out_specs=VMEM,
            compiler_params=PARAMS,
            cost_estimate=cost(1000, 2_400_000),
            name="join",
        )(spots, *shards, received[1])

    near = joined([held[s] for s in range(n_cols)], at_col)
    if n_rows > PAIR:
        across = [lax.ppermute(near, "ha", cycle(n_rows, r)) for r in range(1, n_rows)]
        near = lax.dynamic_slice_in_dim(joined([near, *across], at_row), core * half, half, axis=0)

    def project(block):
        part = jax.ShapeDtypeStruct((tokens, wide), jnp.float32)
        return pl.pallas_call(
            project_kernel,
            out_shape=(part, part),
            in_specs=[VMEM, VMEM],
            out_specs=(VMEM, VMEM),
            compiler_params=PARAMS,
            cost_estimate=cost(2 * tokens * features * wide, 3_000_000),
            name="project",
        )(block, near)

    def total(part, partner):
        return pl.pallas_call(
            total_kernel,
            out_shape=jax.ShapeDtypeStruct((tokens, wide), queries.dtype),
            in_specs=[VMEM, VMEM],
            out_specs=VMEM,
            compiler_params=PARAMS,
            cost_estimate=cost(tokens * wide, 3_000_000),
            name="total",
        )(part, partner)

    products = []
    for block in [attended, *received]:
        part, given = project(block)
        products.append(total(part, lax.ppermute(given, "ha", pairs)))
    back = [products[0]] + [
        lax.ppermute(products[n_time - s], "ta", cycle(n_time, s)) for s in range(1, n_time)
    ]
    late = 1 % n_time
    out = None
    for group in ([s for s in range(n_time) if s != late], [late] if n_time > 1 else []):
        if group:
            origins = jnp.stack([(at_time - s) % n_time for s in group]).astype(jnp.int32)
            out = pl.pallas_call(
                functools.partial(place_kernel, len(group)),
                out_shape=jax.ShapeDtypeStruct((tokens, wide * n_time), jnp.bfloat16),
                in_specs=[SMEM] + [HBM] * (len(group) + (out is not None)),
                out_specs=HBM,
                input_output_aliases={} if out is None else {1 + len(group): 0},
                scratch_shapes=[pltpu.SemaphoreType.DMA((len(group),))],
                compiler_params=PARAMS,
                cost_estimate=cost(1000, 1_200_000),
                name="place",
            )(origins, *[back[s] for s in group], *([] if out is None else [out]))
    return out.reshape(frames, rows, cols, wide * n_time)


def solution(mesh):
    return jax.shard_map(
        shards,
        mesh=mesh,
        in_specs=(
            P("ta", "ha", "wa", None),
            P("ta", "ha", "wa", None),
            P("ta", "ha", "wa", None),
            P(),
            P(("ha", "wa"), None),
        ),
        out_specs=P("ta", "ha", "wa", None),
        check_vma=False,
    )
```

```python
import functools
import math

import jax
import jax.numpy as jnp
import numpy as np
from jax import lax
from jax.experimental import pallas as pl
from jax.experimental.pallas import tpu as pltpu
from jax.sharding import PartitionSpec as P

TILE = 4
PAIR = 2
FAR = -1e30
LANES = 128
STRIDE = 32
VMEM = pl.BlockSpec(memory_space=pltpu.VMEM)
SMEM = pl.BlockSpec(memory_space=pltpu.SMEM)
HBM = pl.BlockSpec(memory_space=pl.ANY)
PARAMS = pltpu.CompilerParams(vmem_limit_bytes=6 * 1024 * 1024)


def cycle(count, step):
    return [(i, (i + step) % count) for i in range(count)]


def swaps(count, phase, n_rows, rows_first):
    pairs = []
    for row in range(n_rows):
        for i in range(count):
            p = (i ^ 1) if phase == 0 else ((i + 1) ^ 1) - 1
            ends = ((row, i), (row, p) if 0 <= p < count else (row ^ 1, i))
            pairs.append(tuple(r * count + j if rows_first else j * n_rows + r for r, j in ends))
    return pairs


def line(count, step):
    return [(i, i + step) for i in range(count) if 0 <= i + step < count]


def sides(index, count):
    even = index % 2 == 0
    inside_after, inside_before = index < count - 1, index > 0
    return (even, ~even), (
        jnp.where(even, inside_after, inside_before),
        jnp.where(even, inside_before, inside_after),
    )


def code_table(rows, cols, rims):
    tile_cols = cols // TILE
    span = rows // TILE
    tables = []
    for core in range(PAIR):
        own = core * span
        other = (1 - core) * span
        blocks = [(own, rows), (other, rows)] + ([(-1, TILE), (2 * span, TILE)] if rims else [])
        for odd in range(2):
            query_row, query_col, key_row, key_col, key_side = [], [], [], [], []
            for base in (own, other):
                for row in range(rows):
                    for col in range(cols):
                        query_row.append(base + row // TILE)
                        query_col.append(col // TILE)
            for base, length in blocks:
                for row in range(length):
                    for col in range(cols):
                        key_row.append(base + row // TILE)
                        key_col.append(col // TILE)
                        key_side.append(-1)
            for phase in range(2):
                for base, length in blocks:
                    for row in range(length):
                        for _ in range(TILE):
                            key_row.append(base + row // TILE)
                            key_col.append(tile_cols if phase == odd else -1)
                            key_side.append(phase)
            key_row, key_col, key_side = (np.array(x)[None] for x in (key_row, key_col, key_side))
            apart_row = np.abs(np.array(query_row)[:, None] - key_row)
            apart_col = np.abs(np.array(query_col)[:, None] - key_col)
            base_code = (
                2 * (apart_row == 1)
                + 4 * (apart_col == 1)
                + 8 * ((apart_row > 1) | (apart_col > 1))
            )
            outside = [key_side == 0, key_side == 1]
            outside += [key_row < 0, key_row >= 2 * span] if rims else []
            for bits in range(2 ** len(outside)):
                code = base_code
                for which, mask in enumerate(outside):
                    if bits >> which & 1:
                        code = np.where(mask, 8, code)
                tables.append(code)
    return np.stack(tables).astype(np.int32)


def head_bias(code, radius_ref, head):
    barred = (
        8
        + jnp.where(radius_ref[head, 1] == 0, 2, 0)
        + jnp.where(radius_ref[head, 2] == 0, 4, 0)
    )
    return jnp.where((code & barred) == 0, 0.0, FAR)


class Window:
    def __init__(self, refs, rims, heads, width):
        refs = list(refs)
        self.blocks = refs[:2]
        self.extra = refs[2 : 5 if rims else 4]
        self.rest = refs[5 if rims else 4 :]
        self.frames = self.blocks[0].shape[1]
        self.width = width

    def near(self, kind, frame, head):
        lanes = pl.ds(head * self.width, self.width)
        return [ref[kind, frame, :, lanes] for ref in self.blocks]

    def query(self, frame, head):
        return jnp.concatenate(self.near(0, frame, head), axis=0)

    def pair(self, frame, head):
        lanes = pl.ds(head * self.width, self.width)
        return [
            jnp.concatenate(
                self.near(1 + kind, frame, head)
                + [ref[kind, frame, :, lanes] for ref in self.extra],
                axis=0,
            )
            for kind in range(2)
        ]


def scores_of(query, key, scale):
    return (
        lax.dot_general(
            query, key, (((1,), (1,)), ((), ())), preferred_element_type=jnp.float32
        )
        * scale
    )


def edge_kernel(rims, cols, meta_ref, *refs):
    own, other = refs[:2]
    rim = refs[2] if rims else None
    sides_out = refs[-2:]
    frames, area, half = other.shape[1:]

    def pick(rows):
        deep = rows * TILE
        shape = (2 * deep, rows * cols)
        to, of = (lax.broadcasted_iota(jnp.int32, shape, d) for d in range(2))
        spot = jnp.where(to < deep, meta_ref[5], meta_ref[6])
        to = lax.rem(to, deep)
        wanted = (to // TILE) * cols + spot * TILE + lax.rem(to, TILE)
        return deep, (of == wanted).astype(jnp.bfloat16)

    block = pick(area // cols)
    strip = pick(TILE)
    for kind in range(2):
        for frame in range(frames):
            work = [
                (own[1 + kind, frame], block),
                (other[1 + kind, frame], block),
            ]
            if rims:
                band = TILE * cols
                work += [(rim[kind, frame, i * band : (i + 1) * band], strip) for i in range(2)]
            begin = 0
            for rows, (deep, chosen) in work:
                found = jnp.dot(chosen, rows, preferred_element_type=jnp.float32)
                found = found.astype(jnp.bfloat16)
                for phase in range(2):
                    sides_out[phase][kind, frame, begin : begin + deep] = found[
                        phase * deep : (phase + 1) * deep
                    ]
                begin += deep


def guest_kernel(rims, heads, width, meta_ref, radius_ref, code_ref, *refs):
    window = Window(refs, rims, heads, width)
    guests, outs = window.rest[:2], window.rest[3:5]
    code = code_ref[...]
    count = code.shape[0]
    scale = 1.0 / math.sqrt(width)
    first = meta_ref[0] * heads
    lane = lax.broadcasted_iota(jnp.int32, (count, LANES), 1)
    tops = [jnp.zeros((count, LANES), jnp.float32) for _ in guests]
    totals = [jnp.ones((count, LANES), jnp.float32) for _ in guests]
    work = [(head, phase) for head in range(heads) for phase in range(2)]
    score, value = {}, {}
    for head in range(heads):
        bias = head_bias(code, radius_ref, first + head)
        for phase in range(2):
            key, value[head, phase] = window.pair(meta_ref[1 + phase], head)
            query = guests[phase][:, pl.ds(head * width, width)]
            score[head, phase] = scores_of(query, key, scale) + bias
    top = {at: jnp.max(score[at], axis=1, keepdims=True) for at in work}
    expo = {at: jnp.exp(score[at] - top[at]) for at in work}
    total = {at: jnp.sum(expo[at], axis=1, keepdims=True) for at in work}
    for at in work:
        head, phase = at
        probs = (expo[at] * (1.0 / total[at])).astype(jnp.bfloat16)
        mixed = jnp.dot(probs, value[at], preferred_element_type=jnp.float32)
        outs[phase][:, pl.ds(head * width, width)] = mixed.astype(jnp.bfloat16)
        tops[phase] = jnp.where(lane == head, top[at], tops[phase])
        totals[phase] = jnp.where(lane == head, total[at], totals[phase])
    for out_ref, top, total in zip(outs, tops, totals):
        rest = top + jnp.log(total)
        stats = jnp.zeros((count, LANES), jnp.float32)
        for part in range(3):
            piece = rest.astype(jnp.bfloat16).astype(jnp.float32)
            rest = rest - piece
            stats = stats + (pltpu.roll(piece, part * STRIDE, 1) if part else piece)
        out_ref[:, pl.ds(heads * width, LANES)] = stats.astype(jnp.bfloat16)


def host_kernel(rims, heads, width, meta_ref, radius_ref, code_ref, *refs):
    window = Window(refs, rims, heads, width)
    mixed_ref, stats_ref = window.rest
    frames = window.frames
    code = code_ref[...]
    count = code.shape[0]
    scale = 1.0 / math.sqrt(width)
    first = meta_ref[0] * heads
    lane = lax.broadcasted_iota(jnp.int32, (count, LANES), 1)
    tops = [jnp.zeros((count, LANES), jnp.float32) for _ in range(frames)]
    totals = [jnp.ones((count, LANES), jnp.float32) for _ in range(frames)]
    work = [(head, f) for head in range(heads) for f in range(frames)]
    score, value = {}, {}
    for head in range(heads):
        bias = head_bias(code, radius_ref, first + head)
        bias_apart = jnp.where(radius_ref[first + head, 0] == 0, FAR, bias)
        query = [window.query(f, head) for f in range(frames)]
        pairs = [window.pair(f, head) for f in range(frames)]
        blocks = {}
        for frame in range(frames):
            near = range(max(0, frame - 1), min(frames, frame + 2))
            block = scores_of(
                jnp.concatenate([query[f] for f in near], axis=0), pairs[frame][0], scale
            )
            for spot, f in enumerate(near):
                blocks[f, frame] = block[spot * count : (spot + 1) * count] + (
                    bias if f == frame else bias_apart
                )
        for f in range(frames):
            near = range(max(0, f - 1), min(frames, f + 2))
            score[head, f] = jnp.concatenate([blocks[f, g] for g in near], axis=1)
            value[head, f] = jnp.concatenate([pairs[g][1] for g in near], axis=0)
    top = {at: jnp.max(score[at], axis=1, keepdims=True) for at in work}
    expo = {at: jnp.exp(score[at] - top[at]) for at in work}
    total = {at: jnp.sum(expo[at], axis=1, keepdims=True) for at in work}
    for at in work:
        head, f = at
        probs = (expo[at] * (1.0 / total[at])).astype(jnp.bfloat16)
        mixed_ref[f, :, pl.ds(head * width, width)] = jnp.dot(
            probs, value[at], preferred_element_type=jnp.float32
        )
        tops[f] = jnp.where(lane == head, top[at], tops[f])
        totals[f] = jnp.where(lane == head, total[at], totals[f])
    for f in range(frames):
        stats_ref[f] = tops[f] + jnp.log(totals[f])


def merge_kernel(
    heads, width, meta_ref, radius_ref, mixed_ref, stats_ref, ref_0, ref_1, out_ref
):
    frames, count, _ = mixed_ref.shape
    half = count // PAIR
    first = meta_ref[0] * heads
    lane = lax.broadcasted_iota(jnp.int32, (count, LANES), 1)
    use = jnp.zeros((count, LANES), jnp.int32)
    for head in range(heads):
        use = jnp.where(lane == head, radius_ref[first + head, 0], use)
    logs, shares = [], []
    for phase, ref in enumerate((ref_0, ref_1)):
        there = jnp.where(meta_ref[3 + phase] == 0, 0, use)
        stats = ref[:, pl.ds(heads * width, LANES)].astype(jnp.float32)
        guest = (
            stats
            + pltpu.roll(stats, LANES - STRIDE, 1)
            + pltpu.roll(stats, LANES - 2 * STRIDE, 1)
        )
        guest = jnp.where(there == 0, FAR, guest)
        own = stats_ref[meta_ref[1 + phase]]
        if frames == 1 and phase == 1:
            own = logs[0]
        top = jnp.maximum(own, guest)
        guest_weight = jnp.exp(guest - top)
        total = jnp.exp(own - top) + guest_weight
        logs.append(top + jnp.log(total) if frames == 1 else None)
        shares.append(guest_weight / total)

    def store(f, lanes, mixed):
        mixed = mixed.astype(out_ref.dtype)
        for part in range(PAIR):
            out_ref[part, f, :, lanes] = mixed[part * half : (part + 1) * half]

    def boundary(spots):
        for head in range(heads):
            lanes = pl.ds(head * width, width)
            for f in sorted(set(spots)):
                mixed = mixed_ref[f, :, lanes]
                for phase, ref in enumerate((ref_0, ref_1)):
                    if spots[phase] == f:
                        guest = ref[:, lanes].astype(jnp.float32)
                        mixed = mixed + (guest - mixed) * shares[phase][:, head : head + 1]
                store(f, lanes, mixed)

    pl.when(meta_ref[1] == 0)(lambda: boundary((0, frames - 1)))
    if frames > 1:
        pl.when(meta_ref[1] != 0)(lambda: boundary((frames - 1, 0)))
    for f in range(1, frames - 1):
        store(f, slice(None), mixed_ref[f])


def join_kernel(count, meta_ref, *refs):
    pieces, out = refs[:count], refs[-1]
    depth = pieces[0].shape[0]
    for spot, ref in enumerate(pieces):
        begin = pl.multiple_of(meta_ref[spot] * depth, depth)
        out[pl.ds(begin, depth)] = ref[...]


def project_kernel(rows, near, own_out, other_out):
    both = jnp.dot(rows[...], near[...], preferred_element_type=jnp.float32)
    half = own_out.shape[0]
    own_out[...] = both[:half]
    other_out[...] = both[half:]


def total_kernel(part, partner, out):
    out[...] = (part[...] + partner[...]).astype(out.dtype)


def place_kernel(count, meta_ref, *refs):
    pieces, out, sems = refs[:count], refs[-2], refs[-1]
    wide = pieces[0].shape[-1]
    copies = []
    for spot, ref in enumerate(pieces):
        where = pl.ds(pl.multiple_of(meta_ref[spot] * wide, LANES), wide)
        copies.append(pltpu.make_async_copy(ref, out.at[:, where], sems.at[spot]))
    for copy in copies:
        copy.start()
    for copy in copies:
        copy.wait()


def cost(flops, size):
    return pl.CostEstimate(flops=flops, bytes_accessed=size, transcendentals=0)


def shards(queries, keys, values, radius, out_weight):
    n_time, n_rows, n_cols = (lax.axis_size(a) for a in ("ta", "ha", "wa"))
    at_time, at_row, at_col = (lax.axis_index(a) for a in ("ta", "ha", "wa"))
    core = at_row % PAIR
    frames, rows, cols, features = queries.shape
    heads = radius.shape[0] // PAIR
    width = features // radius.shape[0]
    half = features // PAIR
    tile_cols = cols // TILE
    area = rows * cols
    rims = n_rows > PAIR

    after, there = sides(at_col, n_cols)
    later, present = sides(at_time, n_time)
    ends = [jnp.where(x, frames - 1, 0) for x in later]
    borders = [jnp.where(x, tile_cols - 1, 0) for x in after]
    meta = jnp.stack([core, *ends, *present, *borders]).astype(jnp.int32)

    raw = [x.reshape(frames, area, features) for x in (queries, keys, values)]
    pairs = [(i, i ^ 1) for i in range(n_rows)]
    stacked = jnp.stack(raw)
    own, other = (
        lax.dynamic_slice_in_dim(stacked, which * half, half, axis=3) for which in (core, 1 - core)
    )
    other = lax.ppermute(other, "ha", pairs)
    rim = None
    if rims:
        even, odd = (jnp.where(core == i, own[1:], other[1:]) for i in range(PAIR))
        band = TILE * cols
        up = lax.ppermute(odd[:, :, -band:], "ha", line(n_rows, PAIR))
        down = lax.ppermute(even[:, :, :band], "ha", line(n_rows, -PAIR))
        rim = jnp.concatenate([up, down], axis=2)
    deep = PAIR * rows * TILE + (PAIR * TILE * TILE if rims else 0)
    side = jax.ShapeDtypeStruct((2, frames, deep, half), queries.dtype)
    edges = pl.pallas_call(
        functools.partial(edge_kernel, rims, cols),
        out_shape=(side, side),
        in_specs=[SMEM] + [VMEM] * (3 if rims else 2),
        out_specs=(VMEM,) * 2,
        compiler_params=PARAMS,
        cost_estimate=cost(1000, 2_000_000),
        name="edge",
    )(meta, own, other, *([rim] if rims else []))
    beside = [lax.ppermute(x, ("ha", "wa"), swaps(n_cols, phase, n_rows, True)) for phase, x in enumerate(edges)]
    guests = []
    for phase, frame in enumerate(ends):
        end = [lax.dynamic_index_in_dim(x[0], frame, 0, keepdims=False) for x in (own, other)]
        end = jnp.concatenate(end, axis=0)
        guests.append(lax.ppermute(end, ("ta", "ha"), swaps(n_time, phase, n_rows, False)))

    slab = features // (n_rows * n_cols)
    wide = out_weight.shape[1] // n_time
    mine = lax.dynamic_slice_in_dim(out_weight, at_time * wide, wide, axis=1)
    held = {0: mine}

    table = jnp.asarray(code_table(rows, cols, rims))
    absent = [~x for x in there]
    if rims:
        absent += [at_row < PAIR, at_row >= n_rows - PAIR]
    spot = core * 2 + at_col % 2
    spot = spot * 2 ** len(absent) + sum(jnp.where(x, 2**i, 0) for i, x in enumerate(absent))
    code = lax.dynamic_index_in_dim(table, spot, 0, keepdims=False)

    parts = [own, other] + ([rim] if rims else []) + beside
    count = PAIR * area
    unit = 4 * heads * width * count * code.shape[1]
    payload = jax.ShapeDtypeStruct((count, half + LANES), jnp.bfloat16)
    *answers, sent = pl.pallas_call(
        functools.partial(guest_kernel, rims, heads, width),
        out_shape=(payload, payload, jax.ShapeDtypeStruct(mine.shape, mine.dtype)),
        in_specs=[SMEM, SMEM] + [VMEM] * (1 + len(parts) + 2) + [HBM],
        out_specs=(VMEM, VMEM, HBM),
        input_output_aliases={5 + len(parts): 2},
        compiler_params=PARAMS,
        cost_estimate=cost(2 * unit, 4_000_000),
        name="guest",
    )(meta, radius, code, *parts, *guests, mine)
    held[0] = sent
    if n_cols > 1:
        held[1] = lax.ppermute(sent, "wa", cycle(n_cols, 1))
    answers = [
        lax.ppermute(x, ("ta", "ha"), swaps(n_time, phase, n_rows, False)) for phase, x in enumerate(answers)
    ]
    mixed_shape, stats_shape = (frames, count, half), (frames, count, LANES)
    mixed, stats = pl.pallas_call(
        functools.partial(host_kernel, rims, heads, width),
        out_shape=(
            jax.ShapeDtypeStruct(mixed_shape, jnp.float32),
            jax.ShapeDtypeStruct(stats_shape, jnp.float32),
        ),
        in_specs=[SMEM, SMEM] + [VMEM] * (1 + len(parts)),
        out_specs=(VMEM, VMEM),
        compiler_params=PARAMS,
        cost_estimate=cost(7 * unit, 6_000_000),
        name="host",
    )(meta, radius, code, *parts)
    attended = pl.pallas_call(
        functools.partial(merge_kernel, heads, width),
        out_shape=jax.ShapeDtypeStruct((PAIR, frames, area, half), jnp.bfloat16),
        in_specs=[SMEM, SMEM] + [VMEM] * 4,
        out_specs=VMEM,
        compiler_params=PARAMS,
        cost_estimate=cost(1000, 3_000_000),
        name="merge",
    )(meta, radius, mixed, stats, *answers)
    tokens = frames * area
    attended = attended.reshape(PAIR * tokens, half)
    if n_cols > 2:
        held[n_cols - 1] = lax.ppermute(sent, "wa", cycle(n_cols, -1))
    for s in range(2, n_cols - 1):
        held[s] = lax.ppermute(held[s - 1], "wa", cycle(n_cols, 1))
    received = [lax.ppermute(attended, "ta", cycle(n_time, s)) for s in range(1, n_time)]

    def joined(shards, at):
        count = len(shards)
        spots = jnp.stack([(at - s) % count for s in range(count)]).astype(jnp.int32)
        if shards[0].shape[0] % 16:
            return jnp.roll(jnp.stack(shards[::-1]), at + 1, axis=0).reshape(-1, wide)
        return pl.pallas_call(
            functools.partial(join_kernel, count),
            out_shape=jax.ShapeDtypeStruct((count * shards[0].shape[0], wide), mine.dtype),
            in_specs=[SMEM] + [VMEM] * count + [HBM],
            out_specs=VMEM,
            compiler_params=PARAMS,
            cost_estimate=cost(1000, 2_400_000),
            name="join",
        )(spots, *shards, received[1])

    near = joined([held[s] for s in range(n_cols)], at_col)
    if n_rows > PAIR:
        across = [lax.ppermute(near, "ha", cycle(n_rows, r)) for r in range(1, n_rows)]
        near = lax.dynamic_slice_in_dim(joined([near, *across], at_row), core * half, half, axis=0)

    weight = 36 * 2 * tokens * features * wide

    def project(block):
        part = jax.ShapeDtypeStruct((tokens, wide), jnp.float32)
        return pl.pallas_call(
            project_kernel,
            out_shape=(part, part),
            in_specs=[VMEM, VMEM],
            out_specs=(VMEM, VMEM),
            compiler_params=PARAMS,
            cost_estimate=cost(weight, 3_000_000),
            name="project",
        )(block, near)

    def total(part, partner):
        return pl.pallas_call(
            total_kernel,
            out_shape=jax.ShapeDtypeStruct((tokens, wide), queries.dtype),
            in_specs=[VMEM, VMEM],
            out_specs=VMEM,
            compiler_params=PARAMS,
            cost_estimate=cost(weight, 3_000_000),
            name="total",
        )(part, partner)

    products = []
    for block in [attended, *received]:
        part, given = project(block)
        products.append(total(part, lax.ppermute(given, "ha", pairs)))
    back = [products[0]] + [
        lax.ppermute(products[n_time - s], "ta", cycle(n_time, s)) for s in range(1, n_time)
    ]
    late = 1 % n_time
    out = None
    for group in ([s for s in range(n_time) if s != late], [late] if n_time > 1 else []):
        if group:
            origins = jnp.stack([(at_time - s) % n_time for s in group]).astype(jnp.int32)
            out = pl.pallas_call(
                functools.partial(place_kernel, len(group)),
                out_shape=jax.ShapeDtypeStruct((tokens, wide * n_time), jnp.bfloat16),
                in_specs=[SMEM] + [HBM] * (len(group) + (out is not None)),
                out_specs=HBM,
                input_output_aliases={} if out is None else {1 + len(group): 0},
                scratch_shapes=[pltpu.SemaphoreType.DMA((len(group),))],
                compiler_params=PARAMS,
                cost_estimate=cost(1000, 1_200_000),
                name="place",
            )(origins, *[back[s] for s in group], *([] if out is None else [out]))
    return out.reshape(frames, rows, cols, wide * n_time)


def solution(mesh):
    return jax.shard_map(
        shards,
        mesh=mesh,
        in_specs=(
            P("ta", "ha", "wa", None),
            P("ta", "ha", "wa", None),
            P("ta", "ha", "wa", None),
            P(),
            P(("ha", "wa"), None),
        ),
        out_specs=P("ta", "ha", "wa", None),
        check_vma=False,
    )
```

```python
import functools
import math

import jax
import jax.numpy as jnp
import numpy as np
from jax import lax
from jax.experimental import pallas as pl
from jax.experimental.pallas import tpu as pltpu
from jax.sharding import PartitionSpec as P

TILE = 4
PAIR = 2
FAR = -1e30
LANES = 128
STRIDE = 32
VMEM = pl.BlockSpec(memory_space=pltpu.VMEM)
SMEM = pl.BlockSpec(memory_space=pltpu.SMEM)
HBM = pl.BlockSpec(memory_space=pl.ANY)
PARAMS = pltpu.CompilerParams(vmem_limit_bytes=6 * 1024 * 1024)


def cycle(count, step):
    return [(i, (i + step) % count) for i in range(count)]


def swaps(count, phase, n_rows, rows_first):
    pairs = []
    for row in range(n_rows):
        for i in range(count):
            p = (i ^ 1) if phase == 0 else ((i + 1) ^ 1) - 1
            ends = ((row, i), (row, p) if 0 <= p < count else (row ^ 1, i))
            pairs.append(tuple(r * count + j if rows_first else j * n_rows + r for r, j in ends))
    return pairs


def line(count, step):
    return [(i, i + step) for i in range(count) if 0 <= i + step < count]


def sides(index, count):
    even = index % 2 == 0
    inside_after, inside_before = index < count - 1, index > 0
    return (even, ~even), (
        jnp.where(even, inside_after, inside_before),
        jnp.where(even, inside_before, inside_after),
    )


def code_table(rows, cols, rims):
    tile_cols = cols // TILE
    span = rows // TILE
    tables = []
    for core in range(PAIR):
        own = core * span
        other = (1 - core) * span
        blocks = [(own, rows), (other, rows)] + ([(-1, TILE), (2 * span, TILE)] if rims else [])
        for odd in range(2):
            query_row, query_col, key_row, key_col, key_side = [], [], [], [], []
            for base in (own, other):
                for row in range(rows):
                    for col in range(cols):
                        query_row.append(base + row // TILE)
                        query_col.append(col // TILE)
            for base, length in blocks:
                for row in range(length):
                    for col in range(cols):
                        key_row.append(base + row // TILE)
                        key_col.append(col // TILE)
                        key_side.append(-1)
            for phase in range(2):
                for base, length in blocks:
                    for row in range(length):
                        for _ in range(TILE):
                            key_row.append(base + row // TILE)
                            key_col.append(tile_cols if phase == odd else -1)
                            key_side.append(phase)
            key_row, key_col, key_side = (np.array(x)[None] for x in (key_row, key_col, key_side))
            apart_row = np.abs(np.array(query_row)[:, None] - key_row)
            apart_col = np.abs(np.array(query_col)[:, None] - key_col)
            base_code = (
                2 * (apart_row == 1)
                + 4 * (apart_col == 1)
                + 8 * ((apart_row > 1) | (apart_col > 1))
            )
            outside = [key_side == 0, key_side == 1]
            outside += [key_row < 0, key_row >= 2 * span] if rims else []
            for bits in range(2 ** len(outside)):
                code = base_code
                for which, mask in enumerate(outside):
                    if bits >> which & 1:
                        code = np.where(mask, 8, code)
                tables.append(code)
    return np.stack(tables).astype(np.int32)


def head_bias(code, radius_ref, head):
    barred = (
        8
        + jnp.where(radius_ref[head, 1] == 0, 2, 0)
        + jnp.where(radius_ref[head, 2] == 0, 4, 0)
    )
    return jnp.where((code & barred) == 0, 0.0, FAR)


class Window:
    def __init__(self, refs, rims, heads, width):
        refs = list(refs)
        self.blocks = refs[:2]
        self.extra = refs[2 : 5 if rims else 4]
        self.rest = refs[5 if rims else 4 :]
        self.frames = self.blocks[0].shape[1]
        self.width = width

    def near(self, kind, frame, head):
        lanes = pl.ds(head * self.width, self.width)
        return [ref[kind, frame, :, lanes] for ref in self.blocks]

    def query(self, frame, head):
        return jnp.concatenate(self.near(0, frame, head), axis=0)

    def pair(self, frame, head):
        lanes = pl.ds(head * self.width, self.width)
        return [
            jnp.concatenate(
                self.near(1 + kind, frame, head)
                + [ref[kind, frame, :, lanes] for ref in self.extra],
                axis=0,
            )
            for kind in range(2)
        ]


def scores_of(query, key, scale):
    return (
        lax.dot_general(
            query, key, (((1,), (1,)), ((), ())), preferred_element_type=jnp.float32
        )
        * scale
    )


def edge_kernel(rims, cols, meta_ref, *refs):
    own, other = refs[:2]
    rim = refs[2] if rims else None
    sides_out = refs[-2:]
    frames, area, half = other.shape[1:]

    def pick(rows):
        deep = rows * TILE
        shape = (2 * deep, rows * cols)
        to, of = (lax.broadcasted_iota(jnp.int32, shape, d) for d in range(2))
        spot = jnp.where(to < deep, meta_ref[5], meta_ref[6])
        to = lax.rem(to, deep)
        wanted = (to // TILE) * cols + spot * TILE + lax.rem(to, TILE)
        return deep, (of == wanted).astype(jnp.bfloat16)

    block = pick(area // cols)
    strip = pick(TILE)
    for kind in range(2):
        for frame in range(frames):
            work = [
                (own[1 + kind, frame], block),
                (other[1 + kind, frame], block),
            ]
            if rims:
                band = TILE * cols
                work += [(rim[kind, frame, i * band : (i + 1) * band], strip) for i in range(2)]
            begin = 0
            for rows, (deep, chosen) in work:
                found = jnp.dot(chosen, rows, preferred_element_type=jnp.float32)
                found = found.astype(jnp.bfloat16)
                for phase in range(2):
                    sides_out[phase][kind, frame, begin : begin + deep] = found[
                        phase * deep : (phase + 1) * deep
                    ]
                begin += deep


def guest_kernel(rims, heads, width, meta_ref, radius_ref, code_ref, *refs):
    window = Window(refs, rims, heads, width)
    guests, outs = window.rest[:2], window.rest[3:5]
    code = code_ref[...]
    count = code.shape[0]
    scale = 1.0 / math.sqrt(width)
    first = meta_ref[0] * heads
    lane = lax.broadcasted_iota(jnp.int32, (count, LANES), 1)
    tops = [jnp.zeros((count, LANES), jnp.float32) for _ in guests]
    totals = [jnp.ones((count, LANES), jnp.float32) for _ in guests]
    work = [(head, phase) for head in range(heads) for phase in range(2)]
    score, value = {}, {}
    for head in range(heads):
        bias = head_bias(code, radius_ref, first + head)
        for phase in range(2):
            key, value[head, phase] = window.pair(meta_ref[1 + phase], head)
            query = guests[phase][:, pl.ds(head * width, width)]
            score[head, phase] = scores_of(query, key, scale) + bias
    top = {at: jnp.max(score[at], axis=1, keepdims=True) for at in work}
    expo = {at: jnp.exp(score[at] - top[at]) for at in work}
    total = {at: jnp.sum(expo[at], axis=1, keepdims=True) for at in work}
    for at in work:
        head, phase = at
        probs = (expo[at] * (1.0 / total[at])).astype(jnp.bfloat16)
        mixed = jnp.dot(probs, value[at], preferred_element_type=jnp.float32)
        outs[phase][:, pl.ds(head * width, width)] = mixed.astype(jnp.bfloat16)
        tops[phase] = jnp.where(lane == head, top[at], tops[phase])
        totals[phase] = jnp.where(lane == head, total[at], totals[phase])
    for out_ref, top, total in zip(outs, tops, totals):
        rest = top + jnp.log(total)
        stats = jnp.zeros((count, LANES), jnp.float32)
        for part in range(3):
            piece = rest.astype(jnp.bfloat16).astype(jnp.float32)
            rest = rest - piece
            stats = stats + (pltpu.roll(piece, part * STRIDE, 1) if part else piece)
        out_ref[:, pl.ds(heads * width, LANES)] = stats.astype(jnp.bfloat16)


def host_kernel(rims, heads, width, meta_ref, radius_ref, code_ref, *refs):
    window = Window(refs, rims, heads, width)
    mixed_ref, stats_ref = window.rest
    frames = window.frames
    code = code_ref[...]
    count = code.shape[0]
    scale = 1.0 / math.sqrt(width)
    first = meta_ref[0] * heads
    lane = lax.broadcasted_iota(jnp.int32, (count, LANES), 1)
    tops = [jnp.zeros((count, LANES), jnp.float32) for _ in range(frames)]
    totals = [jnp.ones((count, LANES), jnp.float32) for _ in range(frames)]
    work = [(head, f) for head in range(heads) for f in range(frames)]
    score, value = {}, {}
    for head in range(heads):
        bias = head_bias(code, radius_ref, first + head)
        bias_apart = jnp.where(radius_ref[first + head, 0] == 0, FAR, bias)
        query = [window.query(f, head) for f in range(frames)]
        pairs = [window.pair(f, head) for f in range(frames)]
        blocks = {}
        for frame in range(frames):
            near = range(max(0, frame - 1), min(frames, frame + 2))
            block = scores_of(
                jnp.concatenate([query[f] for f in near], axis=0), pairs[frame][0], scale
            )
            for spot, f in enumerate(near):
                blocks[f, frame] = block[spot * count : (spot + 1) * count] + (
                    bias if f == frame else bias_apart
                )
        for f in range(frames):
            near = range(max(0, f - 1), min(frames, f + 2))
            score[head, f] = jnp.concatenate([blocks[f, g] for g in near], axis=1)
            value[head, f] = jnp.concatenate([pairs[g][1] for g in near], axis=0)
    top = {at: jnp.max(score[at], axis=1, keepdims=True) for at in work}
    expo = {at: jnp.exp(score[at] - top[at]) for at in work}
    total = {at: jnp.sum(expo[at], axis=1, keepdims=True) for at in work}
    for at in work:
        head, f = at
        probs = (expo[at] * (1.0 / total[at])).astype(jnp.bfloat16)
        mixed_ref[f, :, pl.ds(head * width, width)] = jnp.dot(
            probs, value[at], preferred_element_type=jnp.float32
        )
        tops[f] = jnp.where(lane == head, top[at], tops[f])
        totals[f] = jnp.where(lane == head, total[at], totals[f])
    for f in range(frames):
        stats_ref[f] = tops[f] + jnp.log(totals[f])


def merge_kernel(
    heads, width, meta_ref, radius_ref, mixed_ref, stats_ref, ref_0, ref_1, out_ref
):
    frames, count, _ = mixed_ref.shape
    half = count // PAIR
    first = meta_ref[0] * heads
    lane = lax.broadcasted_iota(jnp.int32, (count, LANES), 1)
    use = jnp.zeros((count, LANES), jnp.int32)
    for head in range(heads):
        use = jnp.where(lane == head, radius_ref[first + head, 0], use)
    logs, shares = [], []
    for phase, ref in enumerate((ref_0, ref_1)):
        there = jnp.where(meta_ref[3 + phase] == 0, 0, use)
        stats = ref[:, pl.ds(heads * width, LANES)].astype(jnp.float32)
        guest = (
            stats
            + pltpu.roll(stats, LANES - STRIDE, 1)
            + pltpu.roll(stats, LANES - 2 * STRIDE, 1)
        )
        guest = jnp.where(there == 0, FAR, guest)
        own = stats_ref[meta_ref[1 + phase]]
        if frames == 1 and phase == 1:
            own = logs[0]
        top = jnp.maximum(own, guest)
        guest_weight = jnp.exp(guest - top)
        total = jnp.exp(own - top) + guest_weight
        logs.append(top + jnp.log(total) if frames == 1 else None)
        shares.append(guest_weight / total)

    def store(f, lanes, mixed):
        mixed = mixed.astype(out_ref.dtype)
        for part in range(PAIR):
            out_ref[part, f, :, lanes] = mixed[part * half : (part + 1) * half]

    def boundary(spots):
        for head in range(heads):
            lanes = pl.ds(head * width, width)
            for f in sorted(set(spots)):
                mixed = mixed_ref[f, :, lanes]
                for phase, ref in enumerate((ref_0, ref_1)):
                    if spots[phase] == f:
                        guest = ref[:, lanes].astype(jnp.float32)
                        mixed = mixed + (guest - mixed) * shares[phase][:, head : head + 1]
                store(f, lanes, mixed)

    pl.when(meta_ref[1] == 0)(lambda: boundary((0, frames - 1)))
    if frames > 1:
        pl.when(meta_ref[1] != 0)(lambda: boundary((frames - 1, 0)))
    for f in range(1, frames - 1):
        store(f, slice(None), mixed_ref[f])


def join_kernel(count, meta_ref, *refs):
    pieces, out = refs[:count], refs[-1]
    depth = pieces[0].shape[0]
    for spot, ref in enumerate(pieces):
        begin = pl.multiple_of(meta_ref[spot] * depth, depth)
        out[pl.ds(begin, depth)] = ref[...]


def project_kernel(rows, near, own_out, other_out):
    both = jnp.dot(rows[...], near[...], preferred_element_type=jnp.float32)
    half = own_out.shape[0]
    own_out[...] = both[:half]
    other_out[...] = both[half:]


def total_kernel(part, partner, out):
    out[...] = (part[...] + partner[...]).astype(out.dtype)


def place_kernel(count, meta_ref, *refs):
    pieces, out, sems = refs[:count], refs[-2], refs[-1]
    wide = pieces[0].shape[-1]
    copies = []
    for spot, ref in enumerate(pieces):
        where = pl.ds(pl.multiple_of(meta_ref[spot] * wide, LANES), wide)
        copies.append(pltpu.make_async_copy(ref, out.at[:, where], sems.at[spot]))
    for copy in copies:
        copy.start()
    for copy in copies:
        copy.wait()


def cost(flops, size):
    return pl.CostEstimate(flops=flops, bytes_accessed=size, transcendentals=0)


def shards(queries, keys, values, radius, out_weight):
    n_time, n_rows, n_cols = (lax.axis_size(a) for a in ("ta", "ha", "wa"))
    at_time, at_row, at_col = (lax.axis_index(a) for a in ("ta", "ha", "wa"))
    core = at_row % PAIR
    frames, rows, cols, features = queries.shape
    heads = radius.shape[0] // PAIR
    width = features // radius.shape[0]
    half = features // PAIR
    tile_cols = cols // TILE
    area = rows * cols
    rims = n_rows > PAIR

    after, there = sides(at_col, n_cols)
    later, present = sides(at_time, n_time)
    ends = [jnp.where(x, frames - 1, 0) for x in later]
    borders = [jnp.where(x, tile_cols - 1, 0) for x in after]
    meta = jnp.stack([core, *ends, *present, *borders]).astype(jnp.int32)

    raw = [x.reshape(frames, area, features) for x in (queries, keys, values)]
    pairs = [(i, i ^ 1) for i in range(n_rows)]
    stacked = jnp.stack(raw)
    own, other = (
        lax.dynamic_slice_in_dim(stacked, which * half, half, axis=3) for which in (core, 1 - core)
    )
    other = lax.ppermute(other, "ha", pairs)
    rim = None
    if rims:
        even, odd = (jnp.where(core == i, own[1:], other[1:]) for i in range(PAIR))
        band = TILE * cols
        up = lax.ppermute(odd[:, :, -band:], "ha", line(n_rows, PAIR))
        down = lax.ppermute(even[:, :, :band], "ha", line(n_rows, -PAIR))
        rim = jnp.concatenate([up, down], axis=2)
    deep = PAIR * rows * TILE + (PAIR * TILE * TILE if rims else 0)
    side = jax.ShapeDtypeStruct((2, frames, deep, half), queries.dtype)
    edges = pl.pallas_call(
        functools.partial(edge_kernel, rims, cols),
        out_shape=(side, side),
        in_specs=[SMEM] + [VMEM] * (3 if rims else 2),
        out_specs=(VMEM,) * 2,
        compiler_params=PARAMS,
        cost_estimate=cost(1000, 2_000_000),
        name="edge",
    )(meta, own, other, *([rim] if rims else []))
    beside = [lax.ppermute(x, ("ha", "wa"), swaps(n_cols, phase, n_rows, True)) for phase, x in enumerate(edges)]
    guests = []
    for phase, frame in enumerate(ends):
        end = [lax.dynamic_index_in_dim(x[0], frame, 0, keepdims=False) for x in (own, other)]
        end = jnp.concatenate(end, axis=0)
        guests.append(lax.ppermute(end, ("ta", "ha"), swaps(n_time, phase, n_rows, False)))

    slab = features // (n_rows * n_cols)
    wide = out_weight.shape[1] // n_time
    mine = lax.dynamic_slice_in_dim(out_weight, at_time * wide, wide, axis=1)
    held = {0: mine}

    table = jnp.asarray(code_table(rows, cols, rims))
    absent = [~x for x in there]
    if rims:
        absent += [at_row < PAIR, at_row >= n_rows - PAIR]
    spot = core * 2 + at_col % 2
    spot = spot * 2 ** len(absent) + sum(jnp.where(x, 2**i, 0) for i, x in enumerate(absent))
    code = lax.dynamic_index_in_dim(table, spot, 0, keepdims=False)

    parts = [own, other] + ([rim] if rims else []) + beside
    count = PAIR * area
    unit = 4 * heads * width * count * code.shape[1]
    payload = jax.ShapeDtypeStruct((count, half + LANES), jnp.bfloat16)
    *answers, sent = pl.pallas_call(
        functools.partial(guest_kernel, rims, heads, width),
        out_shape=(payload, payload, jax.ShapeDtypeStruct(mine.shape, mine.dtype)),
        in_specs=[SMEM, SMEM] + [VMEM] * (1 + len(parts) + 2) + [HBM],
        out_specs=(VMEM, VMEM, HBM),
        input_output_aliases={5 + len(parts): 2},
        compiler_params=PARAMS,
        cost_estimate=cost(2 * unit, 4_000_000),
        name="guest",
    )(meta, radius, code, *parts, *guests, mine)
    held[0] = sent
    if n_cols > 1:
        held[1] = lax.ppermute(sent, "wa", cycle(n_cols, 1))
    answers = [
        lax.ppermute(x, ("ta", "ha"), swaps(n_time, phase, n_rows, False)) for phase, x in enumerate(answers)
    ]
    mixed_shape, stats_shape = (frames, count, half), (frames, count, LANES)
    mixed, stats = pl.pallas_call(
        functools.partial(host_kernel, rims, heads, width),
        out_shape=(
            jax.ShapeDtypeStruct(mixed_shape, jnp.float32),
            jax.ShapeDtypeStruct(stats_shape, jnp.float32),
        ),
        in_specs=[SMEM, SMEM] + [VMEM] * (1 + len(parts)),
        out_specs=(VMEM, VMEM),
        compiler_params=PARAMS,
        cost_estimate=cost(7 * unit, 6_000_000),
        name="host",
    )(meta, radius, code, *parts)
    attended = pl.pallas_call(
        functools.partial(merge_kernel, heads, width),
        out_shape=jax.ShapeDtypeStruct((PAIR, frames, area, half), jnp.bfloat16),
        in_specs=[SMEM, SMEM] + [VMEM] * 4,
        out_specs=VMEM,
        compiler_params=PARAMS,
        cost_estimate=cost(1000, 3_000_000),
        name="merge",
    )(meta, radius, mixed, stats, *answers)
    tokens = frames * area
    attended = attended.reshape(PAIR * tokens, half)
    if n_cols > 2:
        held[n_cols - 1] = lax.ppermute(sent, "wa", cycle(n_cols, -1))
    for s in range(2, n_cols - 1):
        held[s] = lax.ppermute(held[s - 1], "wa", cycle(n_cols, 1))
    received = [lax.ppermute(attended, "ta", cycle(n_time, s)) for s in range(1, n_time)]

    def joined(shards, at):
        count = len(shards)
        spots = jnp.stack([(at - s) % count for s in range(count)]).astype(jnp.int32)
        if shards[0].shape[0] % 16:
            return jnp.roll(jnp.stack(shards[::-1]), at + 1, axis=0).reshape(-1, wide)
        return pl.pallas_call(
            functools.partial(join_kernel, count),
            out_shape=jax.ShapeDtypeStruct((count * shards[0].shape[0], wide), mine.dtype),
            in_specs=[SMEM] + [VMEM] * count + [HBM],
            out_specs=VMEM,
            compiler_params=PARAMS,
            cost_estimate=cost(1000, 2_400_000),
            name="join",
        )(spots, *shards, (received + [attended] * 2)[1])

    near = joined([held[s] for s in range(n_cols)], at_col)
    if n_rows > PAIR:
        across = [lax.ppermute(near, "ha", cycle(n_rows, r)) for r in range(1, n_rows)]
        near = lax.dynamic_slice_in_dim(joined([near, *across], at_row), core * half, half, axis=0)

    weight = 36 * 2 * tokens * features * wide

    def project(block):
        part = jax.ShapeDtypeStruct((tokens, wide), jnp.float32)
        return pl.pallas_call(
            project_kernel,
            out_shape=(part, part),
            in_specs=[VMEM, VMEM],
            out_specs=(VMEM, VMEM),
            compiler_params=PARAMS,
            cost_estimate=cost(weight, 3_000_000),
            name="project",
        )(block, near)

    def total(part, partner):
        return pl.pallas_call(
            total_kernel,
            out_shape=jax.ShapeDtypeStruct((tokens, wide), queries.dtype),
            in_specs=[VMEM, VMEM],
            out_specs=VMEM,
            compiler_params=PARAMS,
            cost_estimate=cost(weight, 3_000_000),
            name="total",
        )(part, partner)

    products = []
    for block in [attended, *received]:
        part, given = project(block)
        products.append(total(part, lax.ppermute(given, "ha", pairs)))
    back = [products[0]] + [
        lax.ppermute(products[n_time - s], "ta", cycle(n_time, s)) for s in range(1, n_time)
    ]
    late = 1 % n_time
    out = None
    for group in ([s for s in range(n_time) if s != late], [late] if n_time > 1 else []):
        if group:
            origins = jnp.stack([(at_time - s) % n_time for s in group]).astype(jnp.int32)
            out = pl.pallas_call(
                functools.partial(place_kernel, len(group)),
                out_shape=jax.ShapeDtypeStruct((tokens, wide * n_time), jnp.bfloat16),
                in_specs=[SMEM] + [HBM] * (len(group) + (out is not None)),
                out_specs=HBM,
                input_output_aliases={} if out is None else {1 + len(group): 0},
                scratch_shapes=[pltpu.SemaphoreType.DMA((len(group),))],
                compiler_params=PARAMS,
                cost_estimate=cost(1000, 1_200_000),
                name="place",
            )(origins, *[back[s] for s in group], *([] if out is None else [out]))
    return out.reshape(frames, rows, cols, wide * n_time)


def solution(mesh):
    return jax.shard_map(
        shards,
        mesh=mesh,
        in_specs=(
            P("ta", "ha", "wa", None),
            P("ta", "ha", "wa", None),
            P("ta", "ha", "wa", None),
            P(),
            P(("ha", "wa"), None),
        ),
        out_specs=P("ta", "ha", "wa", None),
        check_vma=False,
    )
```

```python
import functools
import math

import jax
import jax.numpy as jnp
import numpy as np
from jax import lax
from jax.experimental import pallas as pl
from jax.experimental.pallas import tpu as pltpu
from jax.sharding import PartitionSpec as P

TILE = 4
PAIR = 2
FAR = -1e30
LANES = 128
STRIDE = 32
VMEM = pl.BlockSpec(memory_space=pltpu.VMEM)
SMEM = pl.BlockSpec(memory_space=pltpu.SMEM)
HBM = pl.BlockSpec(memory_space=pl.ANY)
PARAMS = pltpu.CompilerParams(vmem_limit_bytes=6 * 1024 * 1024)


def cycle(count, step):
    return [(i, (i + step) % count) for i in range(count)]


def swaps(count, phase, n_rows, rows_first):
    pairs = []
    for row in range(n_rows):
        for i in range(count):
            p = (i ^ 1) if phase == 0 else ((i + 1) ^ 1) - 1
            ends = ((row, i), (row, p) if 0 <= p < count else (row ^ 1, i))
            pairs.append(tuple(r * count + j if rows_first else j * n_rows + r for r, j in ends))
    return pairs


def line(count, step):
    return [(i, i + step) for i in range(count) if 0 <= i + step < count]


def sides(index, count):
    even = index % 2 == 0
    inside_after, inside_before = index < count - 1, index > 0
    return (even, ~even), (
        jnp.where(even, inside_after, inside_before),
        jnp.where(even, inside_before, inside_after),
    )


def code_table(rows, cols, rims):
    tile_cols = cols // TILE
    span = rows // TILE
    tables = []
    for core in range(PAIR):
        own = core * span
        other = (1 - core) * span
        blocks = [(own, rows), (other, rows)] + ([(-1, TILE), (2 * span, TILE)] if rims else [])
        for odd in range(2):
            query_row, query_col, key_row, key_col, key_side = [], [], [], [], []
            for base in (own, other):
                for row in range(rows):
                    for col in range(cols):
                        query_row.append(base + row // TILE)
                        query_col.append(col // TILE)
            for base, length in blocks:
                for row in range(length):
                    for col in range(cols):
                        key_row.append(base + row // TILE)
                        key_col.append(col // TILE)
                        key_side.append(-1)
            for phase in range(2):
                for base, length in blocks:
                    for row in range(length):
                        for _ in range(TILE):
                            key_row.append(base + row // TILE)
                            key_col.append(tile_cols if phase == odd else -1)
                            key_side.append(phase)
            key_row, key_col, key_side = (np.array(x)[None] for x in (key_row, key_col, key_side))
            apart_row = np.abs(np.array(query_row)[:, None] - key_row)
            apart_col = np.abs(np.array(query_col)[:, None] - key_col)
            base_code = (
                2 * (apart_row == 1)
                + 4 * (apart_col == 1)
                + 8 * ((apart_row > 1) | (apart_col > 1))
            )
            outside = [key_side == 0, key_side == 1]
            outside += [key_row < 0, key_row >= 2 * span] if rims else []
            for bits in range(2 ** len(outside)):
                code = base_code
                for which, mask in enumerate(outside):
                    if bits >> which & 1:
                        code = np.where(mask, 8, code)
                tables.append(code)
    return np.stack(tables).astype(np.int32)


def head_bias(code, radius_ref, head):
    barred = (
        8
        + jnp.where(radius_ref[head, 1] == 0, 2, 0)
        + jnp.where(radius_ref[head, 2] == 0, 4, 0)
    )
    return jnp.where((code & barred) == 0, 0.0, FAR)


class Window:
    def __init__(self, refs, rims, heads, width):
        refs = list(refs)
        self.blocks = refs[:2]
        self.extra = refs[2 : 5 if rims else 4]
        self.rest = refs[5 if rims else 4 :]
        self.frames = self.blocks[0].shape[1]
        self.width = width

    def near(self, kind, frame, head):
        lanes = pl.ds(head * self.width, self.width)
        return [ref[kind, frame, :, lanes] for ref in self.blocks]

    def query(self, frame, head):
        return jnp.concatenate(self.near(0, frame, head), axis=0)

    def pair(self, frame, head):
        lanes = pl.ds(head * self.width, self.width)
        return [
            jnp.concatenate(
                self.near(1 + kind, frame, head)
                + [ref[kind, frame, :, lanes] for ref in self.extra],
                axis=0,
            )
            for kind in range(2)
        ]


def scores_of(query, key, scale):
    return (
        lax.dot_general(
            query, key, (((1,), (1,)), ((), ())), preferred_element_type=jnp.float32
        )
        * scale
    )


def edge_kernel(rims, cols, meta_ref, *refs):
    own, other = refs[:2]
    rim = refs[2] if rims else None
    sides_out = refs[-2:]
    frames, area, half = other.shape[1:]

    def pick(rows):
        deep = rows * TILE
        shape = (2 * deep, rows * cols)
        to, of = (lax.broadcasted_iota(jnp.int32, shape, d) for d in range(2))
        spot = jnp.where(to < deep, meta_ref[5], meta_ref[6])
        to = lax.rem(to, deep)
        wanted = (to // TILE) * cols + spot * TILE + lax.rem(to, TILE)
        return deep, (of == wanted).astype(jnp.bfloat16)

    block = pick(area // cols)
    strip = pick(TILE)
    for kind in range(2):
        for frame in range(frames):
            work = [
                (own[1 + kind, frame], block),
                (other[1 + kind, frame], block),
            ]
            if rims:
                band = TILE * cols
                work += [(rim[kind, frame, i * band : (i + 1) * band], strip) for i in range(2)]
            begin = 0
            for rows, (deep, chosen) in work:
                found = jnp.dot(chosen, rows, preferred_element_type=jnp.float32)
                found = found.astype(jnp.bfloat16)
                for phase in range(2):
                    sides_out[phase][kind, frame, begin : begin + deep] = found[
                        phase * deep : (phase + 1) * deep
                    ]
                begin += deep


def guest_kernel(rims, heads, width, meta_ref, radius_ref, code_ref, *refs):
    window = Window(refs, rims, heads, width)
    guests, outs = window.rest[:2], window.rest[3:5]
    code = code_ref[...]
    count = code.shape[0]
    scale = 1.0 / math.sqrt(width)
    first = meta_ref[0] * heads
    lane = lax.broadcasted_iota(jnp.int32, (count, LANES), 1)
    tops = [jnp.zeros((count, LANES), jnp.float32) for _ in guests]
    totals = [jnp.ones((count, LANES), jnp.float32) for _ in guests]
    work = [(head, phase) for head in range(heads) for phase in range(2)]
    score, value = {}, {}
    for head in range(heads):
        bias = head_bias(code, radius_ref, first + head)
        for phase in range(2):
            key, value[head, phase] = window.pair(meta_ref[1 + phase], head)
            query = guests[phase][:, pl.ds(head * width, width)]
            score[head, phase] = scores_of(query, key, scale) + bias
    top = {at: jnp.max(score[at], axis=1, keepdims=True) for at in work}
    expo = {at: jnp.exp(score[at] - top[at]) for at in work}
    total = {at: jnp.sum(expo[at], axis=1, keepdims=True) for at in work}
    for at in work:
        head, phase = at
        probs = (expo[at] * (1.0 / total[at])).astype(jnp.bfloat16)
        mixed = jnp.dot(probs, value[at], preferred_element_type=jnp.float32)
        outs[phase][:, pl.ds(head * width, width)] = mixed.astype(jnp.bfloat16)
        tops[phase] = jnp.where(lane == head, top[at], tops[phase])
        totals[phase] = jnp.where(lane == head, total[at], totals[phase])
    for out_ref, top, total in zip(outs, tops, totals):
        rest = top + jnp.log(total)
        stats = jnp.zeros((count, LANES), jnp.float32)
        for part in range(3):
            piece = rest.astype(jnp.bfloat16).astype(jnp.float32)
            rest = rest - piece
            stats = stats + (pltpu.roll(piece, part * STRIDE, 1) if part else piece)
        out_ref[:, pl.ds(heads * width, LANES)] = stats.astype(jnp.bfloat16)


def host_kernel(rims, heads, width, meta_ref, radius_ref, code_ref, *refs):
    window = Window(refs, rims, heads, width)
    mixed_ref, stats_ref = window.rest
    frames = window.frames
    code = code_ref[...]
    count = code.shape[0]
    scale = 1.0 / math.sqrt(width)
    first = meta_ref[0] * heads
    lane = lax.broadcasted_iota(jnp.int32, (count, LANES), 1)
    tops = [jnp.zeros((count, LANES), jnp.float32) for _ in range(frames)]
    totals = [jnp.ones((count, LANES), jnp.float32) for _ in range(frames)]
    work = [(head, f) for head in range(heads) for f in range(frames)]
    score, value = {}, {}
    for head in range(heads):
        bias = head_bias(code, radius_ref, first + head)
        bias_apart = jnp.where(radius_ref[first + head, 0] == 0, FAR, bias)
        query = [window.query(f, head) for f in range(frames)]
        pairs = [window.pair(f, head) for f in range(frames)]
        blocks = {}
        for frame in range(frames):
            near = range(max(0, frame - 1), min(frames, frame + 2))
            block = scores_of(
                jnp.concatenate([query[f] for f in near], axis=0), pairs[frame][0], scale
            )
            for spot, f in enumerate(near):
                blocks[f, frame] = block[spot * count : (spot + 1) * count] + (
                    bias if f == frame else bias_apart
                )
        for f in range(frames):
            near = range(max(0, f - 1), min(frames, f + 2))
            score[head, f] = jnp.concatenate([blocks[f, g] for g in near], axis=1)
            value[head, f] = jnp.concatenate([pairs[g][1] for g in near], axis=0)
    top = {at: jnp.max(score[at], axis=1, keepdims=True) for at in work}
    expo = {at: jnp.exp(score[at] - top[at]) for at in work}
    total = {at: jnp.sum(expo[at], axis=1, keepdims=True) for at in work}
    for at in work:
        head, f = at
        probs = (expo[at] * (1.0 / total[at])).astype(jnp.bfloat16)
        mixed_ref[f, :, pl.ds(head * width, width)] = jnp.dot(
            probs, value[at], preferred_element_type=jnp.float32
        )
        tops[f] = jnp.where(lane == head, top[at], tops[f])
        totals[f] = jnp.where(lane == head, total[at], totals[f])
    for f in range(frames):
        stats_ref[f] = tops[f] + jnp.log(totals[f])


def merge_kernel(
    heads, width, meta_ref, radius_ref, mixed_ref, stats_ref, ref_0, ref_1, out_ref
):
    frames, count, _ = mixed_ref.shape
    half = count // PAIR
    first = meta_ref[0] * heads
    lane = lax.broadcasted_iota(jnp.int32, (count, LANES), 1)
    use = jnp.zeros((count, LANES), jnp.int32)
    for head in range(heads):
        use = jnp.where(lane == head, radius_ref[first + head, 0], use)
    logs, shares = [], []
    for phase, ref in enumerate((ref_0, ref_1)):
        there = jnp.where(meta_ref[3 + phase] == 0, 0, use)
        stats = ref[:, pl.ds(heads * width, LANES)].astype(jnp.float32)
        guest = (
            stats
            + pltpu.roll(stats, LANES - STRIDE, 1)
            + pltpu.roll(stats, LANES - 2 * STRIDE, 1)
        )
        guest = jnp.where(there == 0, FAR, guest)
        own = stats_ref[meta_ref[1 + phase]]
        if frames == 1 and phase == 1:
            own = logs[0]
        top = jnp.maximum(own, guest)
        guest_weight = jnp.exp(guest - top)
        total = jnp.exp(own - top) + guest_weight
        logs.append(top + jnp.log(total) if frames == 1 else None)
        shares.append(guest_weight / total)

    def store(f, lanes, mixed):
        mixed = mixed.astype(out_ref.dtype)
        for part in range(PAIR):
            out_ref[part, f, :, lanes] = mixed[part * half : (part + 1) * half]

    def boundary(spots):
        for head in range(heads):
            lanes = pl.ds(head * width, width)
            for f in sorted(set(spots)):
                mixed = mixed_ref[f, :, lanes]
                for phase, ref in enumerate((ref_0, ref_1)):
                    if spots[phase] == f:
                        guest = ref[:, lanes].astype(jnp.float32)
                        mixed = mixed + (guest - mixed) * shares[phase][:, head : head + 1]
                store(f, lanes, mixed)

    pl.when(meta_ref[1] == 0)(lambda: boundary((0, frames - 1)))
    if frames > 1:
        pl.when(meta_ref[1] != 0)(lambda: boundary((frames - 1, 0)))
    for f in range(1, frames - 1):
        store(f, slice(None), mixed_ref[f])


def join_kernel(count, meta_ref, *refs):
    pieces, out = refs[:count], refs[-1]
    depth = pieces[0].shape[0]
    for spot, ref in enumerate(pieces):
        begin = pl.multiple_of(meta_ref[spot] * depth, depth)
        out[pl.ds(begin, depth)] = ref[...]


def project_kernel(rows, near, own_out, other_out):
    both = jnp.dot(rows[...], near[...], preferred_element_type=jnp.float32)
    half = own_out.shape[0]
    own_out[...] = both[:half]
    other_out[...] = both[half:].astype(other_out.dtype)


def total_kernel(part, partner, out):
    out[...] = (part[...] + partner[...].astype(jnp.float32)).astype(out.dtype)


def place_kernel(count, meta_ref, *refs):
    pieces, out, sems = refs[:count], refs[-2], refs[-1]
    wide = pieces[0].shape[-1]
    copies = []
    for spot, ref in enumerate(pieces):
        where = pl.ds(pl.multiple_of(meta_ref[spot] * wide, LANES), wide)
        copies.append(pltpu.make_async_copy(ref, out.at[:, where], sems.at[spot]))
    for copy in copies:
        copy.start()
    for copy in copies:
        copy.wait()


def cost(flops, size):
    return pl.CostEstimate(flops=flops, bytes_accessed=size, transcendentals=0)


def shards(queries, keys, values, radius, out_weight):
    n_time, n_rows, n_cols = (lax.axis_size(a) for a in ("ta", "ha", "wa"))
    at_time, at_row, at_col = (lax.axis_index(a) for a in ("ta", "ha", "wa"))
    core = at_row % PAIR
    frames, rows, cols, features = queries.shape
    heads = radius.shape[0] // PAIR
    width = features // radius.shape[0]
    half = features // PAIR
    tile_cols = cols // TILE
    area = rows * cols
    rims = n_rows > PAIR

    after, there = sides(at_col, n_cols)
    later, present = sides(at_time, n_time)
    ends = [jnp.where(x, frames - 1, 0) for x in later]
    borders = [jnp.where(x, tile_cols - 1, 0) for x in after]
    meta = jnp.stack([core, *ends, *present, *borders]).astype(jnp.int32)

    raw = [x.reshape(frames, area, features) for x in (queries, keys, values)]
    pairs = [(i, i ^ 1) for i in range(n_rows)]
    stacked = jnp.stack(raw)
    own, other = (
        lax.dynamic_slice_in_dim(stacked, which * half, half, axis=3) for which in (core, 1 - core)
    )
    other = lax.ppermute(other, "ha", pairs)
    rim = None
    if rims:
        even, odd = (jnp.where(core == i, own[1:], other[1:]) for i in range(PAIR))
        band = TILE * cols
        up = lax.ppermute(odd[:, :, -band:], "ha", line(n_rows, PAIR))
        down = lax.ppermute(even[:, :, :band], "ha", line(n_rows, -PAIR))
        rim = jnp.concatenate([up, down], axis=2)
    deep = PAIR * rows * TILE + (PAIR * TILE * TILE if rims else 0)
    side = jax.ShapeDtypeStruct((2, frames, deep, half), queries.dtype)
    edges = pl.pallas_call(
        functools.partial(edge_kernel, rims, cols),
        out_shape=(side, side),
        in_specs=[SMEM] + [VMEM] * (3 if rims else 2),
        out_specs=(VMEM,) * 2,
        compiler_params=PARAMS,
        cost_estimate=cost(1000, 2_000_000),
        name="edge",
    )(meta, own, other, *([rim] if rims else []))
    beside = [lax.ppermute(x, ("ha", "wa"), swaps(n_cols, phase, n_rows, True)) for phase, x in enumerate(edges)]
    guests = []
    for phase, frame in enumerate(ends):
        end = [lax.dynamic_index_in_dim(x[0], frame, 0, keepdims=False) for x in (own, other)]
        end = jnp.concatenate(end, axis=0)
        guests.append(lax.ppermute(end, ("ta", "ha"), swaps(n_time, phase, n_rows, False)))

    slab = features // (n_rows * n_cols)
    wide = out_weight.shape[1] // n_time
    mine = lax.dynamic_slice_in_dim(out_weight, at_time * wide, wide, axis=1)
    held = {0: mine}

    table = jnp.asarray(code_table(rows, cols, rims))
    absent = [~x for x in there]
    if rims:
        absent += [at_row < PAIR, at_row >= n_rows - PAIR]
    spot = core * 2 + at_col % 2
    spot = spot * 2 ** len(absent) + sum(jnp.where(x, 2**i, 0) for i, x in enumerate(absent))
    code = lax.dynamic_index_in_dim(table, spot, 0, keepdims=False)

    parts = [own, other] + ([rim] if rims else []) + beside
    count = PAIR * area
    unit = 4 * heads * width * count * code.shape[1]
    payload = jax.ShapeDtypeStruct((count, half + LANES), jnp.bfloat16)
    *answers, sent = pl.pallas_call(
        functools.partial(guest_kernel, rims, heads, width),
        out_shape=(payload, payload, jax.ShapeDtypeStruct(mine.shape, mine.dtype)),
        in_specs=[SMEM, SMEM] + [VMEM] * (1 + len(parts) + 2) + [HBM],
        out_specs=(VMEM, VMEM, HBM),
        input_output_aliases={5 + len(parts): 2},
        compiler_params=PARAMS,
        cost_estimate=cost(2 * unit, 4_000_000),
        name="guest",
    )(meta, radius, code, *parts, *guests, mine)
    held[0] = sent
    if n_cols > 1:
        held[1] = lax.ppermute(sent, "wa", cycle(n_cols, 1))
    answers = [
        lax.ppermute(x, ("ta", "ha"), swaps(n_time, phase, n_rows, False)) for phase, x in enumerate(answers)
    ]
    mixed_shape, stats_shape = (frames, count, half), (frames, count, LANES)
    mixed, stats = pl.pallas_call(
        functools.partial(host_kernel, rims, heads, width),
        out_shape=(
            jax.ShapeDtypeStruct(mixed_shape, jnp.float32),
            jax.ShapeDtypeStruct(stats_shape, jnp.float32),
        ),
        in_specs=[SMEM, SMEM] + [VMEM] * (1 + len(parts)),
        out_specs=(VMEM, VMEM),
        compiler_params=PARAMS,
        cost_estimate=cost(7 * unit, 6_000_000),
        name="host",
    )(meta, radius, code, *parts)
    attended = pl.pallas_call(
        functools.partial(merge_kernel, heads, width),
        out_shape=jax.ShapeDtypeStruct((PAIR, frames, area, half), jnp.bfloat16),
        in_specs=[SMEM, SMEM] + [VMEM] * 4,
        out_specs=VMEM,
        compiler_params=PARAMS,
        cost_estimate=cost(1000, 3_000_000),
        name="merge",
    )(meta, radius, mixed, stats, *answers)
    tokens = frames * area
    attended = attended.reshape(PAIR * tokens, half)
    if n_cols > 2:
        held[n_cols - 1] = lax.ppermute(sent, "wa", cycle(n_cols, -1))
    for s in range(2, n_cols - 1):
        held[s] = lax.ppermute(held[s - 1], "wa", cycle(n_cols, 1))
    received = [lax.ppermute(attended, "ta", cycle(n_time, s)) for s in range(1, n_time)]

    def joined(shards, at):
        count = len(shards)
        spots = jnp.stack([(at - s) % count for s in range(count)]).astype(jnp.int32)
        if shards[0].shape[0] % 16:
            return jnp.roll(jnp.stack(shards[::-1]), at + 1, axis=0).reshape(-1, wide)
        return pl.pallas_call(
            functools.partial(join_kernel, count),
            out_shape=jax.ShapeDtypeStruct((count * shards[0].shape[0], wide), mine.dtype),
            in_specs=[SMEM] + [VMEM] * count + [HBM],
            out_specs=VMEM,
            compiler_params=PARAMS,
            cost_estimate=cost(1000, 2_400_000),
            name="join",
        )(spots, *shards, (received + [attended] * 2)[1])

    near = joined([held[s] for s in range(n_cols)], at_col)
    if n_rows > PAIR:
        across = [lax.ppermute(near, "ha", cycle(n_rows, r)) for r in range(1, n_rows)]
        near = lax.dynamic_slice_in_dim(joined([near, *across], at_row), core * half, half, axis=0)

    weight = 36 * 2 * tokens * features * wide

    def project(block):
        part = jax.ShapeDtypeStruct((tokens, wide), jnp.float32)
        return pl.pallas_call(
            project_kernel,
            out_shape=(part, jax.ShapeDtypeStruct(part.shape, queries.dtype)),
            in_specs=[VMEM, VMEM],
            out_specs=(VMEM, VMEM),
            compiler_params=PARAMS,
            cost_estimate=cost(weight, 3_000_000),
            name="project",
        )(block, near)

    def total(part, partner):
        return pl.pallas_call(
            total_kernel,
            out_shape=jax.ShapeDtypeStruct((tokens, wide), queries.dtype),
            in_specs=[VMEM, VMEM],
            out_specs=VMEM,
            compiler_params=PARAMS,
            cost_estimate=cost(weight, 3_000_000),
            name="total",
        )(part, partner)

    products = []
    for block in [attended, *received]:
        part, given = project(block)
        products.append(total(part, lax.ppermute(given, "ha", pairs)))
    back = [products[0]] + [
        lax.ppermute(products[n_time - s], "ta", cycle(n_time, s)) for s in range(1, n_time)
    ]
    late = 1 % n_time
    out = None
    for group in ([s for s in range(n_time) if s != late], [late] if n_time > 1 else []):
        if group:
            origins = jnp.stack([(at_time - s) % n_time for s in group]).astype(jnp.int32)
            out = pl.pallas_call(
                functools.partial(place_kernel, len(group)),
                out_shape=jax.ShapeDtypeStruct((tokens, wide * n_time), jnp.bfloat16),
                in_specs=[SMEM] + [HBM] * (len(group) + (out is not None)),
                out_specs=HBM,
                input_output_aliases={} if out is None else {1 + len(group): 0},
                scratch_shapes=[pltpu.SemaphoreType.DMA((len(group),))],
                compiler_params=PARAMS,
                cost_estimate=cost(1000, 1_200_000),
                name="place",
            )(origins, *[back[s] for s in group], *([] if out is None else [out]))
    return out.reshape(frames, rows, cols, wide * n_time)


def solution(mesh):
    return jax.shard_map(
        shards,
        mesh=mesh,
        in_specs=(
            P("ta", "ha", "wa", None),
            P("ta", "ha", "wa", None),
            P("ta", "ha", "wa", None),
            P(),
            P(("ha", "wa"), None),
        ),
        out_specs=P("ta", "ha", "wa", None),
        check_vma=False,
    )
```

```python
import functools
import math

import jax
import jax.numpy as jnp
import numpy as np
from jax import lax
from jax.experimental import pallas as pl
from jax.experimental.pallas import tpu as pltpu
from jax.sharding import PartitionSpec as P

TILE = 4
PAIR = 2
FAR = -1e30
LANES = 128
STRIDE = 32
VMEM = pl.BlockSpec(memory_space=pltpu.VMEM)
SMEM = pl.BlockSpec(memory_space=pltpu.SMEM)
HBM = pl.BlockSpec(memory_space=pl.ANY)
PARAMS = pltpu.CompilerParams(vmem_limit_bytes=6 * 1024 * 1024)


def cycle(count, step):
    return [(i, (i + step) % count) for i in range(count)]


def swaps(count, phase, n_rows, rows_first):
    pairs = []
    for row in range(n_rows):
        for i in range(count):
            p = (i ^ 1) if phase == 0 else ((i + 1) ^ 1) - 1
            ends = ((row, i), (row, p) if 0 <= p < count else (row ^ 1, i))
            pairs.append(tuple(r * count + j if rows_first else j * n_rows + r for r, j in ends))
    return pairs


def exchange(count, step):
    return cycle(count, step) if count & (count - 1) else [(i, i ^ step) for i in range(count)]


def line(count, step):
    return [(i, i + step) for i in range(count) if 0 <= i + step < count]


def sides(index, count):
    even = index % 2 == 0
    inside_after, inside_before = index < count - 1, index > 0
    return (even, ~even), (
        jnp.where(even, inside_after, inside_before),
        jnp.where(even, inside_before, inside_after),
    )


def code_table(rows, cols, rims):
    tile_cols = cols // TILE
    span = rows // TILE
    tables = []
    for core in range(PAIR):
        own = core * span
        other = (1 - core) * span
        blocks = [(own, rows), (other, rows)] + ([(-1, TILE), (2 * span, TILE)] if rims else [])
        for odd in range(2):
            query_row, query_col, key_row, key_col, key_side = [], [], [], [], []
            for base in (own, other):
                for row in range(rows):
                    for col in range(cols):
                        query_row.append(base + row // TILE)
                        query_col.append(col // TILE)
            for base, length in blocks:
                for row in range(length):
                    for col in range(cols):
                        key_row.append(base + row // TILE)
                        key_col.append(col // TILE)
                        key_side.append(-1)
            for phase in range(2):
                for base, length in blocks:
                    for row in range(length):
                        for _ in range(TILE):
                            key_row.append(base + row // TILE)
                            key_col.append(tile_cols if phase == odd else -1)
                            key_side.append(phase)
            key_row, key_col, key_side = (np.array(x)[None] for x in (key_row, key_col, key_side))
            apart_row = np.abs(np.array(query_row)[:, None] - key_row)
            apart_col = np.abs(np.array(query_col)[:, None] - key_col)
            base_code = (
                2 * (apart_row == 1)
                + 4 * (apart_col == 1)
                + 8 * ((apart_row > 1) | (apart_col > 1))
            )
            outside = [key_side == 0, key_side == 1]
            outside += [key_row < 0, key_row >= 2 * span] if rims else []
            for bits in range(2 ** len(outside)):
                code = base_code
                for which, mask in enumerate(outside):
                    if bits >> which & 1:
                        code = np.where(mask, 8, code)
                tables.append(code)
    return np.stack(tables).astype(np.int32)


def head_bias(code, radius_ref, head):
    barred = (
        8
        + jnp.where(radius_ref[head, 1] == 0, 2, 0)
        + jnp.where(radius_ref[head, 2] == 0, 4, 0)
    )
    return jnp.where((code & barred) == 0, 0.0, FAR)


class Window:
    def __init__(self, refs, rims, heads, width):
        refs = list(refs)
        self.blocks = refs[:2]
        self.extra = refs[2 : 5 if rims else 4]
        self.rest = refs[5 if rims else 4 :]
        self.frames = self.blocks[0].shape[1]
        self.width = width

    def near(self, kind, frame, head):
        lanes = pl.ds(head * self.width, self.width)
        return [ref[kind, frame, :, lanes] for ref in self.blocks]

    def query(self, frame, head):
        return jnp.concatenate(self.near(0, frame, head), axis=0)

    def pair(self, frame, head):
        lanes = pl.ds(head * self.width, self.width)
        return [
            jnp.concatenate(
                self.near(1 + kind, frame, head)
                + [ref[kind, frame, :, lanes] for ref in self.extra],
                axis=0,
            )
            for kind in range(2)
        ]


def scores_of(query, key, scale):
    return (
        lax.dot_general(
            query, key, (((1,), (1,)), ((), ())), preferred_element_type=jnp.float32
        )
        * scale
    )


def edge_kernel(rims, cols, meta_ref, *refs):
    own, other = refs[:2]
    rim = refs[2] if rims else None
    sides_out = refs[-2:]
    frames, area, half = other.shape[1:]

    def pick(rows):
        deep = rows * TILE
        shape = (2 * deep, rows * cols)
        to, of = (lax.broadcasted_iota(jnp.int32, shape, d) for d in range(2))
        spot = jnp.where(to < deep, meta_ref[5], meta_ref[6])
        to = lax.rem(to, deep)
        wanted = (to // TILE) * cols + spot * TILE + lax.rem(to, TILE)
        return deep, (of == wanted).astype(jnp.bfloat16)

    block = pick(area // cols)
    strip = pick(TILE)
    for kind in range(2):
        for frame in range(frames):
            work = [
                (own[1 + kind, frame], block),
                (other[1 + kind, frame], block),
            ]
            if rims:
                band = TILE * cols
                work += [(rim[kind, frame, i * band : (i + 1) * band], strip) for i in range(2)]
            begin = 0
            for rows, (deep, chosen) in work:
                found = jnp.dot(chosen, rows, preferred_element_type=jnp.float32)
                found = found.astype(jnp.bfloat16)
                for phase in range(2):
                    sides_out[phase][kind, frame, begin : begin + deep] = found[
                        phase * deep : (phase + 1) * deep
                    ]
                begin += deep


def guest_kernel(rims, heads, width, meta_ref, radius_ref, code_ref, *refs):
    window = Window(refs, rims, heads, width)
    guests, outs = window.rest[:2], window.rest[3:5]
    code = code_ref[...]
    count = code.shape[0]
    scale = 1.0 / math.sqrt(width)
    first = meta_ref[0] * heads
    lane = lax.broadcasted_iota(jnp.int32, (count, LANES), 1)
    tops = [jnp.zeros((count, LANES), jnp.float32) for _ in guests]
    totals = [jnp.ones((count, LANES), jnp.float32) for _ in guests]
    work = [(head, phase) for head in range(heads) for phase in range(2)]
    score, value = {}, {}
    for head in range(heads):
        bias = head_bias(code, radius_ref, first + head)
        for phase in range(2):
            key, value[head, phase] = window.pair(meta_ref[1 + phase], head)
            query = guests[phase][:, pl.ds(head * width, width)]
            score[head, phase] = scores_of(query, key, scale) + bias
    top = {at: jnp.max(score[at], axis=1, keepdims=True) for at in work}
    expo = {at: jnp.exp(score[at] - top[at]) for at in work}
    total = {at: jnp.sum(expo[at], axis=1, keepdims=True) for at in work}
    for at in work:
        head, phase = at
        probs = (expo[at] * (1.0 / total[at])).astype(jnp.bfloat16)
        mixed = jnp.dot(probs, value[at], preferred_element_type=jnp.float32)
        outs[phase][:, pl.ds(head * width, width)] = mixed.astype(jnp.bfloat16)
        tops[phase] = jnp.where(lane == head, top[at], tops[phase])
        totals[phase] = jnp.where(lane == head, total[at], totals[phase])
    for out_ref, top, total in zip(outs, tops, totals):
        rest = top + jnp.log(total)
        stats = jnp.zeros((count, LANES), jnp.float32)
        for part in range(3):
            piece = rest.astype(jnp.bfloat16).astype(jnp.float32)
            rest = rest - piece
            stats = stats + (pltpu.roll(piece, part * STRIDE, 1) if part else piece)
        out_ref[:, pl.ds(heads * width, LANES)] = stats.astype(jnp.bfloat16)


def host_kernel(rims, heads, width, meta_ref, radius_ref, code_ref, *refs):
    window = Window(refs, rims, heads, width)
    mixed_ref, stats_ref = window.rest
    frames = window.frames
    code = code_ref[...]
    count = code.shape[0]
    scale = 1.0 / math.sqrt(width)
    first = meta_ref[0] * heads
    lane = lax.broadcasted_iota(jnp.int32, (count, LANES), 1)
    tops = [jnp.zeros((count, LANES), jnp.float32) for _ in range(frames)]
    totals = [jnp.ones((count, LANES), jnp.float32) for _ in range(frames)]
    work = [(head, f) for head in range(heads) for f in range(frames)]
    score, value = {}, {}
    for head in range(heads):
        bias = head_bias(code, radius_ref, first + head)
        bias_apart = jnp.where(radius_ref[first + head, 0] == 0, FAR, bias)
        query = [window.query(f, head) for f in range(frames)]
        pairs = [window.pair(f, head) for f in range(frames)]
        blocks = {}
        for frame in range(frames):
            near = range(max(0, frame - 1), min(frames, frame + 2))
            block = scores_of(
                jnp.concatenate([query[f] for f in near], axis=0), pairs[frame][0], scale
            )
            for spot, f in enumerate(near):
                blocks[f, frame] = block[spot * count : (spot + 1) * count] + (
                    bias if f == frame else bias_apart
                )
        for f in range(frames):
            near = range(max(0, f - 1), min(frames, f + 2))
            score[head, f] = jnp.concatenate([blocks[f, g] for g in near], axis=1)
            value[head, f] = jnp.concatenate([pairs[g][1] for g in near], axis=0)
    top = {at: jnp.max(score[at], axis=1, keepdims=True) for at in work}
    expo = {at: jnp.exp(score[at] - top[at]) for at in work}
    total = {at: jnp.sum(expo[at], axis=1, keepdims=True) for at in work}
    for at in work:
        head, f = at
        probs = (expo[at] * (1.0 / total[at])).astype(jnp.bfloat16)
        mixed_ref[f, :, pl.ds(head * width, width)] = jnp.dot(
            probs, value[at], preferred_element_type=jnp.float32
        )
        tops[f] = jnp.where(lane == head, top[at], tops[f])
        totals[f] = jnp.where(lane == head, total[at], totals[f])
    for f in range(frames):
        stats_ref[f] = tops[f] + jnp.log(totals[f])


def merge_kernel(
    heads, width, meta_ref, radius_ref, mixed_ref, stats_ref, ref_0, ref_1, out_ref
):
    frames, count, _ = mixed_ref.shape
    half = count // PAIR
    first = meta_ref[0] * heads
    lane = lax.broadcasted_iota(jnp.int32, (count, LANES), 1)
    use = jnp.zeros((count, LANES), jnp.int32)
    for head in range(heads):
        use = jnp.where(lane == head, radius_ref[first + head, 0], use)
    logs, shares = [], []
    for phase, ref in enumerate((ref_0, ref_1)):
        there = jnp.where(meta_ref[3 + phase] == 0, 0, use)
        stats = ref[:, pl.ds(heads * width, LANES)].astype(jnp.float32)
        guest = (
            stats
            + pltpu.roll(stats, LANES - STRIDE, 1)
            + pltpu.roll(stats, LANES - 2 * STRIDE, 1)
        )
        guest = jnp.where(there == 0, FAR, guest)
        own = stats_ref[meta_ref[1 + phase]]
        if frames == 1 and phase == 1:
            own = logs[0]
        top = jnp.maximum(own, guest)
        guest_weight = jnp.exp(guest - top)
        total = jnp.exp(own - top) + guest_weight
        logs.append(top + jnp.log(total) if frames == 1 else None)
        shares.append(guest_weight / total)

    def store(f, lanes, mixed):
        mixed = mixed.astype(out_ref.dtype)
        for part in range(PAIR):
            out_ref[part, f, :, lanes] = mixed[part * half : (part + 1) * half]

    def boundary(spots):
        for head in range(heads):
            lanes = pl.ds(head * width, width)
            for f in sorted(set(spots)):
                mixed = mixed_ref[f, :, lanes]
                for phase, ref in enumerate((ref_0, ref_1)):
                    if spots[phase] == f:
                        guest = ref[:, lanes].astype(jnp.float32)
                        mixed = mixed + (guest - mixed) * shares[phase][:, head : head + 1]
                store(f, lanes, mixed)

    pl.when(meta_ref[1] == 0)(lambda: boundary((0, frames - 1)))
    if frames > 1:
        pl.when(meta_ref[1] != 0)(lambda: boundary((frames - 1, 0)))
    for f in range(1, frames - 1):
        store(f, slice(None), mixed_ref[f])


def join_kernel(count, meta_ref, *refs):
    pieces, out = refs[:count], refs[-1]
    depth = pieces[0].shape[0]
    for spot, ref in enumerate(pieces):
        begin = pl.multiple_of(meta_ref[spot] * depth, depth)
        out[pl.ds(begin, depth)] = ref[...]


def project_kernel(rows, near, own_out, other_out):
    both = jnp.dot(rows[...], near[...], preferred_element_type=jnp.float32)
    half = own_out.shape[0]
    own_out[...] = both[:half]
    other_out[...] = both[half:]


def total_kernel(part, partner, out):
    out[...] = (part[...] + partner[...]).astype(out.dtype)


def place_kernel(count, meta_ref, *refs):
    pieces, out, sems = refs[:count], refs[-2], refs[-1]
    wide = pieces[0].shape[-1]
    copies = []
    for spot, ref in enumerate(pieces):
        where = pl.ds(pl.multiple_of(meta_ref[spot] * wide, LANES), wide)
        copies.append(pltpu.make_async_copy(ref, out.at[:, where], sems.at[spot]))
    for copy in copies:
        copy.start()
    for copy in copies:
        copy.wait()


def cost(flops, size):
    return pl.CostEstimate(flops=flops, bytes_accessed=size, transcendentals=0)


def shards(queries, keys, values, radius, out_weight):
    n_time, n_rows, n_cols = (lax.axis_size(a) for a in ("ta", "ha", "wa"))
    at_time, at_row, at_col = (lax.axis_index(a) for a in ("ta", "ha", "wa"))
    core = at_row % PAIR
    frames, rows, cols, features = queries.shape
    heads = radius.shape[0] // PAIR
    width = features // radius.shape[0]
    half = features // PAIR
    tile_cols = cols // TILE
    area = rows * cols
    rims = n_rows > PAIR

    after, there = sides(at_col, n_cols)
    later, present = sides(at_time, n_time)
    ends = [jnp.where(x, frames - 1, 0) for x in later]
    borders = [jnp.where(x, tile_cols - 1, 0) for x in after]
    meta = jnp.stack([core, *ends, *present, *borders]).astype(jnp.int32)

    raw = [x.reshape(frames, area, features) for x in (queries, keys, values)]
    pairs = [(i, i ^ 1) for i in range(n_rows)]
    stacked = jnp.stack(raw)
    own, other = (
        lax.dynamic_slice_in_dim(stacked, which * half, half, axis=3) for which in (core, 1 - core)
    )
    other = lax.ppermute(other, "ha", pairs)
    rim = None
    if rims:
        even, odd = (jnp.where(core == i, own[1:], other[1:]) for i in range(PAIR))
        band = TILE * cols
        up = lax.ppermute(odd[:, :, -band:], "ha", line(n_rows, PAIR))
        down = lax.ppermute(even[:, :, :band], "ha", line(n_rows, -PAIR))
        rim = jnp.concatenate([up, down], axis=2)
    deep = PAIR * rows * TILE + (PAIR * TILE * TILE if rims else 0)
    side = jax.ShapeDtypeStruct((2, frames, deep, half), queries.dtype)
    edges = pl.pallas_call(
        functools.partial(edge_kernel, rims, cols),
        out_shape=(side, side),
        in_specs=[SMEM] + [VMEM] * (3 if rims else 2),
        out_specs=(VMEM,) * 2,
        compiler_params=PARAMS,
        cost_estimate=cost(1000, 2_000_000),
        name="edge",
    )(meta, own, other, *([rim] if rims else []))
    beside = [lax.ppermute(x, ("ha", "wa"), swaps(n_cols, phase, n_rows, True)) for phase, x in enumerate(edges)]
    guests = []
    for phase, frame in enumerate(ends):
        end = [lax.dynamic_index_in_dim(x[0], frame, 0, keepdims=False) for x in (own, other)]
        end = jnp.concatenate(end, axis=0)
        guests.append(lax.ppermute(end, ("ta", "ha"), swaps(n_time, phase, n_rows, False)))

    slab = features // (n_rows * n_cols)
    wide = out_weight.shape[1] // n_time
    mine = lax.dynamic_slice_in_dim(out_weight, at_time * wide, wide, axis=1)
    held = {0: mine}

    table = jnp.asarray(code_table(rows, cols, rims))
    absent = [~x for x in there]
    if rims:
        absent += [at_row < PAIR, at_row >= n_rows - PAIR]
    spot = core * 2 + at_col % 2
    spot = spot * 2 ** len(absent) + sum(jnp.where(x, 2**i, 0) for i, x in enumerate(absent))
    code = lax.dynamic_index_in_dim(table, spot, 0, keepdims=False)

    parts = [own, other] + ([rim] if rims else []) + beside
    count = PAIR * area
    unit = 4 * heads * width * count * code.shape[1]
    payload = jax.ShapeDtypeStruct((count, half + LANES), jnp.bfloat16)
    *answers, sent = pl.pallas_call(
        functools.partial(guest_kernel, rims, heads, width),
        out_shape=(payload, payload, jax.ShapeDtypeStruct(mine.shape, mine.dtype)),
        in_specs=[SMEM, SMEM] + [VMEM] * (1 + len(parts) + 2) + [HBM],
        out_specs=(VMEM, VMEM, HBM),
        input_output_aliases={5 + len(parts): 2},
        compiler_params=PARAMS,
        cost_estimate=cost(2 * unit, 4_000_000),
        name="guest",
    )(meta, radius, code, *parts, *guests, mine)
    held[0] = sent
    if n_cols > 1:
        held[1] = lax.ppermute(sent, "wa", cycle(n_cols, 1))
    answers = [
        lax.ppermute(x, ("ta", "ha"), swaps(n_time, phase, n_rows, False)) for phase, x in enumerate(answers)
    ]
    mixed_shape, stats_shape = (frames, count, half), (frames, count, LANES)
    mixed, stats = pl.pallas_call(
        functools.partial(host_kernel, rims, heads, width),
        out_shape=(
            jax.ShapeDtypeStruct(mixed_shape, jnp.float32),
            jax.ShapeDtypeStruct(stats_shape, jnp.float32),
        ),
        in_specs=[SMEM, SMEM] + [VMEM] * (1 + len(parts)),
        out_specs=(VMEM, VMEM),
        compiler_params=PARAMS,
        cost_estimate=cost(7 * unit, 6_000_000),
        name="host",
    )(meta, radius, code, *parts)
    attended = pl.pallas_call(
        functools.partial(merge_kernel, heads, width),
        out_shape=jax.ShapeDtypeStruct((PAIR, frames, area, half), jnp.bfloat16),
        in_specs=[SMEM, SMEM] + [VMEM] * 4,
        out_specs=VMEM,
        compiler_params=PARAMS,
        cost_estimate=cost(1000, 3_000_000),
        name="merge",
    )(meta, radius, mixed, stats, *answers)
    tokens = frames * area
    attended = attended.reshape(PAIR * tokens, half)
    if n_cols > 2:
        held[n_cols - 1] = lax.ppermute(sent, "wa", cycle(n_cols, -1))
    for s in range(2, n_cols - 1):
        held[s] = lax.ppermute(held[s - 1], "wa", cycle(n_cols, 1))
    received = [lax.ppermute(attended, "ta", exchange(n_time, s)) for s in range(1, n_time)]

    def joined(shards, at):
        count = len(shards)
        spots = jnp.stack([(at - s) % count for s in range(count)]).astype(jnp.int32)
        if shards[0].shape[0] % 16:
            return jnp.roll(jnp.stack(shards[::-1]), at + 1, axis=0).reshape(-1, wide)
        return pl.pallas_call(
            functools.partial(join_kernel, count),
            out_shape=jax.ShapeDtypeStruct((count * shards[0].shape[0], wide), mine.dtype),
            in_specs=[SMEM] + [VMEM] * count + [HBM] * 1,
            out_specs=VMEM,
            compiler_params=PARAMS,
            cost_estimate=cost(1000, 2_400_000),
            name="join",
        )(spots, *shards, (received + [attended] * 3)[2])

    near = joined([held[s] for s in range(n_cols)], at_col)
    if n_rows > PAIR:
        across = [lax.ppermute(near, "ha", cycle(n_rows, r)) for r in range(1, n_rows)]
        near = lax.dynamic_slice_in_dim(joined([near, *across], at_row), core * half, half, axis=0)

    weight = 36 * 2 * tokens * features * wide

    def project(block):
        part = jax.ShapeDtypeStruct((tokens, wide), jnp.float32)
        return pl.pallas_call(
            project_kernel,
            out_shape=(part, part),
            in_specs=[VMEM, VMEM],
            out_specs=(VMEM, VMEM),
            compiler_params=PARAMS,
            cost_estimate=cost(weight, 3_000_000),
            name="project",
        )(block, near)

    def total(part, partner):
        return pl.pallas_call(
            total_kernel,
            out_shape=jax.ShapeDtypeStruct((tokens, wide), queries.dtype),
            in_specs=[VMEM, VMEM],
            out_specs=VMEM,
            compiler_params=PARAMS,
            cost_estimate=cost(weight, 3_000_000),
            name="total",
        )(part, partner)

    products = []
    for block in [attended, *received]:
        part, given = project(block)
        products.append(total(part, lax.ppermute(given, "ha", pairs)))
    paired = n_time & (n_time - 1) == 0
    back = [products[0]] + [
        lax.ppermute(products[s if paired else n_time - s], "ta", exchange(n_time, s))
        for s in range(1, n_time)
    ]
    late = 1 % n_time
    out = None
    for group in ([s for s in range(n_time) if s != late], [late] if n_time > 1 else []):
        if group:
            origins = [at_time ^ s if paired else (at_time - s) % n_time for s in group]
            origins = jnp.stack(origins).astype(jnp.int32)
            out = pl.pallas_call(
                functools.partial(place_kernel, len(group)),
                out_shape=jax.ShapeDtypeStruct((tokens, wide * n_time), jnp.bfloat16),
                in_specs=[SMEM] + [HBM] * (len(group) + (out is not None)),
                out_specs=HBM,
                input_output_aliases={} if out is None else {1 + len(group): 0},
                scratch_shapes=[pltpu.SemaphoreType.DMA((len(group),))],
                compiler_params=PARAMS,
                cost_estimate=cost(1000, 1_200_000),
                name="place",
            )(origins, *[back[s] for s in group], *([] if out is None else [out]))
    return out.reshape(frames, rows, cols, wide * n_time)


def solution(mesh):
    return jax.shard_map(
        shards,
        mesh=mesh,
        in_specs=(
            P("ta", "ha", "wa", None),
            P("ta", "ha", "wa", None),
            P("ta", "ha", "wa", None),
            P(),
            P(("ha", "wa"), None),
        ),
        out_specs=P("ta", "ha", "wa", None),
        check_vma=False,
    )
```
